32 devices in a mesh: seq: 4 (over y, x), fsdp: 8 (over z, core).
Axes of the slice: x: 2, y: 2, z: 4, core: 2. Of those that a mesh axis runs over, the one named last changes fastest.
Arguments:
- tokens: bfloat16 [2, 3072, 2048], P(None, ('seq', 'fsdp')), may hold values from -6 to 6
- cotangent: bfloat16 [2, 3072, 2048], P(None, ('seq', 'fsdp')), may hold values from -6 to 6
- ids: int32 [2, 3072, 4], P(None, ('seq', 'fsdp')), may hold values from 0 to 7, all different within a row; in each aligned block of 96 rows (0 to 95, 96 to 191, ..., all dimensions but the last counted through in order) at most 72 rows name the same one
- deal: int32 [2, 8, 8], replicated, may hold values from 0 to 7, each once within a row
- lengths: int32 [2, 8, 4], replicated, may hold values from 1 to 337, 384 in all within a row
- w_qkv: bfloat16 [2048, 6144], P(('seq', 'fsdp')), may hold values from -0.125 to 0.125
- b_qkv: bfloat16 [6144], P(('seq', 'fsdp')), may hold values from -1.5 to 1.5
- w_out: bfloat16 [2048, 2048], P(('seq', 'fsdp')), may hold values from -0.5 to 0.5
- gain_attn: bfloat16 [2048], P(('seq', 'fsdp')), may hold values from 0.5 to 1.5
- gain_ffn: bfloat16 [2048], P(('seq', 'fsdp')), may hold values from 0.5 to 1.5
- w_router: bfloat16 [2048, 8], P(('seq', 'fsdp')), may hold values from -0.0625 to 0.0625
- w_shared_gate: bfloat16 [2048], P(('seq', 'fsdp')), may hold values from -0.125 to 0.125
- e_gate: bfloat16 [8, 2048, 1408], P('fsdp', 'seq'), may hold values from -0.125 to 0.125
- e_up: bfloat16 [8, 2048, 1408], P('fsdp', 'seq'), may hold values from -0.125 to 0.125
- e_down: bfloat16 [8, 1408, 2048], P('fsdp', None, 'seq'), may hold values from -0.875 to 0.875
- s_gate: bfloat16 [2048, 5632], P('seq', 'fsdp'), may hold values from -0.125 to 0.125
- s_up: bfloat16 [2048, 5632], P('seq', 'fsdp'), may hold values from -0.125 to 0.125
- s_down: bfloat16 [5632, 2048], P('fsdp', 'seq'), may hold values from -0.21875 to 0.21875
Outputs:
- mixed: bfloat16 [2, 3072, 2048], P(None, ('seq', 'fsdp'))
- grad_tokens: float32 [2, 3072, 2048], P(None, ('seq', 'fsdp'))
- grad_w_qkv: float32 [2048, 6144], P(('seq', 'fsdp'))
- grad_b_qkv: float32 [6144], P(('seq', 'fsdp'))
- grad_w_out: float32 [2048, 2048], P(('seq', 'fsdp'))
- grad_gain_attn: float32 [2048], P(('seq', 'fsdp'))
- grad_gain_ffn: float32 [2048], P(('seq', 'fsdp'))
- grad_w_router: float32 [2048, 8], P(('seq', 'fsdp'))
- grad_w_shared_gate: float32 [2048], P(('seq', 'fsdp'))
- grad_e_gate: float32 [8, 2048, 1408], P('fsdp', 'seq')
- grad_e_up: float32 [8, 2048, 1408], P('fsdp', 'seq')
- grad_e_down: float32 [8, 1408, 2048], P('fsdp', None, 'seq')
- grad_s_gate: float32 [2048, 5632], P('seq', 'fsdp')
- grad_s_up: float32 [2048, 5632], P('seq', 'fsdp')
- grad_s_down: float32 [5632, 2048], P('fsdp', 'seq')
The draws below stay inside these ranges and needn't reach their ends.
Inputs may be any that keep to these rules, and one draw needn't show every extreme that they name: `ids`: within the rows of one device in one micro-batch (aligned blocks of 96 rows) no expert is named by more than 72 rows, a bound that some block reaches; a token names 4 different experts. Each row deal[m, j, :] holds every data group once. Each lengths[m, g, :] sums to 384 and its largest entry is exactly 337.
All inputs are finite; a program needn't handle non-finite values.
Results may differ from the reference program's by a relative error of at most 0.028.
Values may be sent and summed in bfloat16 or wider, within the bound.
A program may use at most 576 MiB of HBM per device.

```python
import math
import jax
import jax.numpy as jnp
import numpy as np
from jax import lax

D = 2048
H = 16
HD = 128
FFE = 1408
FFS = 5632
TOP = 4
MB = 2
NSEQ = 4
TOK_MB = 96
EXPERTS = 8
PIECE = 12
PACK = 384
TOKENS_MB = 3072
LONG = 337
CAP = 72
N_FSDP = 8


def block_levels(stream_key, extent, shards, least, top_value):
    level = 1.0
    for dim, blocks in shards:
        heights = jax.random.uniform(jax.random.fold_in(jax.random.fold_in(stream_key, 6), dim), (blocks,), jnp.float32, least / len(shards), top_value / len(shards))
        level = level * jnp.repeat(jnp.exp(heights), extent[dim] // blocks).reshape((-1,) + (1,) * (len(extent) - 1 - dim))
    return level


def split_up(number_of, total, most, lean):
    portions = [(1 << 20) // math.isqrt(grade ** lean) + 1 for grade in range(2, number_of + 1)]
    spare, given = total - most - (number_of - 1), [1] * (number_of - 1)
    while spare > 0:
        movable = [i for i in range(number_of - 1) if given[i] < most]
        whole, remaining = sum([portions[i] for i in movable]), spare
        for i in movable:
            more = min(most - given[i], max(1, remaining * portions[i] // whole), spare)
            given[i] = given[i] + more
            spare = spare - more
    return np.array([most] + given)


def ragged_sizes(rng, number_of, total, reach, slope):
    if number_of == 2:
        one = jax.random.randint(rng, (), max(1, total - reach), min(reach, total - 1) + 1)
        return jnp.stack([one, total - one])
    sizes = jnp.asarray(split_up(number_of, total, reach, slope), jnp.int32)
    couples = (number_of - 1) // 2
    donor, taker = sizes[1:1 + 2 * couples:2], sizes[2:2 + 2 * couples:2]
    slack = jnp.minimum(donor - 1, reach - taker)
    moved = jax.random.randint(jax.random.fold_in(rng, 1), (couples,), 0, 1 << 20) % (slack + 1)
    sizes = sizes.at[1:1 + 2 * couples:2].set(donor - moved).at[2:2 + 2 * couples:2].set(taker + moved)
    return sizes[jax.random.permutation(jax.random.fold_in(rng, 2), number_of)]


def routed_block(rng, own, number, rows, amount, top, bound, lean):
    sequence = jax.random.permutation(rng, amount)
    crowded, ordinary = load_shares(amount, rows * top, bound, lean, True), load_shares(amount, rows * top, bound, lean, False)
    places = jnp.arange(amount)

    def named(sizes, rotation):
        used = int((sizes > 0).sum())
        fixed = max(1, used // 4)
        passed = fixed + (places - fixed + rotation * (used - fixed)) % max(1, amount - fixed)
        return jnp.zeros((amount,), jnp.int32).at[sequence[jnp.where(places < fixed, places, passed)]].set(jnp.asarray(sizes, jnp.int32))

    sizes = jnp.where(number % 4 == 0, named(crowded, number // 4), named(ordinary, number - number // 4 - 1))
    mixed = jax.random.permutation(jax.random.fold_in(own, 3), amount)
    source_of, taker = mixed[0:amount // 2 * 2:2], mixed[1:amount // 2 * 2:2]
    slack = jnp.minimum(sizes[source_of] - 1, bound - sizes[taker]) // 2
    slack = jnp.where((source_of == sequence[0]) | (taker == sequence[0]) | (sizes[taker] == 0), 0, jnp.maximum(slack, 0))
    passed = jax.random.randint(jax.random.fold_in(own, 4), (amount // 2,), 0, 1 << 20) % (slack + 1)
    sizes = sizes.at[source_of].add(-passed).at[taker].add(passed)
    members = jnp.searchsorted(jnp.cumsum(sizes), jnp.arange(rows * top), side="right").astype(jnp.int32)
    listing = members.reshape(top, rows).T
    listing = listing[jax.random.permutation(jax.random.fold_in(own, 1), rows)]
    rotation = jax.random.randint(jax.random.fold_in(own, 2), (rows, 1), 0, top)
    return jnp.take_along_axis(listing, (jnp.arange(top)[None, :] + rotation) % top, axis=1)


def load_shares(amount, total, limit, lean, full):
    loads = [(1 << 20) // math.isqrt(standing ** lean) + 1 for standing in range(1, amount + 1)]
    largest = limit if full else min(limit, max(-(-total // amount), total * loads[0] // sum(loads)))
    least = 1 if total - largest >= amount - 1 else 0
    holding, surplus = [largest] + [least] * (amount - 1), total - largest - least * (amount - 1)
    while surplus > 0:
        movable = [i for i in range(1, amount) if holding[i] < largest] or [i for i in range(1, amount) if holding[i] < limit]
        mass, budget = sum([loads[i] for i in movable]), surplus
        for i in movable:
            extra = min(limit - holding[i], max(1, budget * loads[i] // mass), surplus)
            holding[i] = holding[i] + extra
            surplus = surplus - extra
    return np.array(holding)


def noise(own_key, dims, spread, reach, pieces=(), kind=jnp.bfloat16):
    factor_of = block_levels(own_key, dims, pieces, -0.22, 0.18) if pieces else 1.0
    array = jax.random.normal(own_key, dims, jnp.float32) * spread * factor_of
    return jnp.minimum(jnp.maximum(array, -reach), reach).astype(kind)


def setup_inputs(seed: int = 0) -> dict:
    key_of = jax.random.split(jax.random.key(seed), 19)
    tokens = noise(key_of[0], (MB, TOKENS_MB, D), 1.0, 6.0, ((1, 32),))
    cotangent = noise(key_of[1], (MB, TOKENS_MB, D), 1.0, 6.0, ((1, 32),))
    ids_keys = jax.random.split(jax.random.fold_in(key_of[2], 1), MB * TOKENS_MB // TOK_MB)
    ids_turns = jax.random.permutation(jax.random.fold_in(key_of[2], 3), MB * TOKENS_MB // TOK_MB)
    ids = jax.vmap(lambda own, number: routed_block(jax.random.fold_in(key_of[2], 2), own, number, TOK_MB, EXPERTS, TOP, CAP, 2))(ids_keys, ids_turns).reshape((MB, TOKENS_MB, TOP))
    deal = jax.vmap(lambda own: jax.random.permutation(own, N_FSDP))(jax.random.split(key_of[3], MB * N_FSDP)).reshape((MB, N_FSDP, N_FSDP)).astype(jnp.int32)
    lengths = jax.vmap(lambda own: ragged_sizes(own, NSEQ, PACK, LONG, 2))(jax.random.split(key_of[4], MB * N_FSDP)).reshape((MB, N_FSDP, NSEQ)).astype(jnp.int32)
    w_qkv = noise(key_of[5], (D, 3 * D), D ** -0.5, 0.125, ((0, 32),))
    b_qkv = noise(key_of[6], (3 * D,), 0.3, 1.5, ((0, 32),))
    w_out = noise(key_of[7], (D, D), (D // 16) ** -0.5, 0.5, ((0, 32),))
    gain_attn = jnp.clip(1.0 + 0.1 * jax.random.normal(key_of[8], (D,), jnp.float32), 0.5, 1.5).astype(jnp.bfloat16)
    gain_ffn = jnp.clip(1.0 + 0.1 * jax.random.normal(key_of[9], (D,), jnp.float32), 0.5, 1.5).astype(jnp.bfloat16)
    w_router = noise(key_of[10], (D, EXPERTS), (4 * D) ** -0.5, 0.0625, ((0, 32),))
    w_shared_gate = noise(key_of[11], (D,), D ** -0.5, 0.125, ((0, 32),))
    e_gate = noise(key_of[12], (EXPERTS, D, FFE), D ** -0.5, 0.125, ((0, 8), (1, 4)))
    e_up = noise(key_of[13], (EXPERTS, D, FFE), D ** -0.5, 0.125, ((0, 8), (1, 4)))
    e_down = noise(key_of[14], (EXPERTS, FFE, D), (max(1, 2 * FFE // (EXPERTS * EXPERTS))) ** -0.5, 0.875, ((0, 8), (2, 4)))
    s_gate = noise(key_of[15], (D, FFS), D ** -0.5, 0.125, ((0, 4), (1, 8)))
    s_up = noise(key_of[16], (D, FFS), D ** -0.5, 0.125, ((0, 4), (1, 8)))
    s_down = noise(key_of[17], (FFS, D), (FFS // 8) ** -0.5, 0.21875, ((0, 8), (1, 4)))
    return dict(tokens=tokens, cotangent=cotangent, ids=ids, deal=deal, lengths=lengths, w_qkv=w_qkv, b_qkv=b_qkv, w_out=w_out, gain_attn=gain_attn, gain_ffn=gain_ffn, w_router=w_router, w_shared_gate=w_shared_gate, e_gate=e_gate, e_up=e_up, e_down=e_down, s_gate=s_gate, s_up=s_up, s_down=s_down)


@jax.custom_vjp
def low(v):
    return lax.optimization_barrier(v.astype(jnp.bfloat16)).astype(jnp.float32)

@jax.custom_vjp
def low_back(v):
    return v

def low_keep(v):
    return (low(v), None)

def low_pass(kept, grad):
    return (grad,)

def back_keep(v):
    return (v, None)

def back_low(kept, grad):
    return (low(grad),)
low.defvjp(low_keep, low_pass)
low_back.defvjp(back_keep, back_low)
eps = 1e-06
theta = 1000000.0
masked_score = -1e+30

def matmul(left, right):
    return jnp.dot(left, right, precision=lax.Precision.HIGHEST)

def sigmoid_linear(values):
    return values * jax.nn.sigmoid(values)

def rms_norm(values, gain):
    inverse = lax.rsqrt(lax.optimization_barrier(jnp.mean(values * values, axis=-1, keepdims=True)) + eps)
    return values * inverse * gain

def rotate(values, cosine, sine):
    half = values.shape[-1] // 2
    turned = jnp.concatenate([-values[..., half:], values[..., :half]], axis=-1)
    return values * cosine + turned * sine

def rotary(position):
    frequency = theta ** (-jnp.arange(0, HD, 2, dtype=jnp.float32) / HD)
    angle = position.astype(jnp.float32)[:, None] * frequency[None, :]
    angle = jnp.concatenate([angle, angle], axis=1)
    return (jnp.cos(angle), jnp.sin(angle))

def layout(deal_table, length_table):
    rows = jnp.arange(TOKENS_MB, dtype=jnp.int32)
    block_index = rows // TOK_MB
    seq_part = block_index // N_FSDP
    source = block_index % N_FSDP
    within = rows % TOK_MB
    start_shift = within // N_FSDP
    piece = within % N_FSDP
    group = deal_table[source, piece]
    place = (seq_part * PIECE + start_shift) * N_FSDP + source
    ends = jnp.cumsum(length_table, axis=1).astype(jnp.int32)
    row_ends = ends[group]
    row_lengths = length_table[group]
    start = lax.optimization_barrier(jnp.sum(jnp.where(row_ends <= place[:, None], row_lengths, 0), axis=1)).astype(jnp.int32)
    position = place - start
    flat = (group * PACK + place).astype(jnp.int32)
    order = jnp.argsort(flat).astype(jnp.int32)
    spots = jnp.arange(PACK, dtype=jnp.int32)
    segment = lax.optimization_barrier(jnp.sum((ends[:, None, :] <= spots[None, :, None]).astype(jnp.int32), axis=2))
    return (position, flat, order, segment)

def attend(inputs):
    query, key, value, segment = inputs
    raw = low_back(jnp.einsum('qhd,khd->hqk', query, key, precision=lax.Precision.HIGHEST))
    scores = raw * HD ** (-0.5)
    spots = jnp.arange(PACK, dtype=jnp.int32)
    allowed = (segment[:, None] == segment[None, :]) & (spots[None, :] <= spots[:, None])
    scores = jnp.where(allowed[None], scores, masked_score)
    weights = jnp.exp(scores - lax.optimization_barrier(jnp.max(scores, axis=-1, keepdims=True)))
    chance = low(weights / lax.optimization_barrier(jnp.sum(weights, axis=-1, keepdims=True)))
    return jnp.einsum('hqk,khd->qhd', chance, value, precision=lax.Precision.HIGHEST)

def forward(params, tokens, ids, cosine, sine, flat, order, segment):
    w_qkv, b_qkv, w_out, gain_attn, gain_ffn, w_router, w_shared_gate, e_gate, e_up, e_down, s_gate, s_up, s_down = params
    normed = low(rms_norm(tokens, gain_attn))
    projected = low_back(matmul(normed, w_qkv) + b_qkv).reshape(TOKENS_MB, 3, H, HD)
    cos_rows = cosine[:, None, :]
    sin_rows = sine[:, None, :]
    moved = jnp.stack([rotate(projected[:, 0], cos_rows, sin_rows), rotate(projected[:, 1], cos_rows, sin_rows), projected[:, 2]], axis=1)
    moved = low(low_back(moved))
    packed = moved[order].reshape(N_FSDP, PACK, 3, H, HD)
    context = lax.map(jax.checkpoint(attend), (packed[:, :, 0], packed[:, :, 1], packed[:, :, 2], segment))
    context = context.reshape(TOKENS_MB, D)[flat]
    context = low(low_back(context))
    hidden = tokens + low_back(matmul(context, w_out))
    normed2 = low(rms_norm(hidden, gain_ffn))
    logits = low_back(matmul(normed2, w_router))
    shifted = jnp.exp(logits - lax.optimization_barrier(jnp.max(logits, axis=-1, keepdims=True)))
    router = shifted / lax.optimization_barrier(jnp.sum(shifted, axis=-1, keepdims=True))
    choose = (ids[:, :, None] == jnp.arange(EXPERTS, dtype=jnp.int32)[None, None, :]).astype(jnp.float32)
    gates = lax.optimization_barrier(jnp.sum(router[:, None, :] * choose, axis=2))
    share = lax.optimization_barrier(jnp.sum(gates[:, :, None] * choose, axis=1)).T

    def expert_pass(total, weights):
        gate_weight, up_weight, down_weight, portion = weights
        entry = low_back(normed2)
        gate = low_back(matmul(entry, gate_weight))
        upward = low_back(matmul(entry, up_weight))
        activation = low(sigmoid_linear(gate) * upward)
        result = low(low_back(matmul(activation, down_weight)))
        return (total + portion[:, None] * result, None)
    routed, _ = lax.scan(jax.checkpoint(expert_pass), jnp.zeros_like(tokens), (e_gate, e_up, e_down, share))
    shared_gate = low_back(matmul(normed2, s_gate))
    shared_up = low_back(matmul(normed2, s_up))
    shared_act = low(sigmoid_linear(shared_gate) * shared_up)
    shared_out = low_back(matmul(shared_act, s_down))
    sigma = jax.nn.sigmoid(matmul(normed2, w_shared_gate))
    return hidden + routed + sigma[:, None] * shared_out

def reference(tokens, cotangent, ids, deal, lengths, w_qkv, b_qkv, w_out, gain_attn, gain_ffn, w_router, w_shared_gate, e_gate, e_up, e_down, s_gate, s_up, s_down):
    params = tuple((weight.astype(jnp.float32) for weight in (w_qkv, b_qkv, w_out, gain_attn, gain_ffn, w_router, w_shared_gate, e_gate, e_up, e_down, s_gate, s_up, s_down)))
    mixed_parts = []
    input_grads = []
    totals = None
    for micro in range(MB):
        position, flat, order, segment = layout(deal[micro], lengths[micro])
        cosine, sine = rotary(position)
        chosen = ids[micro]

        def layer(tokens_in, weights):
            return forward(weights, tokens_in, chosen, cosine, sine, flat, order, segment)
        result, pullback = jax.vjp(layer, tokens[micro].astype(jnp.float32), params)
        grad_in, grad_params = pullback(cotangent[micro].astype(jnp.float32))
        mixed_parts.append(result.astype(jnp.bfloat16))
        input_grads.append(grad_in)
        if totals is None:
            totals = grad_params
        else:
            totals = jax.tree.map(jnp.add, totals, grad_params)
    return (jnp.stack(mixed_parts), jnp.stack(input_grads), totals[0], totals[1], totals[2], totals[3], totals[4], totals[5], totals[6], totals[7], totals[8], totals[9], totals[10], totals[11], totals[12])
```

```python
import jax
import jax.numpy as jnp
from jax import lax
from jax.sharding import PartitionSpec as P

H = 16
HD = 128
TOP = 4
EPS = 1e-06
THETA = 1000000.0
MASKED = -1e30
F32 = jnp.float32
BF16 = jnp.bfloat16

ORDER = ((0, 0), (0, 1), (2, 0), (1, 1), (1, 0), (3, 0), (2, 1), (3, 1))


def dot(a, b):
    return jnp.dot(a, b, preferred_element_type=F32)


def dot_t(a, b):
    return lax.dot_general(a, b, (((0,), (0,)), ((), ())), preferred_element_type=F32)


def dot_nt(a, b):
    return lax.dot_general(a, b, (((1,), (1,)), ((), ())), preferred_element_type=F32)


def turn(u):
    half = u.shape[-1] // 2
    return jnp.concatenate([-u[..., half:], u[..., :half]], axis=-1)


def turn_back(u):
    half = u.shape[-1] // 2
    return jnp.concatenate([u[..., half:], -u[..., :half]], axis=-1)


def rms_forward(values):
    inverse = lax.rsqrt(jnp.mean(values * values, axis=-1, keepdims=True) + EPS)
    return values * inverse, inverse


def rms_backward(grad, unit, inverse, gain):
    scaled = grad * gain
    grad_gain = jnp.sum(grad * unit, axis=tuple(range(grad.ndim - 1)))
    return inverse * (scaled - unit * jnp.mean(scaled * unit, axis=-1, keepdims=True)), grad_gain


def across(a, which):
    return lax.ppermute(a, "seq", [(i, i ^ which) for i in range(4)])


def split3(v):
    hi = lax.reduce_precision(v, 8, 7)
    mid = lax.reduce_precision(v - hi, 8, 7)
    low = lax.reduce_precision(v - hi - mid, 8, 7)
    return hi, mid, low


def swiglu_back(grad_act, gate, up):
    sig = jax.nn.sigmoid(gate)
    grad_gate = (grad_act * up * sig * (1.0 + gate * (1.0 - sig))).astype(BF16)
    grad_up = (grad_act * gate * sig).astype(BF16)
    return grad_gate, grad_up


def gather_in(a, b):
    half = a.shape[0] // 2
    ax, ay = across(a, 1), across(a, 2)
    ad0, ad1 = across(ax[:half], 2), across(ay[half:], 1)
    full_a = jnp.concatenate([a, ay[:half], ax[half:], ax[:half], ad0, ay[half:], ad1], axis=0)
    bx, by = across(b, 1), across(b, 2)
    bd0, bd1 = across(bx[:, :half], 2), across(by[:, half:], 1)
    full_b = jnp.concatenate(
        [b, by[:, :half], bx[:, half:], bx[:, :half], bd0, by[:, half:], bd1], axis=1
    )
    return full_a, full_b


def shards(
    tokens, cotangent, ids, deal, lengths, w_qkv, b_qkv, w_out, gain_attn, gain_ffn, w_router,
    w_shared_gate, e_gate, e_up, e_down, s_gate, s_up, s_down,
):
    S, N = lax.axis_size("seq"), lax.axis_size("fsdp")
    s, f = lax.axis_index("seq"), lax.axis_index("fsdp")
    MB, T, D = tokens.shape
    E = w_router.shape[1]
    assert S == 4 and e_gate.shape[0] == 1 and E == N
    FE, FS = e_gate.shape[2], s_gate.shape[1]
    piece = T // N
    pack = T * S
    heads = H // S
    width = heads * HD
    rows = N * MB * T
    own = w_out.shape[0]

    stack_a = jnp.concatenate([e_gate[0], e_up[0], s_gate, s_up], axis=1)
    stack_b = jnp.concatenate([e_down[0], s_down], axis=0)
    full_a, full_b = gather_in(stack_a, stack_b)

    small = jnp.concatenate([gain_attn, gain_ffn, w_router.reshape(-1), w_shared_gate, b_qkv])
    small = lax.all_gather(small, ("seq", "fsdp"), axis=0)
    cuts = (own, 2 * own, 2 * own + own * E, 3 * own + own * E)
    gain_1 = small[:, : cuts[0]].reshape(D).astype(F32)
    gain_2 = small[:, cuts[0] : cuts[1]].reshape(D).astype(F32)
    router_w = small[:, cuts[1] : cuts[2]].reshape(D, E)
    shared_w = small[:, cuts[2] : cuts[3]].reshape(D)
    bias = lax.dynamic_slice_in_dim(small[:, cuts[3] :].reshape(3, S, width), s, 1, 1)
    bias = bias.reshape(3 * width).astype(F32)

    w = lax.all_to_all(w_qkv.reshape(own, 3, S, width), "seq", split_axis=2, concat_axis=0, tiled=True)
    w = lax.all_gather(w.reshape(S, own, 3 * width), "fsdp", axis=1, tiled=True)
    w_in = w.reshape(D, 3 * width)
    w_back = lax.all_gather(w_out, "fsdp", axis=0, tiled=True)

    pad = 128
    extra = jnp.pad(ids.astype(BF16), ((0, 0), (0, 0), (0, pad - TOP)))
    send = jnp.concatenate([tokens, cotangent, extra], axis=2).reshape(MB, piece, N, 2 * D + pad)
    inverse_deal = jnp.argsort(deal[:, f], axis=1)
    send = jnp.stack([jnp.take(send[m], inverse_deal[m], axis=1) for m in range(MB)])
    dealt = lax.all_to_all(send, "fsdp", split_axis=2, concat_axis=2, tiled=True)
    dealt = dealt.reshape(MB, T, 2 * D + pad)
    x0 = dealt[..., :D].astype(F32)
    cot = dealt[..., D : 2 * D]
    tags = dealt[..., 2 * D :]

    order = jnp.stack([jnp.bitwise_xor(s, rel) * 2 + half for rel, half in ORDER])
    inverse_order = jnp.argsort(order)

    def arrange(u, by):
        return jnp.take(u.reshape(u.shape[:-1] + (8, D // 8)), by, axis=u.ndim - 1).reshape(u.shape)

    g_all = lax.all_gather(
        jnp.concatenate([arrange(cot, order), tags], axis=2).reshape(MB * T, D + pad), "fsdp", axis=0, tiled=True
    )
    g_rows = g_all[:, :D]
    chosen = g_all[:, D : D + TOP].astype(jnp.int32)

    ends = jnp.cumsum(lengths[:, f], axis=1)
    spots = jnp.arange(pack, dtype=jnp.int32)
    past = ends[:, None, :] <= spots[None, :, None]
    segment = jnp.sum(past.astype(jnp.int32), axis=2)
    start = jnp.sum(jnp.where(past, lengths[:, f][:, None, :], 0), axis=2)
    frequency = THETA ** (-jnp.arange(0, HD, 2, dtype=F32) / HD)
    angle = (spots[None] - start).astype(F32)[..., None] * frequency
    angle = jnp.concatenate([angle, angle], axis=2)
    cosine, sine = jnp.cos(angle)[:, None, None], jnp.sin(angle)[:, None, None]
    allowed = (segment[:, :, None] == segment[:, None, :]) & (spots[None, None, :] <= spots[None, :, None])
    allowed = allowed[:, None]

    unit_1, inverse_1 = rms_forward(x0)
    normed = (unit_1 * gain_1).astype(BF16)
    normed_all = lax.all_gather(normed, "seq", axis=1, tiled=True)
    flat = normed_all.reshape(MB * pack, D)
    qkv = (dot(flat, w_in) + bias).reshape(MB, pack, 3, heads, HD).transpose(0, 2, 3, 1, 4)
    qk = qkv[:, :2]
    qk = (qk * cosine + turn(qk) * sine).astype(BF16)
    q, k, v = qk[:, 0], qk[:, 1], qkv[:, 2].astype(BF16)
    scale = HD ** -0.5
    raw = jnp.einsum("mhqd,mhkd->mhqk", q, k, preferred_element_type=F32)
    scores = jnp.where(allowed, raw * scale, MASKED)
    weights = jnp.exp(scores - jnp.max(scores, axis=-1, keepdims=True))
    chance = weights / jnp.sum(weights, axis=-1, keepdims=True)
    chance_low = chance.astype(BF16)
    context = jnp.einsum("mhqk,mhkd->mqhd", chance_low, v, preferred_element_type=F32).astype(BF16)
    context = context.reshape(MB * pack, width)
    partial = dot(context, w_back).astype(BF16).reshape(MB, S, T, D)
    partial = lax.all_to_all(partial, "seq", split_axis=1, concat_axis=1, tiled=True)
    hidden = x0 + jnp.sum(partial.astype(F32), axis=1)
    unit_2, inverse_2 = rms_forward(hidden)
    normed2 = (unit_2 * gain_2).astype(BF16)

    x = lax.all_gather(arrange(normed2, order).reshape(MB * T, D), "fsdp", axis=0, tiled=True)
    lead = jnp.concatenate([router_w, shared_w[:, None]], axis=1)
    lead_order = jnp.take(lead.reshape(8, D // 8, E + 1), order, axis=0).reshape(D, E + 1)
    logits = dot(x, lead_order)
    shifted = jnp.exp(logits[:, :E] - jnp.max(logits[:, :E], axis=-1, keepdims=True))
    router_f = jnp.sum(jnp.where(jnp.arange(E) == f, shifted, 0.0), axis=1) / jnp.sum(shifted, axis=1)
    gate_f = jnp.where(jnp.any(chosen == f, axis=1), router_f, 0.0)[:, None]
    sigma_rows = jax.nn.sigmoid(logits[:, E])[:, None]
    g32 = g_rows.astype(F32)
    geo = (gate_f * g32).astype(BF16)
    gso = (sigma_rows * g32).astype(BF16)

    eg, eu, sg, su = jnp.split(full_a, (FE, 2 * FE, 2 * FE + FS), axis=1)
    ed, sd = full_b[:FE], full_b[FE:]
    gate, up = dot(x, eg), dot(x, eu)
    act = (jax.nn.silu(gate) * up).astype(BF16)
    out_e = dot(act, ed).astype(BF16).astype(F32)
    sgate, sup = dot(x, sg), dot(x, su)
    sact = (jax.nn.silu(sgate) * sup).astype(BF16)
    out_s = dot(sact, sd)
    y = (gate_f * out_e + sigma_rows * out_s).astype(BF16)
    y = lax.psum_scatter(y, "fsdp", scatter_dimension=0, tiled=True)
    gg = jnp.sum(g32 * out_e, axis=1)
    gs = jnp.sum(g32 * out_s, axis=1)

    grad_gate, grad_up = swiglu_back(dot_nt(geo, ed), gate, up)
    grad_sgate, grad_sup = swiglu_back(dot_nt(gso, sd), sgate, sup)
    dx_e = (dot_nt(grad_gate, eg) + dot_nt(grad_up, eu)).astype(BF16).astype(F32)
    dx = dx_e + dot_nt(grad_sgate, sg) + dot_nt(grad_sup, su)
    mine = (jnp.arange(N) == f).astype(F32)
    notes = [part[:, None] * mine for value in (gg, gs) for part in split3(value)]
    note_pad = -(6 * N) % 128
    payload = jnp.concatenate([dx] + notes + [jnp.zeros((rows, note_pad), F32)], axis=1).astype(BF16)
    dx = lax.psum_scatter(payload, "fsdp", scatter_dimension=0, tiled=True).astype(F32)

    cat_grad = jnp.concatenate([grad_gate, grad_up, grad_sgate, grad_sup], axis=1)
    half = D // 8
    send_x = dot_t(x[:, 4 * half : 6 * half], cat_grad).astype(BF16)
    send_y = dot_t(x[:, 6 * half :], cat_grad).astype(BF16)
    from_x, from_y = across(send_x, 1), across(send_y, 2)

    def down_grad(lo, hi):
        return jnp.concatenate([dot_t(act, geo[:, lo:hi]), dot_t(sact, gso[:, lo:hi])], axis=0)

    bsend_x = down_grad(4 * half, 6 * half).astype(BF16)
    bsend_y = down_grad(6 * half, 8 * half).astype(BF16)
    bfrom_x, bfrom_y = across(bsend_x, 1), across(bsend_y, 2)
    keep = dot_t(x[:, : 4 * half], cat_grad)
    bkeep = down_grad(0, 4 * half)
    to_y = (keep[2 * half : 3 * half] + from_x[half:].astype(F32)).astype(BF16)
    to_x = (keep[3 * half :] + from_y[half:].astype(F32)).astype(BF16)
    last_y, last_x = across(to_y, 2), across(to_x, 1)
    bto_y = (bkeep[:, 2 * half : 3 * half] + bfrom_x[:, half:].astype(F32)).astype(BF16)
    bto_x = (bkeep[:, 3 * half :] + bfrom_y[:, half:].astype(F32)).astype(BF16)
    blast_y, blast_x = across(bto_y, 2), across(bto_x, 1)
    grad_a = jnp.concatenate(
        [
            keep[:half] + from_x[:half].astype(F32) + last_y.astype(F32),
            keep[half : 2 * half] + from_y[:half].astype(F32) + last_x.astype(F32),
        ],
        axis=0,
    )
    grad_b = jnp.concatenate(
        [
            bkeep[:, :half] + bfrom_x[:, :half].astype(F32) + blast_y.astype(F32),
            bkeep[:, half : 2 * half] + bfrom_y[:, :half].astype(F32) + blast_x.astype(F32),
        ],
        axis=1,
    )
    g_eg, g_eu, g_sg, g_su = jnp.split(grad_a, (FE, 2 * FE, 2 * FE + FS), axis=1)

    y = arrange(y.astype(F32).reshape(MB, T, D), inverse_order)
    mixed = (hidden + y).astype(BF16)
    base = D
    gg_own = sum(dx[:, base + i * N : base + (i + 1) * N] for i in range(3))
    gs_own = jnp.sum(dx[:, base + 3 * N : base + 6 * N], axis=1)
    grad_normed2 = arrange(dx[:, :D], inverse_order)
    flat2 = normed2.reshape(MB * T, D)
    logits = dot(flat2, lead)
    shifted = jnp.exp(logits[:, :E] - jnp.max(logits[:, :E], axis=-1, keepdims=True))
    router = shifted / jnp.sum(shifted, axis=-1, keepdims=True)
    sigma = jax.nn.sigmoid(logits[:, E])
    own_ids = tags[..., :TOP].reshape(MB * T, TOP).astype(jnp.int32)
    picked = jnp.any(own_ids[:, :, None] == jnp.arange(E)[None, None, :], axis=1)
    grad_router = jnp.where(picked, gg_own, 0.0)
    grad_logits = (router * (grad_router - jnp.sum(router * grad_router, axis=-1, keepdims=True))).astype(BF16)
    grad_sigma = gs_own * sigma * (1.0 - sigma)
    grad_normed2 = grad_normed2 + dot_nt(grad_logits, router_w) + grad_sigma[:, None] * shared_w.astype(F32)[None, :]
    g_router = dot_t(flat2, grad_logits)
    g_shared = jnp.sum(grad_sigma[:, None] * flat2.astype(F32), axis=0)
    from_norm, g_gain_2 = rms_backward(grad_normed2.reshape(MB, T, D), unit_2, inverse_2, gain_2)
    grad_hidden = cot.astype(F32) + from_norm

    grad_attn = lax.all_gather(grad_hidden.astype(BF16), "seq", axis=1, tiled=True).reshape(MB * pack, D)
    g_out = dot_t(context, grad_attn)
    gc = dot_nt(grad_attn, w_back).astype(BF16).reshape(MB, pack, heads, HD).transpose(0, 2, 1, 3)
    grad_chance = jnp.einsum("mhqd,mhkd->mhqk", gc, v, preferred_element_type=F32)
    delta = jnp.sum(chance * grad_chance, axis=-1, keepdims=True)
    grad_raw = (chance * (grad_chance - delta) * scale).astype(BF16)
    gq = jnp.einsum("mhqk,mhkd->mhqd", grad_raw, k, preferred_element_type=F32)
    gk = jnp.einsum("mhqk,mhqd->mhkd", grad_raw, q, preferred_element_type=F32)
    gv = jnp.einsum("mhqk,mhqd->mhkd", chance_low, gc, preferred_element_type=F32)
    gqk = jnp.stack([gq, gk], axis=1).astype(BF16).astype(F32)
    gqk = (gqk * cosine + turn_back(gqk * sine)).astype(BF16)
    grad_qkv = jnp.concatenate([gqk, gv.astype(BF16)[:, None]], axis=1).transpose(0, 3, 1, 2, 4)
    grad_qkv = grad_qkv.reshape(MB * pack, 3 * width)
    g_bias = jnp.sum(grad_qkv.astype(F32), axis=0)
    g_in = dot_t(flat, grad_qkv)
    partial = dot_nt(grad_qkv, w_in).astype(BF16).reshape(MB, S, T, D)
    partial = lax.all_to_all(partial, "seq", split_axis=1, concat_axis=1, tiled=True)
    grad_normed = jnp.sum(partial.astype(F32), axis=1)
    from_first, g_gain_1 = rms_backward(grad_normed, unit_1, inverse_1, gain_1)
    grad_x = (grad_hidden + from_first).astype(BF16)

    back = jnp.concatenate([mixed, grad_x], axis=2).reshape(MB, piece, N, 2 * D)
    back = lax.all_to_all(back, "fsdp", split_axis=2, concat_axis=2, tiled=True)
    back = jnp.stack([jnp.take(back[m], deal[m, f], axis=1) for m in range(MB)]).reshape(MB, T, 2 * D)
    mixed, grad_tokens = back[..., :D], back[..., D:].astype(F32)

    g_in = lax.psum_scatter(g_in.astype(BF16).reshape(S, N * own, 3 * width), "fsdp", scatter_dimension=1, tiled=True)
    g_in = lax.all_to_all(g_in, "seq", split_axis=0, concat_axis=0, tiled=True)
    g_in = g_in.reshape(S, own, 3, width).transpose(1, 2, 0, 3).reshape(own, 3 * D).astype(F32)
    g_out = lax.psum_scatter(g_out.astype(BF16), "fsdp", scatter_dimension=0, tiled=True).astype(F32)
    g_bias = jnp.where(jnp.arange(S)[None, :, None] == s, g_bias.reshape(3, 1, width), 0.0)
    count = S * N
    small = jnp.concatenate(
        [
            g_gain_1.reshape(count, own), g_gain_2.reshape(count, own), g_router.reshape(count, own * E),
            g_shared.reshape(count, own), g_bias.reshape(count, 3 * own),
        ],
        axis=1,
    )
    small = lax.psum_scatter(small, ("seq", "fsdp"), scatter_dimension=0, tiled=True)[0]
    return (
        mixed, grad_tokens, g_in, small[cuts[3] :], g_out, small[: cuts[0]], small[cuts[0] : cuts[1]],
        small[cuts[1] : cuts[2]].reshape(own, E), small[cuts[2] : cuts[3]],
        g_eg[None], g_eu[None], grad_b[:FE][None], g_sg, g_su, grad_b[FE:],
    )


def solution(mesh):
    both = ("seq", "fsdp")
    in_specs = (
        P(None, both, None), P(None, both, None), P(None, both, None), P(), P(), P(both, None), P(both), P(both, None),
        P(both), P(both), P(both, None), P(both), P("fsdp", "seq", None), P("fsdp", "seq", None),
        P("fsdp", None, "seq"), P("seq", "fsdp"), P("seq", "fsdp"), P("fsdp", "seq"),
    )
    out_specs = (
        P(None, both, None), P(None, both, None), P(both, None), P(both), P(both, None), P(both), P(both),
        P(both, None), P(both), P("fsdp", "seq", None), P("fsdp", "seq", None), P("fsdp", None, "seq"),
        P("seq", "fsdp"), P("seq", "fsdp"), P("fsdp", "seq"),
    )
    return jax.shard_map(shards, mesh=mesh, in_specs=in_specs, out_specs=out_specs, check_vma=False)
```

```python
import functools

import jax
import jax.numpy as jnp
from jax import lax
from jax.experimental import pallas as pl
from jax.experimental.pallas import tpu as pltpu
from jax.sharding import PartitionSpec as P

H = 16
HD = 128
TOP = 4
EPS = 1e-06
THETA = 1000000.0
MASKED = -1e30
F32 = jnp.float32
BF16 = jnp.bfloat16
MESH = pl.DeviceIdType.MESH
VMEM_LIMIT = 56 * 2**20

ORDER = ((0, 0), (0, 1), (2, 0), (1, 1), (1, 0), (3, 0), (2, 1), (3, 1))


def dot(a, b):
    return jnp.dot(a, b, preferred_element_type=F32)


def dot_t(a, b):
    return lax.dot_general(a, b, (((0,), (0,)), ((), ())), preferred_element_type=F32)


def dot_nt(a, b):
    return lax.dot_general(a, b, (((1,), (1,)), ((), ())), preferred_element_type=F32)


def turn(u):
    half = u.shape[-1] // 2
    return jnp.concatenate([-u[..., half:], u[..., :half]], axis=-1)


def turn_back(u):
    half = u.shape[-1] // 2
    return jnp.concatenate([u[..., half:], -u[..., :half]], axis=-1)


def rms_forward(values):
    inverse = lax.rsqrt(jnp.mean(values * values, axis=-1, keepdims=True) + EPS)
    return values * inverse, inverse


def rms_backward(grad, unit, inverse, gain):
    scaled = grad * gain
    grad_gain = jnp.sum(grad * unit, axis=tuple(range(grad.ndim - 1)))
    return inverse * (scaled - unit * jnp.mean(scaled * unit, axis=-1, keepdims=True)), grad_gain


def across(a, which):
    return lax.ppermute(a, "seq", [(i, i ^ which) for i in range(4)])


def split3(v):
    hi = lax.reduce_precision(v, 8, 7)
    mid = lax.reduce_precision(v - hi, 8, 7)
    low = lax.reduce_precision(v - hi - mid, 8, 7)
    return hi, mid, low


def swiglu_back(grad_act, gate, up):
    sig = jax.nn.sigmoid(gate)
    grad_gate = (grad_act * up * sig * (1.0 + gate * (1.0 - sig))).astype(BF16)
    grad_up = (grad_act * gate * sig).astype(BF16)
    return grad_gate, grad_up


def partners(s):
    return s + 1 - 2 * lax.rem(s, 2), lax.rem(s + 2, 4), 3 - s


def greet(s, f, S, N):
    barrier = pltpu.get_barrier_semaphore()
    for other in partners(s):
        pl.semaphore_signal(barrier, inc=1, device_id=(other, f), device_id_type=MESH)
    for step in range(1, N):
        pl.semaphore_signal(barrier, inc=1, device_id=(s, lax.rem(f + step, N)), device_id_type=MESH)
    pl.semaphore_wait(barrier, S - 1 + N - 1)


class Line:
    def __init__(self, s, f, N, block, move_send, move_recv, side_send, side_recv):
        self.s, self.chip, self.core, self.n = s, f // 2, lax.rem(f, 2), N // 2
        self.block = block
        self.move_send, self.move_recv = move_send, move_recv
        self.side_send, self.side_recv = side_send, side_recv

    def move(self, way, step, origin, to):
        ref = self.block(2 * origin + self.core)
        return pltpu.make_async_remote_copy(
            ref, ref, self.move_send.at[way, step], self.move_recv.at[way, step],
            device_id=(self.s, 2 * to + self.core), device_id_type=MESH,
        )

    def side(self, origin, core):
        ref = self.block(2 * origin + core)
        return pltpu.make_async_remote_copy(
            ref, ref, self.side_send.at[origin], self.side_recv.at[origin],
            device_id=(self.s, 2 * self.chip + 1 - self.core), device_id_type=MESH,
        )

    def send(self, step, act):
        q, n = self.chip, self.n

        @pl.when((q - step >= 0) & (q + 1 < n))
        def _():
            act(self.move(0, step, jnp.maximum(q - step, 0), jnp.minimum(q + 1, n - 1)))

        @pl.when((q + step < n) & (q >= 1))
        def _():
            act(self.move(1, step, jnp.minimum(q + step, n - 1), jnp.maximum(q - 1, 0)))

    def begin(self):
        self.send(0, lambda copy: copy.start())
        self.side(self.chip, self.core).start()

    def step(self, step):
        q, n = self.chip, self.n

        @pl.when(q - 1 - step >= 0)
        def _():
            origin = jnp.maximum(q - 1 - step, 0)
            self.move(0, step, origin, jnp.maximum(q - 1, 0)).wait_recv()
            if step + 1 < n - 1:

                @pl.when(q + 1 < n)
                def _():
                    self.move(0, step + 1, origin, jnp.minimum(q + 1, n - 1)).start()

            self.side(origin, self.core).start()

        @pl.when(q + 1 + step < n)
        def _():
            origin = jnp.minimum(q + 1 + step, n - 1)
            self.move(1, step, origin, jnp.minimum(q + 1, n - 1)).wait_recv()
            if step + 1 < n - 1:

                @pl.when(q >= 1)
                def _():
                    self.move(1, step + 1, origin, jnp.maximum(q - 1, 0)).start()

            self.side(origin, self.core).start()

    def finish(self):
        for step in range(self.n - 1):
            self.send(step, lambda copy: copy.wait_send())
        for origin in range(self.n):
            self.side(origin, self.core).wait_send()
            self.side(origin, 1 - self.core).wait_recv()


PLACE = {key: i for i, key in enumerate(ORDER)}


def prologue_kernel(
    S, N, shapes, tok, cot, wq, wo, small, *rest,
):
    shards_in, rest = rest[:6], rest[6:]
    d_tok, g_all, w_in, w_back, small_all, *rest = rest
    fulls, rest = rest[:6], rest[6:]
    bounce, rest = rest[:11], rest[11:]
    local_sem, deal_send, deal_recv, seq_send, seq_recv, small_send, small_recv, half_send, half_recv, *line_sems = rest
    s, f = lax.axis_index("seq"), lax.axis_index("fsdp")
    px, py, pd = partners(s)
    eighth = shapes[0]

    def spot(full, i, place):
        cut = pl.ds(place * eighth, eighth)
        return full.at[cut] if i < 4 else full.at[:, cut]

    def own_half(shard, i, half):
        cut = pl.ds(half * eighth, eighth)
        return shard.at[cut] if i < 4 else shard.at[:, cut]

    places = [small_all.at[f, s], w_in.at[s, f], w_back.at[f], d_tok.at[f], g_all.at[f, f]]
    for i in range(6):
        cut = pl.ds(0, 2 * eighth)
        places.append(fulls[i].at[cut] if i < 4 else fulls[i].at[:, cut])
    sources = [small, wq.at[s], wo, tok.at[f], cot.at[f], *shards_in]
    take = [pltpu.make_async_copy(src, by, local_sem.at[i]) for i, (src, by) in enumerate(zip(sources, bounce))]
    put = [pltpu.make_async_copy(by, dst, local_sem.at[i]) for i, (by, dst) in enumerate(zip(bounce, places))]
    for copy in take:
        copy.start()
    greet(s, f, S, N)

    def remote(src, dst, send, recv, device):
        return pltpu.make_async_remote_copy(src, dst, send, recv, device_id=device, device_id_type=MESH)

    over_seq = []
    for k, other in enumerate((px, py, pd)):
        over_seq.append(remote(small, small_all.at[f, s], seq_send.at[0, k], seq_recv.at[0, k], (other, f)))
        over_seq.append(remote(wq.at[other], w_in.at[s, f], seq_send.at[1, k], seq_recv.at[1, k], (other, f)))
    for copy in over_seq:
        copy.start()
    dealt = []
    for k in range(1, N):
        to = lax.rem(f + k, N)
        dealt.append(remote(tok.at[to], d_tok.at[f], deal_send.at[0, k - 1], deal_recv.at[0, k - 1], (s, to)))
    for k in range(1, N):
        to = lax.rem(f + k, N)
        dealt.append(remote(cot.at[to], g_all.at[to, f], deal_send.at[1, k - 1], deal_recv.at[1, k - 1], (s, to)))
    for copy in dealt:
        copy.start()

    def half_copy(i, k):
        where, rel, half = ((px, 1, 0), (py, 2, 1), (py, 2, 0), (px, 1, 1))[k]
        return remote(
            own_half(shards_in[i], i, half), spot(fulls[i], i, PLACE[rel, half]), half_send.at[i, k], half_recv.at[i, k],
            (where, f),
        )

    def pass_on(i, k):
        where, rel, half = ((py, 1, 0), (px, 2, 1))[k]
        return remote(
            spot(fulls[i], i, PLACE[rel, half]), spot(fulls[i], i, PLACE[3, half]), half_send.at[i, 4 + k],
            half_recv.at[i, 4 + k], (where, f),
        )

    for i in range(6):
        for k in range(4):
            half_copy(i, k).start()

    for copy, after in zip(take, put):
        copy.wait()
        after.start()
    for copy in put:
        copy.wait()
    for copy in over_seq:
        copy.wait_recv()
    to_all = []
    for k in range(1, N):
        to = lax.rem(f + k, N)
        to_all.append(remote(small_all.at[f], small_all.at[f], small_send.at[k - 1], small_recv.at[k - 1], (s, to)))
    for copy in to_all:
        copy.start()
    lines = [
        Line(s, f, N, lambda j: w_in.at[:, j], *line_sems[0:4]),
        Line(s, f, N, lambda j: w_back.at[j], *line_sems[4:8]),
        Line(s, f, N, lambda j: g_all.at[j], *line_sems[8:12]),
    ]
    lines[0].begin()
    lines[1].begin()
    for copy in dealt:
        copy.wait_recv()
    for step in range(N // 2 - 1):
        lines[0].step(step)
        lines[1].step(step)
    lines[2].begin()
    for step in range(N // 2 - 1):
        lines[2].step(step)
    for i in range(6):
        for k in range(2):
            half_copy(i, k).wait_recv()
            pass_on(i, k).start()
    for i in range(6):
        for k in range(2, 4):
            half_copy(i, k).wait_recv()
        for k in range(2):
            pass_on(i, k).wait_recv()
    for i in range(6):
        for k in range(4):
            half_copy(i, k).wait_send()
        for k in range(2):
            pass_on(i, k).wait_send()
    for line in lines:
        line.finish()
    for copy in over_seq + dealt:
        copy.wait_send()
    for copy in to_all:
        copy.wait()


def prologue(S, N, tok, cot, wq, wo, small, shards_in):
    D = wo.shape[1]
    own = wo.shape[0]
    chips = N // 2
    dma = pltpu.SemaphoreType.DMA
    line = [dma((2, chips - 1)), dma((2, chips - 1)), dma((chips,)), dma((chips,))]
    out = [
        jax.ShapeDtypeStruct(tok.shape, BF16),
        jax.ShapeDtypeStruct((N,) + cot.shape, BF16),
        jax.ShapeDtypeStruct((S, N) + wq.shape[1:], BF16),
        jax.ShapeDtypeStruct((N,) + wo.shape, BF16),
        jax.ShapeDtypeStruct((N, S) + small.shape, F32),
    ]
    for i, shard in enumerate(shards_in):
        rows, columns = shard.shape
        out.append(jax.ShapeDtypeStruct((4 * rows, columns) if i < 4 else (rows, 4 * columns), BF16))
    anywhere = pl.BlockSpec(memory_space=pl.ANY)
    return pl.pallas_call(
        functools.partial(prologue_kernel, S, N, (D // 8,)),
        out_shape=out,
        in_specs=[anywhere] * 11,
        out_specs=[anywhere] * 11,
        scratch_shapes=[pltpu.VMEM(u.shape, u.dtype) for u in (small, wq[0], wo, tok[0], cot[0], *shards_in)]
        + [
            dma((11,)), dma((2, N - 1)), dma((2, N - 1)), dma((2, 3)), dma((2, 3)), dma((N - 1,)), dma((N - 1,)),
            dma((6, 6)), dma((6, 6)),
        ] + line * 3,
        compiler_params=pltpu.CompilerParams(collective_id=0, has_side_effects=True, vmem_limit_bytes=VMEM_LIMIT),
        name="prologue",
    )(tok, cot, wq, wo, small, *shards_in)


def shards(
    tokens, cotangent, ids, deal, lengths, w_qkv, b_qkv, w_out, gain_attn, gain_ffn, w_router,
    w_shared_gate, e_gate, e_up, e_down, s_gate, s_up, s_down,
):
    S, N = lax.axis_size("seq"), lax.axis_size("fsdp")
    s, f = lax.axis_index("seq"), lax.axis_index("fsdp")
    MB, T, D = tokens.shape
    E = w_router.shape[1]
    assert S == 4 and e_gate.shape[0] == 1 and E == N
    FE, FS = e_gate.shape[2], s_gate.shape[1]
    piece = T // N
    pack = T * S
    heads = H // S
    width = heads * HD
    rows = N * MB * T
    own = w_out.shape[0]

    order = jnp.stack([jnp.bitwise_xor(s, rel) * 2 + half for rel, half in ORDER])
    inverse_order = jnp.argsort(order)

    def arrange(u, by):
        return jnp.take(u.reshape(u.shape[:-1] + (8, D // 8)), by, axis=u.ndim - 1).reshape(u.shape)

    inverse_deal = jnp.argsort(deal, axis=2)

    def deal_out(u):
        u = u.reshape(MB, piece, N, D)
        u = jnp.stack([jnp.take(u[m], inverse_deal[m, f], axis=1) for m in range(MB)])
        return u.transpose(2, 0, 1, 3).reshape(N, MB * piece, D)

    small = jnp.concatenate([gain_attn, gain_ffn, w_router.reshape(-1), w_shared_gate, b_qkv]).astype(F32)
    small = jnp.concatenate([small, ids.reshape(-1).astype(F32)])
    n_small = small.shape[0]
    small = jnp.pad(small, (0, -n_small % 1024)).reshape(-1, 128)
    wq = w_qkv.reshape(own, 3, S, width).transpose(2, 0, 1, 3).reshape(S, own, 3 * width)
    d_tok, g_all, w_in, w_back, small, *fulls = prologue(
        S, N, deal_out(tokens), deal_out(arrange(cotangent, order)), wq, w_out, small,
        (e_gate[0], e_up[0], s_gate, s_up, e_down[0], s_down),
    )
    small = small.reshape(N, S, -1)[:, :, :n_small]
    cuts = (own, 2 * own, 2 * own + own * E, 3 * own + own * E, 6 * own + own * E)
    small, all_ids = small[:, :, : cuts[4]].swapaxes(0, 1).reshape(S * N, cuts[4]), small[:, :, cuts[4] :]
    gain_1 = small[:, : cuts[0]].reshape(D)
    gain_2 = small[:, cuts[0] : cuts[1]].reshape(D)
    router_w = small[:, cuts[1] : cuts[2]].reshape(D, E).astype(BF16)
    shared_w = small[:, cuts[2] : cuts[3]].reshape(D).astype(BF16)
    bias = lax.dynamic_slice_in_dim(small[:, cuts[3] :].reshape(3, S, width), s, 1, 1).reshape(3 * width)
    w_in, w_back = w_in.reshape(D, 3 * width), w_back.reshape(width, D)
    eg, eu, sg, su, ed, sd = fulls
    x0 = d_tok.reshape(N, MB, piece, D).transpose(1, 2, 0, 3).reshape(MB, T, D).astype(F32)
    d_cot = lax.dynamic_index_in_dim(g_all, f, 0, keepdims=False)
    cot = arrange(d_cot.reshape(N, MB, piece, D).transpose(1, 2, 0, 3).reshape(MB, T, D), inverse_order)
    g_rows = g_all.reshape(rows, D)
    all_ids = lax.dynamic_index_in_dim(all_ids, s, 1, keepdims=False).reshape(N, MB, piece, N, TOP)
    where = inverse_deal.transpose(2, 1, 0)
    chosen = jnp.take_along_axis(
        all_ids[None], where[:, :, :, None, None, None], axis=4
    ).reshape(N, MB * T, TOP).astype(jnp.int32)
    own_ids = lax.dynamic_index_in_dim(chosen, f, 0, keepdims=False)
    own_ids = own_ids.reshape(N, MB, piece, TOP).transpose(1, 2, 0, 3).reshape(MB * T, TOP)
    chosen = chosen.reshape(rows, TOP)

    def to_rows(u):
        return u.reshape(MB, piece, N, -1).transpose(2, 0, 1, 3).reshape(MB * T, -1)

    def to_pack(u):
        return u.reshape(N, MB, piece, -1).transpose(1, 2, 0, 3).reshape(MB * T, -1)

    ends = jnp.cumsum(lengths[:, f], axis=1)
    spots = jnp.arange(pack, dtype=jnp.int32)
    past = ends[:, None, :] <= spots[None, :, None]
    segment = jnp.sum(past.astype(jnp.int32), axis=2)
    start = jnp.sum(jnp.where(past, lengths[:, f][:, None, :], 0), axis=2)
    frequency = THETA ** (-jnp.arange(0, HD, 2, dtype=F32) / HD)
    angle = (spots[None] - start).astype(F32)[..., None] * frequency
    angle = jnp.concatenate([angle, angle], axis=2)
    cosine, sine = jnp.cos(angle)[:, None, None], jnp.sin(angle)[:, None, None]
    allowed = (segment[:, :, None] == segment[:, None, :]) & (spots[None, None, :] <= spots[None, :, None])
    allowed = allowed[:, None]

    unit_1, inverse_1 = rms_forward(x0)
    normed = (unit_1 * gain_1).astype(BF16)
    normed_all = lax.all_gather(normed, "seq", axis=1, tiled=True)
    flat = normed_all.reshape(MB * pack, D)
    qkv = (dot(flat, w_in) + bias).reshape(MB, pack, 3, heads, HD).transpose(0, 2, 3, 1, 4)
    qk = qkv[:, :2]
    qk = (qk * cosine + turn(qk) * sine).astype(BF16)
    q, k, v = qk[:, 0], qk[:, 1], qkv[:, 2].astype(BF16)
    scale = HD ** -0.5
    raw = jnp.einsum("mhqd,mhkd->mhqk", q, k, preferred_element_type=F32)
    scores = jnp.where(allowed, raw * scale, MASKED)
    weights = jnp.exp(scores - jnp.max(scores, axis=-1, keepdims=True))
    chance = weights / jnp.sum(weights, axis=-1, keepdims=True)
    chance_low = chance.astype(BF16)
    context = jnp.einsum("mhqk,mhkd->mqhd", chance_low, v, preferred_element_type=F32).astype(BF16)
    context = context.reshape(MB * pack, width)
    partial = dot(context, w_back).astype(BF16).reshape(MB, S, T, D)
    partial = lax.all_to_all(partial, "seq", split_axis=1, concat_axis=1, tiled=True)
    hidden = x0 + jnp.sum(partial.astype(F32), axis=1)
    unit_2, inverse_2 = rms_forward(hidden)
    normed2 = (unit_2 * gain_2).astype(BF16)

    x = lax.all_gather(to_rows(arrange(normed2, order)), "fsdp", axis=0, tiled=True)
    lead = jnp.concatenate([router_w, shared_w[:, None]], axis=1)
    lead_order = jnp.take(lead.reshape(8, D // 8, E + 1), order, axis=0).reshape(D, E + 1)
    logits = dot(x, lead_order)
    shifted = jnp.exp(logits[:, :E] - jnp.max(logits[:, :E], axis=-1, keepdims=True))
    router_f = jnp.sum(jnp.where(jnp.arange(E) == f, shifted, 0.0), axis=1) / jnp.sum(shifted, axis=1)
    gate_f = jnp.where(jnp.any(chosen == f, axis=1), router_f, 0.0)[:, None]
    sigma_rows = jax.nn.sigmoid(logits[:, E])[:, None]
    g32 = g_rows.astype(F32)
    geo = (gate_f * g32).astype(BF16)
    gso = (sigma_rows * g32).astype(BF16)

    gate, up = dot(x, eg), dot(x, eu)
    act = (jax.nn.silu(gate) * up).astype(BF16)
    out_e = dot(act, ed).astype(BF16).astype(F32)
    sgate, sup = dot(x, sg), dot(x, su)
    sact = (jax.nn.silu(sgate) * sup).astype(BF16)
    out_s = dot(sact, sd)
    y = (gate_f * out_e + sigma_rows * out_s).astype(BF16)
    y = lax.psum_scatter(y, "fsdp", scatter_dimension=0, tiled=True)
    gg = jnp.sum(g32 * out_e, axis=1)
    gs = jnp.sum(g32 * out_s, axis=1)

    grad_gate, grad_up = swiglu_back(dot_nt(geo, ed), gate, up)
    grad_sgate, grad_sup = swiglu_back(dot_nt(gso, sd), sgate, sup)
    dx_e = (dot_nt(grad_gate, eg) + dot_nt(grad_up, eu)).astype(BF16).astype(F32)
    dx = dx_e + dot_nt(grad_sgate, sg) + dot_nt(grad_sup, su)
    mine = (jnp.arange(N) == f).astype(F32)
    notes = [part[:, None] * mine for value in (gg, gs) for part in split3(value)]
    note_pad = -(6 * N) % 128
    payload = jnp.concatenate([dx] + notes + [jnp.zeros((rows, note_pad), F32)], axis=1).astype(BF16)
    dx = lax.psum_scatter(payload, "fsdp", scatter_dimension=0, tiled=True).astype(F32)

    cat_grad = jnp.concatenate([grad_gate, grad_up, grad_sgate, grad_sup], axis=1)
    half = D // 8
    send_x = dot_t(x[:, 4 * half : 6 * half], cat_grad).astype(BF16)
    send_y = dot_t(x[:, 6 * half :], cat_grad).astype(BF16)
    from_x, from_y = across(send_x, 1), across(send_y, 2)

    def down_grad(lo, hi):
        return jnp.concatenate([dot_t(act, geo[:, lo:hi]), dot_t(sact, gso[:, lo:hi])], axis=0)

    bsend_x = down_grad(4 * half, 6 * half).astype(BF16)
    bsend_y = down_grad(6 * half, 8 * half).astype(BF16)
    bfrom_x, bfrom_y = across(bsend_x, 1), across(bsend_y, 2)
    keep = dot_t(x[:, : 4 * half], cat_grad)
    bkeep = down_grad(0, 4 * half)
    to_y = (keep[2 * half : 3 * half] + from_x[half:].astype(F32)).astype(BF16)
    to_x = (keep[3 * half :] + from_y[half:].astype(F32)).astype(BF16)
    last_y, last_x = across(to_y, 2), across(to_x, 1)
    bto_y = (bkeep[:, 2 * half : 3 * half] + bfrom_x[:, half:].astype(F32)).astype(BF16)
    bto_x = (bkeep[:, 3 * half :] + bfrom_y[:, half:].astype(F32)).astype(BF16)
    blast_y, blast_x = across(bto_y, 2), across(bto_x, 1)
    grad_a = jnp.concatenate(
        [
            keep[:half] + from_x[:half].astype(F32) + last_y.astype(F32),
            keep[half : 2 * half] + from_y[:half].astype(F32) + last_x.astype(F32),
        ],
        axis=0,
    )
    grad_b = jnp.concatenate(
        [
            bkeep[:, :half] + bfrom_x[:, :half].astype(F32) + blast_y.astype(F32),
            bkeep[:, half : 2 * half] + bfrom_y[:, :half].astype(F32) + blast_x.astype(F32),
        ],
        axis=1,
    )
    g_eg, g_eu, g_sg, g_su = jnp.split(grad_a, (FE, 2 * FE, 2 * FE + FS), axis=1)

    y = arrange(to_pack(y).astype(F32).reshape(MB, T, D), inverse_order)
    dx = to_pack(dx)
    mixed = (hidden + y).astype(BF16)
    base = D
    gg_own = sum(dx[:, base + i * N : base + (i + 1) * N] for i in range(3))
    gs_own = jnp.sum(dx[:, base + 3 * N : base + 6 * N], axis=1)
    grad_normed2 = arrange(dx[:, :D], inverse_order)
    flat2 = normed2.reshape(MB * T, D)
    logits = dot(flat2, lead)
    shifted = jnp.exp(logits[:, :E] - jnp.max(logits[:, :E], axis=-1, keepdims=True))
    router = shifted / jnp.sum(shifted, axis=-1, keepdims=True)
    sigma = jax.nn.sigmoid(logits[:, E])
    picked = jnp.any(own_ids[:, :, None] == jnp.arange(E)[None, None, :], axis=1)
    grad_router = jnp.where(picked, gg_own, 0.0)
    grad_logits = (router * (grad_router - jnp.sum(router * grad_router, axis=-1, keepdims=True))).astype(BF16)
    grad_sigma = gs_own * sigma * (1.0 - sigma)
    grad_normed2 = grad_normed2 + dot_nt(grad_logits, router_w) + grad_sigma[:, None] * shared_w.astype(F32)[None, :]
    g_router = dot_t(flat2, grad_logits)
    g_shared = jnp.sum(grad_sigma[:, None] * flat2.astype(F32), axis=0)
    from_norm, g_gain_2 = rms_backward(grad_normed2.reshape(MB, T, D), unit_2, inverse_2, gain_2)
    grad_hidden = cot.astype(F32) + from_norm

    grad_attn = lax.all_gather(grad_hidden.astype(BF16), "seq", axis=1, tiled=True).reshape(MB * pack, D)
    g_out = dot_t(context, grad_attn)
    gc = dot_nt(grad_attn, w_back).astype(BF16).reshape(MB, pack, heads, HD).transpose(0, 2, 1, 3)
    grad_chance = jnp.einsum("mhqd,mhkd->mhqk", gc, v, preferred_element_type=F32)
    delta = jnp.sum(chance * grad_chance, axis=-1, keepdims=True)
    grad_raw = (chance * (grad_chance - delta) * scale).astype(BF16)
    gq = jnp.einsum("mhqk,mhkd->mhqd", grad_raw, k, preferred_element_type=F32)
    gk = jnp.einsum("mhqk,mhqd->mhkd", grad_raw, q, preferred_element_type=F32)
    gv = jnp.einsum("mhqk,mhqd->mhkd", chance_low, gc, preferred_element_type=F32)
    gqk = jnp.stack([gq, gk], axis=1).astype(BF16).astype(F32)
    gqk = (gqk * cosine + turn_back(gqk * sine)).astype(BF16)
    grad_qkv = jnp.concatenate([gqk, gv.astype(BF16)[:, None]], axis=1).transpose(0, 3, 1, 2, 4)
    grad_qkv = grad_qkv.reshape(MB * pack, 3 * width)
    g_bias = jnp.sum(grad_qkv.astype(F32), axis=0)
    g_in = dot_t(flat, grad_qkv)
    partial = dot_nt(grad_qkv, w_in).astype(BF16).reshape(MB, S, T, D)
    partial = lax.all_to_all(partial, "seq", split_axis=1, concat_axis=1, tiled=True)
    grad_normed = jnp.sum(partial.astype(F32), axis=1)
    from_first, g_gain_1 = rms_backward(grad_normed, unit_1, inverse_1, gain_1)
    grad_x = (grad_hidden + from_first).astype(BF16)

    back = jnp.concatenate([mixed, grad_x], axis=2).reshape(MB, piece, N, 2 * D)
    back = lax.all_to_all(back, "fsdp", split_axis=2, concat_axis=2, tiled=True)
    back = jnp.stack([jnp.take(back[m], deal[m, f], axis=1) for m in range(MB)]).reshape(MB, T, 2 * D)
    mixed, grad_tokens = back[..., :D], back[..., D:].astype(F32)

    g_in = lax.psum_scatter(g_in.astype(BF16).reshape(S, N * own, 3 * width), "fsdp", scatter_dimension=1, tiled=True)
    g_in = lax.all_to_all(g_in, "seq", split_axis=0, concat_axis=0, tiled=True)
    g_in = g_in.reshape(S, own, 3, width).transpose(1, 2, 0, 3).reshape(own, 3 * D).astype(F32)
    g_out = lax.psum_scatter(g_out.astype(BF16), "fsdp", scatter_dimension=0, tiled=True).astype(F32)
    g_bias = jnp.where(jnp.arange(S)[None, :, None] == s, g_bias.reshape(3, 1, width), 0.0)
    count = S * N
    small = jnp.concatenate(
        [
            g_gain_1.reshape(count, own), g_gain_2.reshape(count, own), g_router.reshape(count, own * E),
            g_shared.reshape(count, own), g_bias.reshape(count, 3 * own),
        ],
        axis=1,
    )
    small = lax.psum_scatter(small, ("seq", "fsdp"), scatter_dimension=0, tiled=True)[0]
    return (
        mixed, grad_tokens, g_in, small[cuts[3] :], g_out, small[: cuts[0]], small[cuts[0] : cuts[1]],
        small[cuts[1] : cuts[2]].reshape(own, E), small[cuts[2] : cuts[3]],
        g_eg[None], g_eu[None], grad_b[:FE][None], g_sg, g_su, grad_b[FE:],
    )


def solution(mesh):
    both = ("seq", "fsdp")
    in_specs = (
        P(None, both, None), P(None, both, None), P(None, both, None), P(), P(), P(both, None), P(both), P(both, None),
        P(both), P(both), P(both, None), P(both), P("fsdp", "seq", None), P("fsdp", "seq", None),
        P("fsdp", None, "seq"), P("seq", "fsdp"), P("seq", "fsdp"), P("fsdp", "seq"),
    )
    out_specs = (
        P(None, both, None), P(None, both, None), P(both, None), P(both), P(both, None), P(both), P(both),
        P(both, None), P(both), P("fsdp", "seq", None), P("fsdp", "seq", None), P("fsdp", None, "seq"),
        P("seq", "fsdp"), P("seq", "fsdp"), P("fsdp", "seq"),
    )
    return jax.shard_map(shards, mesh=mesh, in_specs=in_specs, out_specs=out_specs, check_vma=False)
```

```python
import functools

import jax
import jax.numpy as jnp
from jax import lax
from jax.experimental import pallas as pl
from jax.experimental.pallas import tpu as pltpu
from jax.sharding import PartitionSpec as P

H = 16
HD = 128
TOP = 4
EPS = 1e-06
THETA = 1000000.0
MASKED = -1e30
F32 = jnp.float32
BF16 = jnp.bfloat16
MESH = pl.DeviceIdType.MESH
VMEM_LIMIT = 56 * 2**20

ORDER = ((0, 0), (0, 1), (2, 0), (1, 1), (1, 0), (3, 0), (2, 1), (3, 1))


def dot(a, b):
    return jnp.dot(a, b, preferred_element_type=F32)


def dot_t(a, b):
    return lax.dot_general(a, b, (((0,), (0,)), ((), ())), preferred_element_type=F32)


def dot_nt(a, b):
    return lax.dot_general(a, b, (((1,), (1,)), ((), ())), preferred_element_type=F32)


def turn(u):
    half = u.shape[-1] // 2
    return jnp.concatenate([-u[..., half:], u[..., :half]], axis=-1)


def turn_back(u):
    half = u.shape[-1] // 2
    return jnp.concatenate([u[..., half:], -u[..., :half]], axis=-1)


def rms_forward(values):
    inverse = lax.rsqrt(jnp.mean(values * values, axis=-1, keepdims=True) + EPS)
    return values * inverse, inverse


def rms_backward(grad, unit, inverse, gain):
    scaled = grad * gain
    grad_gain = jnp.sum(grad * unit, axis=tuple(range(grad.ndim - 1)))
    return inverse * (scaled - unit * jnp.mean(scaled * unit, axis=-1, keepdims=True)), grad_gain


def across(a, which):
    return lax.ppermute(a, "seq", [(i, i ^ which) for i in range(4)])


def split3(v):
    hi = lax.reduce_precision(v, 8, 7)
    mid = lax.reduce_precision(v - hi, 8, 7)
    low = lax.reduce_precision(v - hi - mid, 8, 7)
    return hi, mid, low


def swiglu_back(grad_act, gate, up):
    sig = jax.nn.sigmoid(gate)
    grad_gate = (grad_act * up * sig * (1.0 + gate * (1.0 - sig))).astype(BF16)
    grad_up = (grad_act * gate * sig).astype(BF16)
    return grad_gate, grad_up


def partners(s):
    return s + 1 - 2 * lax.rem(s, 2), lax.rem(s + 2, 4), 3 - s


def greet(s, f, S, N):
    barrier = pltpu.get_barrier_semaphore()
    for other in partners(s):
        pl.semaphore_signal(barrier, inc=1, device_id=(other, f), device_id_type=MESH)
    for step in range(1, N):
        pl.semaphore_signal(barrier, inc=1, device_id=(s, lax.rem(f + step, N)), device_id_type=MESH)
    pl.semaphore_wait(barrier, S - 1 + N - 1)


class Line:
    def __init__(self, s, f, N, block, move_send, move_recv, side_send, side_recv):
        self.s, self.chip, self.core, self.n = s, f // 2, lax.rem(f, 2), N // 2
        self.block = block
        self.move_send, self.move_recv = move_send, move_recv
        self.side_send, self.side_recv = side_send, side_recv

    def move(self, way, step, origin, to):
        ref = self.block(2 * origin + self.core)
        return pltpu.make_async_remote_copy(
            ref, ref, self.move_send.at[way, step], self.move_recv.at[way, step],
            device_id=(self.s, 2 * to + self.core), device_id_type=MESH,
        )

    def side(self, origin, core):
        ref = self.block(2 * origin + core)
        return pltpu.make_async_remote_copy(
            ref, ref, self.side_send.at[origin], self.side_recv.at[origin],
            device_id=(self.s, 2 * self.chip + 1 - self.core), device_id_type=MESH,
        )

    def send(self, step, act):
        q, n = self.chip, self.n

        @pl.when((q - step >= 0) & (q + 1 < n))
        def _():
            act(self.move(0, step, jnp.maximum(q - step, 0), jnp.minimum(q + 1, n - 1)))

        @pl.when((q + step < n) & (q >= 1))
        def _():
            act(self.move(1, step, jnp.minimum(q + step, n - 1), jnp.maximum(q - 1, 0)))

    def begin(self):
        self.send(0, lambda copy: copy.start())
        self.side(self.chip, self.core).start()

    def step(self, step):
        q, n = self.chip, self.n

        @pl.when(q - 1 - step >= 0)
        def _():
            origin = jnp.maximum(q - 1 - step, 0)
            self.move(0, step, origin, jnp.maximum(q - 1, 0)).wait_recv()
            if step + 1 < n - 1:

                @pl.when(q + 1 < n)
                def _():
                    self.move(0, step + 1, origin, jnp.minimum(q + 1, n - 1)).start()

            self.side(origin, self.core).start()

        @pl.when(q + 1 + step < n)
        def _():
            origin = jnp.minimum(q + 1 + step, n - 1)
            self.move(1, step, origin, jnp.minimum(q + 1, n - 1)).wait_recv()
            if step + 1 < n - 1:

                @pl.when(q >= 1)
                def _():
                    self.move(1, step + 1, origin, jnp.maximum(q - 1, 0)).start()

            self.side(origin, self.core).start()

    def arrive(self):
        for origin in range(self.n):
            self.side(origin, 1 - self.core).wait_recv()

    def drain(self):
        for step in range(self.n - 1):
            self.send(step, lambda copy: copy.wait_send())
        for origin in range(self.n):
            self.side(origin, self.core).wait_send()


PLACE = {key: i for i, key in enumerate(ORDER)}


def gather_vector(small, row, length, own, N):
    per = 128 // own
    for block in range(length // 128):
        total = None
        for i in range(block * per, (block + 1) * per):
            part = small[i % N, i // N, row : row + 1, :]
            total = part if total is None else total + part
        yield block, total


def forward_kernel(S, N, sizes, *refs):
    MB, piece, D, own, heads = sizes
    tok, cot, wq, wo, small, *refs = refs
    shards_in, refs = refs[:6], refs[6:]
    cos, sin, first, place, place_row, *refs = refs
    x_rows, g_all, w_in, w_back, small_all, normed_out, qkv_out, ctx_out, hid_out, x_all, *refs = refs
    fulls, refs = refs[:6], refs[6:]
    cot_by, shard_by, refs = refs[0], refs[1:7], refs[7:]
    small_v, tok_v, w_v, wb_v, x_v, gain_v, bias_v, na_v, qkv_v, ctx_v, part_send, part_recv, hid_v, n2_v, xo_v, *refs = refs
    (local_sem, deal_send, deal_recv, seq_send, seq_recv, small_send, small_recv, half_send, half_recv, part_sems,
     part_semr, norm_sems, norm_semr, out_sem, *line_sems) = refs
    s, f = lax.axis_index("seq"), lax.axis_index("fsdp")
    px, py, pd = partners(s)
    eighth = D // 8
    pr = MB * piece
    L = pr * N
    R = S * L
    width = heads * HD

    def spot(full, i, where):
        cut = pl.ds(where * eighth, eighth)
        return full.at[cut] if i < 4 else full.at[:, cut]

    def own_half(shard, i, half):
        cut = pl.ds(half * eighth, eighth)
        return shard.at[cut] if i < 4 else shard.at[:, cut]

    def remote(src, dst, send, recv, device):
        return pltpu.make_async_remote_copy(src, dst, send, recv, device_id=device, device_id_type=MESH)

    pairs = [
        (small, small_v.at[f, s]), (wq.at[s], w_v.at[s, f]), (wo, wb_v.at[f]), (tok.at[f], tok_v.at[f]), (cot.at[f], cot_by),
    ] + list(zip(shards_in, shard_by))
    take = [pltpu.make_async_copy(a, b, local_sem.at[i]) for i, (a, b) in enumerate(pairs)]
    put = [pltpu.make_async_copy(cot_by, g_all.at[f, f], local_sem.at[4])]
    for i in range(6):
        cut = pl.ds(0, 2 * eighth)
        target = fulls[i].at[cut] if i < 4 else fulls[i].at[:, cut]
        put.append(pltpu.make_async_copy(shard_by[i], target, local_sem.at[5 + i]))
    for copy in take:
        copy.start()
    greet(s, f, S, N)

    over_seq = []
    for k, other in enumerate((px, py, pd)):
        over_seq.append(remote(small, small_v.at[f, s], seq_send.at[0, k], seq_recv.at[0, k], (other, f)))
        over_seq.append(remote(wq.at[other], w_v.at[s, f], seq_send.at[1, k], seq_recv.at[1, k], (other, f)))
    for copy in over_seq:
        copy.start()
    deal_tok, deal_cot, to_all = [], [], []
    for k in range(1, N):
        to = lax.rem(f + k, N)
        deal_tok.append(remote(tok.at[to], tok_v.at[f], deal_send.at[0, k - 1], deal_recv.at[0, k - 1], (s, to)))
        deal_cot.append(remote(cot.at[to], g_all.at[to, f], deal_send.at[1, k - 1], deal_recv.at[1, k - 1], (s, to)))
        to_all.append(remote(small_v.at[f], small_v.at[f], small_send.at[k - 1], small_recv.at[k - 1], (s, to)))
    for copy in deal_tok:
        copy.start()

    def half_copy(i, k):
        where, rel, half = ((px, 1, 0), (py, 2, 1), (py, 2, 0), (px, 1, 1))[k]
        return remote(
            own_half(shards_in[i], i, half), spot(fulls[i], i, PLACE[rel, half]), half_send.at[i, k], half_recv.at[i, k],
            (where, f),
        )

    def pass_copy(i, k):
        where, rel, half = ((py, 1, 0), (px, 2, 1))[k]
        return remote(
            spot(fulls[i], i, PLACE[rel, half]), spot(fulls[i], i, PLACE[3, half]), half_send.at[i, 4 + k],
            half_recv.at[i, 4 + k], (where, f),
        )

    def give(i):
        for k in range(4):
            half_copy(i, k).start()

    def pass_on(i):
        for k in range(2):
            half_copy(i, k).wait_recv()
            pass_copy(i, k).start()

    give(0)
    for copy in take:
        copy.wait()
    for copy in put:
        copy.start()
    for copy in over_seq:
        copy.wait_recv()
    for copy in to_all:
        copy.start()
    w_line = Line(s, f, N, lambda j: w_v.at[:, j], *line_sems[0:4])
    b_line = Line(s, f, N, lambda j: wb_v.at[j], *line_sems[4:8])
    g_line = Line(s, f, N, lambda j: g_all.at[j], *line_sems[8:12])
    x_line = Line(s, f, N, lambda j: x_all.at[j], *line_sems[12:16])
    w_line.begin()
    b_line.begin()

    for copy in deal_tok + to_all:
        copy.wait_recv()
    for row in range(2):
        for block, part in gather_vector(small_v, row, D, own, N):
            gain_v[row : row + 1, block * 128 : (block + 1) * 128] = part
    nb = 3 * own
    for line in range(3 * D // 128):
        total = None
        for i in range(S * N):
            for half in range(2):
                if (i * nb) // 128 + half == line and (half == 0 or (i * nb) % 128 + nb > 128):
                    part = small_v[i % N, i // N, 2 + half : 3 + half, :]
                    total = part if total is None else total + part
        bias_v[line : line + 1, :] = total
    for j in range(N):
        x_v[j * pr : (j + 1) * pr, :] = tok_v[j].astype(F32)
    x = x_v[...]
    inverse = lax.rsqrt(jnp.mean(x * x, axis=-1, keepdims=True) + EPS)
    na_v[s] = (x * inverse * gain_v[0:1, :]).astype(BF16)
    spread = [
        remote(na_v.at[s], na_v.at[s], norm_sems.at[k], norm_semr.at[k], (other, f)) for k, other in enumerate((px, py, pd))
    ]
    for copy in spread:
        copy.start()
    for copy in deal_cot:
        copy.start()
    give(1)
    chips = N // 2
    for step in range(chips - 1):
        w_line.step(step)
        b_line.step(step)
        if step == 0:
            give(4)
        if step == 1:
            pass_on(0)
    pass_on(1)
    give(2)
    for copy in deal_cot:
        copy.wait_recv()
    for copy in put:
        copy.wait()
    g_line.begin()
    w_line.arrive()
    b_line.arrive()
    for copy in spread:
        copy.wait_recv()

    for t in range(3):

        def project(pair, carry, t=t):
            column = pl.multiple_of(t * width + pair * 2 * HD, 2 * HD)
            w = w_v[:, :, :, pl.ds(column, 2 * HD)].reshape(D, 2 * HD)
            out = dot(na_v[...].reshape(R, D), w)
            for k in range(2):
                u = out[:, k * HD : (k + 1) * HD]
                u = u + bias_v[pl.ds(t * (D // 128) + s * heads + 2 * pair + k, 1), :]
                if t < 2:
                    u = u * cos[...] + pltpu.roll(u, HD // 2, 1) * sin[...]
                qkv_v[t * heads + 2 * pair + k] = u.astype(BF16)
            return carry

        lax.fori_loop(0, heads // 2, project, 0)
    g_line.step(0)

    def attend(h, carry):
        rows = R // 4
        for block in range(4):
            cut = pl.ds(block * rows, rows)
            raw = dot_nt(qkv_v[h, cut, :], qkv_v[heads + h])
            ok = (first[cut, :] <= place_row[...]) & (place_row[...] <= place[cut, :])
            scores = jnp.where(ok, raw * HD**-0.5, MASKED)
            weights = jnp.exp(scores - jnp.max(scores, axis=-1, keepdims=True))
            chance = (weights / jnp.sum(weights, axis=-1, keepdims=True)).astype(BF16)
            ctx_v[cut, pl.ds(pl.multiple_of(h * HD, HD), HD)] = dot(chance, qkv_v[2 * heads + h]).astype(BF16)
        return carry

    lax.fori_loop(0, heads, attend, 0)
    for step in range(1, chips - 1):
        g_line.step(step)
        if step == 1:
            give(3)
            give(5)

    wb = wb_v[...].reshape(width, D)
    exchange = []
    for k, other in enumerate((px, py, pd)):
        rows = pl.ds(pl.multiple_of(other * L, L), L)
        part_send[k] = dot(ctx_v[rows, :], wb).astype(BF16)
        exchange.append(remote(part_send.at[k], part_recv.at[k], part_sems.at[k], part_semr.at[k], (other, f)))
        exchange[-1].start()
    pass_on(4)
    hid_v[...] = x_v[...] + dot(ctx_v[pl.ds(pl.multiple_of(s * L, L), L), :], wb)
    outs = [
        (tok_v, x_rows), (w_v, w_in), (wb_v, w_back), (small_v, small_all), (na_v, normed_out), (qkv_v, qkv_out),
        (ctx_v, ctx_out), (hid_v, hid_out), (xo_v, x_all.at[f]),
    ]
    outs = [pltpu.make_async_copy(a, b, out_sem.at[i]) for i, (a, b) in enumerate(outs)]
    for k in range(3):
        exchange[k].wait_recv()
        hid_v[...] += part_recv[k].astype(F32)
    hidden = hid_v[...]
    inverse = lax.rsqrt(jnp.mean(hidden * hidden, axis=-1, keepdims=True) + EPS)
    n2_v[...] = (hidden * inverse * gain_v[1:2, :]).astype(BF16)
    owners = (s, px, py, pd)
    for i, (rel, half) in enumerate(ORDER):
        column = pl.multiple_of((owners[rel] * 2 + half) * eighth, eighth)
        xo_v[:, i * eighth : (i + 1) * eighth] = n2_v[:, pl.ds(column, eighth)]
    outs[8].start()
    outs[8].wait()
    x_line.begin()
    pass_on(2)
    for step in range(chips - 1):
        x_line.step(step)
    pass_on(3)
    pass_on(5)
    for line in (w_line, b_line):
        line.drain()
    for copy in over_seq + to_all + spread:
        copy.wait_send()
    for copy in outs[:8]:
        copy.start()
    for i in range(6):
        for k in range(2, 4):
            half_copy(i, k).wait_recv()
        for k in range(2):
            pass_copy(i, k).wait_recv()
    for i in range(6):
        for k in range(4):
            half_copy(i, k).wait_send()
        for k in range(2):
            pass_copy(i, k).wait_send()
    for line in (g_line, x_line):
        line.arrive()
        line.drain()
    for copy in deal_tok + deal_cot + exchange:
        copy.wait_send()
    for copy in outs[:8]:
        copy.wait()


def forward(S, N, MB, tok, cot, wq, wo, small, shards_in, tables):
    own, D = wo.shape
    pr = tok.shape[1]
    L = pr * N
    R = S * L
    heads = H // S
    width = heads * HD
    chips = N // 2
    dma = pltpu.SemaphoreType.DMA
    line = [dma((2, chips - 1)), dma((2, chips - 1)), dma((chips,)), dma((chips,))]
    shape = jax.ShapeDtypeStruct
    w_shape, wb_shape, small_shape = (S, N) + wq.shape[1:], (N,) + wo.shape, (N, S) + small.shape
    out = [
        shape(tok.shape, BF16), shape((N,) + cot.shape, BF16), shape(w_shape, BF16), shape(wb_shape, BF16),
        shape(small_shape, F32), shape((S, L, D), BF16), shape((3 * heads, R, HD), BF16), shape((R, width), BF16),
        shape((L, D), F32), shape((N, L, D), BF16),
    ]
    for i, shard in enumerate(shards_in):
        rows, columns = shard.shape
        out.append(shape((4 * rows, columns) if i < 4 else (rows, 4 * columns), BF16))
    anywhere = pl.BlockSpec(memory_space=pl.ANY)
    in_vmem = pl.BlockSpec(memory_space=pltpu.VMEM)
    vmem = pltpu.VMEM
    return pl.pallas_call(
        functools.partial(forward_kernel, S, N, (MB, pr // MB, D, own, heads)),
        out_shape=out,
        in_specs=[anywhere] * 11 + [in_vmem] * 5,
        out_specs=[anywhere] * 16,
        scratch_shapes=[vmem(u.shape, u.dtype) for u in (cot[0], *shards_in)]
        + [
            vmem(small_shape, F32), vmem(tok.shape, BF16), vmem(w_shape, BF16), vmem(wb_shape, BF16), vmem((L, D), F32),
            vmem((8, D), F32), vmem((3 * D // 128, 128), F32), vmem((S, L, D), BF16), vmem((3 * heads, R, HD), BF16),
            vmem((R, width), BF16), vmem((3, L, D), BF16), vmem((3, L, D), BF16), vmem((L, D), F32), vmem((L, D), BF16),
            vmem((L, D), BF16),
            dma((11,)), dma((2, N - 1)), dma((2, N - 1)), dma((2, 3)), dma((2, 3)), dma((N - 1,)), dma((N - 1,)),
            dma((6, 6)), dma((6, 6)), dma((3,)), dma((3,)), dma((3,)), dma((3,)), dma((9,)),
        ] + line * 4,
        compiler_params=pltpu.CompilerParams(collective_id=0, has_side_effects=True, vmem_limit_bytes=VMEM_LIMIT),
        name="forward",
    )(tok, cot, wq, wo, small, *shards_in, *tables)


def shards(
    tokens, cotangent, ids, deal, lengths, w_qkv, b_qkv, w_out, gain_attn, gain_ffn, w_router,
    w_shared_gate, e_gate, e_up, e_down, s_gate, s_up, s_down,
):
    S, N = lax.axis_size("seq"), lax.axis_size("fsdp")
    s, f = lax.axis_index("seq"), lax.axis_index("fsdp")
    MB, T, D = tokens.shape
    E = w_router.shape[1]
    assert S == 4 and e_gate.shape[0] == 1 and E == N
    FE, FS = e_gate.shape[2], s_gate.shape[1]
    piece = T // N
    pack = T * S
    heads = H // S
    width = heads * HD
    rows = N * MB * T
    own = w_out.shape[0]

    order = jnp.stack([jnp.bitwise_xor(s, rel) * 2 + half for rel, half in ORDER])
    inverse_order = jnp.argsort(order)

    def arrange(u, by):
        return jnp.take(u.reshape(u.shape[:-1] + (8, D // 8)), by, axis=u.ndim - 1).reshape(u.shape)

    inverse_deal = jnp.argsort(deal, axis=2)

    def deal_out(u):
        u = u.reshape(MB, piece, N, D)
        u = jnp.stack([jnp.take(u[m], inverse_deal[m, f], axis=1) for m in range(MB)])
        return u.transpose(2, 0, 1, 3).reshape(N, MB * piece, D)

    index = s * N + f

    def placed(u, length):
        return lax.dynamic_update_slice(jnp.zeros((length,), F32), u.astype(F32), ((index * u.shape[0]) % 128,))

    parts = [placed(gain_attn, 128), placed(gain_ffn, 128), placed(b_qkv, 256), placed(w_shared_gate, 128)]
    for u in (w_router.reshape(-1), ids.reshape(-1)):
        parts.append(jnp.pad(u.astype(F32), (0, -u.shape[0] % 128)))
    r_line = 5
    i_line = r_line + parts[4].shape[0] // 128
    small = jnp.concatenate(parts)
    small = jnp.pad(small, (0, -small.shape[0] % 1024)).reshape(-1, 128)

    spots = ((jnp.arange(S)[:, None, None] * piece + jnp.arange(piece)[None, None, :]) * N + jnp.arange(N)[None, :, None])
    spots = jnp.broadcast_to(spots[:, :, None, :], (S, N, MB, piece)).astype(jnp.int32)
    micro = jnp.arange(MB, dtype=jnp.int32)[None, None, :, None]
    my_lengths = lengths[:, f]
    ends = jnp.cumsum(my_lengths, axis=1)
    past = ends[None, None, :, None, :] <= spots[..., None]
    start = jnp.sum(jnp.where(past, my_lengths[None, None, :, None, :], 0), axis=4)
    frequency = THETA ** (-jnp.arange(0, HD, 2, dtype=F32) / HD)
    angle = (spots - start).astype(F32).reshape(-1, 1) * frequency
    cosine, sine = jnp.cos(angle), jnp.sin(angle)
    cosine = jnp.concatenate([cosine, cosine], axis=1)
    sine = jnp.concatenate([-sine, sine], axis=1)
    place = (spots + pack * micro).reshape(-1)
    first = (start + pack * micro).reshape(-1)
    tables = (cosine, sine, first[:, None], place[:, None], place[None, :])

    wq = w_qkv.reshape(own, 3, S, width).transpose(2, 0, 1, 3).reshape(S, own, 3 * width)
    x_rows, g_all, w_in, w_back, small, normed_all, qkv, context, hidden, x_all, *fulls = forward(
        S, N, MB, deal_out(tokens), deal_out(arrange(cotangent, order)), wq, w_out, small,
        (e_gate[0], e_up[0], s_gate, s_up, e_down[0], s_down), tables,
    )
    L, R = MB * T, MB * pack

    def vector(row):
        return small[:, :, row].swapaxes(0, 1).reshape(D // 128, 128 // own, 128).sum(1).reshape(D)

    gain_1, gain_2, shared_w = vector(0), vector(1), vector(4).astype(BF16)
    router_w = small[:, :, r_line:i_line].swapaxes(0, 1).reshape(S * N, -1)[:, : own * E].reshape(D, E).astype(BF16)
    all_ids = small[:, :, i_line:].reshape(N, S, -1)[:, :, : MB * T * TOP]
    w_in, w_back = w_in.reshape(D, 3 * width), w_back.reshape(width, D)
    eg, eu, sg, su, ed, sd = fulls
    x0 = x_rows.reshape(L, D).astype(F32)
    cot = arrange(lax.dynamic_index_in_dim(g_all, f, 0, keepdims=False).reshape(L, D), inverse_order)
    g_rows = g_all.reshape(rows, D)
    all_ids = lax.dynamic_index_in_dim(all_ids, s, 1, keepdims=False).reshape(N, MB, piece, N, TOP)
    where = inverse_deal.transpose(2, 1, 0)
    chosen = jnp.take_along_axis(
        all_ids[None], where[:, :, :, None, None, None], axis=4
    ).reshape(N, L, TOP).astype(jnp.int32)
    own_ids = lax.dynamic_index_in_dim(chosen, f, 0, keepdims=False)
    chosen = chosen.reshape(rows, TOP)
    x = x_all.reshape(rows, D)
    x_own = lax.dynamic_index_in_dim(x_all, f, 0, keepdims=False)
    unit_1, inverse_1 = rms_forward(x0)
    unit_2, inverse_2 = rms_forward(hidden)

    lead = jnp.concatenate([router_w, shared_w[:, None]], axis=1)
    lead_order = jnp.take(lead.reshape(8, D // 8, E + 1), order, axis=0).reshape(D, E + 1)
    logits = dot(x, lead_order)
    shifted = jnp.exp(logits[:, :E] - jnp.max(logits[:, :E], axis=-1, keepdims=True))
    router_f = jnp.sum(jnp.where(jnp.arange(E) == f, shifted, 0.0), axis=1) / jnp.sum(shifted, axis=1)
    gate_f = jnp.where(jnp.any(chosen == f, axis=1), router_f, 0.0)[:, None]
    sigma_rows = jax.nn.sigmoid(logits[:, E])[:, None]
    g32 = g_rows.astype(F32)
    geo = (gate_f * g32).astype(BF16)
    gso = (sigma_rows * g32).astype(BF16)

    gate, up = dot(x, eg), dot(x, eu)
    act = (jax.nn.silu(gate) * up).astype(BF16)
    out_e = dot(act, ed).astype(BF16).astype(F32)
    sgate, sup = dot(x, sg), dot(x, su)
    sact = (jax.nn.silu(sgate) * sup).astype(BF16)
    out_s = dot(sact, sd)
    y = (gate_f * out_e + sigma_rows * out_s).astype(BF16)
    y = lax.psum_scatter(y, "fsdp", scatter_dimension=0, tiled=True)
    gg = jnp.sum(g32 * out_e, axis=1)
    gs = jnp.sum(g32 * out_s, axis=1)

    grad_gate, grad_up = swiglu_back(dot_nt(geo, ed), gate, up)
    grad_sgate, grad_sup = swiglu_back(dot_nt(gso, sd), sgate, sup)
    dx_e = (dot_nt(grad_gate, eg) + dot_nt(grad_up, eu)).astype(BF16).astype(F32)
    dx = dx_e + dot_nt(grad_sgate, sg) + dot_nt(grad_sup, su)
    mine = (jnp.arange(N) == f).astype(F32)
    notes = [part[:, None] * mine for value in (gg, gs) for part in split3(value)]
    note_pad = -(6 * N) % 128
    payload = jnp.concatenate([dx] + notes + [jnp.zeros((rows, note_pad), F32)], axis=1).astype(BF16)
    dx = lax.psum_scatter(payload, "fsdp", scatter_dimension=0, tiled=True).astype(F32)

    cat_grad = jnp.concatenate([grad_gate, grad_up, grad_sgate, grad_sup], axis=1)
    half = D // 8
    send_x = dot_t(x[:, 4 * half : 6 * half], cat_grad).astype(BF16)
    send_y = dot_t(x[:, 6 * half :], cat_grad).astype(BF16)
    from_x, from_y = across(send_x, 1), across(send_y, 2)

    def down_grad(lo, hi):
        return jnp.concatenate([dot_t(act, geo[:, lo:hi]), dot_t(sact, gso[:, lo:hi])], axis=0)

    bsend_x = down_grad(4 * half, 6 * half).astype(BF16)
    bsend_y = down_grad(6 * half, 8 * half).astype(BF16)
    bfrom_x, bfrom_y = across(bsend_x, 1), across(bsend_y, 2)
    keep = dot_t(x[:, : 4 * half], cat_grad)
    bkeep = down_grad(0, 4 * half)
    to_y = (keep[2 * half : 3 * half] + from_x[half:].astype(F32)).astype(BF16)
    to_x = (keep[3 * half :] + from_y[half:].astype(F32)).astype(BF16)
    last_y, last_x = across(to_y, 2), across(to_x, 1)
    bto_y = (bkeep[:, 2 * half : 3 * half] + bfrom_x[:, half:].astype(F32)).astype(BF16)
    bto_x = (bkeep[:, 3 * half :] + bfrom_y[:, half:].astype(F32)).astype(BF16)
    blast_y, blast_x = across(bto_y, 2), across(bto_x, 1)
    grad_a = jnp.concatenate(
        [
            keep[:half] + from_x[:half].astype(F32) + last_y.astype(F32),
            keep[half : 2 * half] + from_y[:half].astype(F32) + last_x.astype(F32),
        ],
        axis=0,
    )
    grad_b = jnp.concatenate(
        [
            bkeep[:, :half] + bfrom_x[:, :half].astype(F32) + blast_y.astype(F32),
            bkeep[:, half : 2 * half] + bfrom_y[:, :half].astype(F32) + blast_x.astype(F32),
        ],
        axis=1,
    )
    g_eg, g_eu, g_sg, g_su = jnp.split(grad_a, (FE, 2 * FE, 2 * FE + FS), axis=1)

    mixed = (hidden + arrange(y, inverse_order).astype(F32)).astype(BF16)
    base = D
    gg_own = sum(dx[:, base + i * N : base + (i + 1) * N] for i in range(3))
    gs_own = jnp.sum(dx[:, base + 3 * N : base + 6 * N], axis=1)
    grad_normed2 = arrange(dx[:, :D], inverse_order)
    flat2 = arrange(x_own, inverse_order)
    logits = dot(x_own, lead_order)
    shifted = jnp.exp(logits[:, :E] - jnp.max(logits[:, :E], axis=-1, keepdims=True))
    router = shifted / jnp.sum(shifted, axis=-1, keepdims=True)
    sigma = jax.nn.sigmoid(logits[:, E])
    picked = jnp.any(own_ids[:, :, None] == jnp.arange(E)[None, None, :], axis=1)
    grad_router = jnp.where(picked, gg_own, 0.0)
    grad_logits = (router * (grad_router - jnp.sum(router * grad_router, axis=-1, keepdims=True))).astype(BF16)
    grad_sigma = gs_own * sigma * (1.0 - sigma)
    grad_normed2 = grad_normed2 + dot_nt(grad_logits, router_w) + grad_sigma[:, None] * shared_w.astype(F32)[None, :]
    g_router = dot_t(flat2, grad_logits)
    g_shared = jnp.sum(grad_sigma[:, None] * flat2.astype(F32), axis=0)
    from_norm, g_gain_2 = rms_backward(grad_normed2, unit_2, inverse_2, gain_2)
    grad_hidden = cot.astype(F32) + from_norm

    grad_attn = lax.all_gather(grad_hidden.astype(BF16), "seq", axis=0, tiled=True)
    g_out = dot_t(context, grad_attn)
    gc = dot_nt(grad_attn, w_back).astype(BF16)

    def by_micro(u):
        u = u.reshape(u.shape[0], S * N, MB, piece, HD).transpose(2, 0, 1, 3, 4)
        return u.reshape(MB, u.shape[1], pack, HD)

    qkv = by_micro(qkv)
    q, k, v = qkv[:, :heads], qkv[:, heads : 2 * heads], qkv[:, 2 * heads :]
    gc = by_micro(gc.reshape(R, heads, HD).swapaxes(0, 1))
    at = spots[:, :, 0].reshape(-1)
    low = start.transpose(2, 0, 1, 3).reshape(MB, pack)
    allowed = (low[:, :, None] <= at[None, None, :]) & (at[None, None, :] <= at[None, :, None])
    scale = HD ** -0.5
    raw = jnp.einsum("mhqd,mhkd->mhqk", q, k, preferred_element_type=F32)
    scores = jnp.where(allowed[:, None], raw * scale, MASKED)
    weights = jnp.exp(scores - jnp.max(scores, axis=-1, keepdims=True))
    chance = weights / jnp.sum(weights, axis=-1, keepdims=True)
    chance_low = chance.astype(BF16)
    grad_chance = jnp.einsum("mhqd,mhkd->mhqk", gc, v, preferred_element_type=F32)
    delta = jnp.sum(chance * grad_chance, axis=-1, keepdims=True)
    grad_raw = (chance * (grad_chance - delta) * scale).astype(BF16)
    gq = jnp.einsum("mhqk,mhkd->mhqd", grad_raw, k, preferred_element_type=F32)
    gk = jnp.einsum("mhqk,mhqd->mhkd", grad_raw, q, preferred_element_type=F32)
    gv = jnp.einsum("mhqk,mhqd->mhkd", chance_low, gc, preferred_element_type=F32)
    moved = jnp.stack([gq, gk, gv], axis=0).astype(BF16)
    moved = moved.reshape(3, MB, heads, S * N, piece, HD).transpose(3, 1, 4, 0, 2, 5).reshape(R, 3, heads, HD)
    gqk = moved[:, :2].astype(F32)
    gqk = (gqk * cosine[:, None, None] + jnp.roll(gqk * sine[:, None, None], HD // 2, axis=-1)).astype(BF16)
    grad_qkv = jnp.concatenate([gqk, moved[:, 2:]], axis=1).reshape(R, 3 * width)
    g_bias = jnp.sum(grad_qkv.astype(F32), axis=0)
    g_in = dot_t(normed_all.reshape(R, D), grad_qkv)
    partial = dot_nt(grad_qkv, w_in).astype(BF16).reshape(S, L, D)
    partial = lax.all_to_all(partial, "seq", split_axis=0, concat_axis=0, tiled=True)
    grad_normed = jnp.sum(partial.astype(F32), axis=0)
    from_first, g_gain_1 = rms_backward(grad_normed, unit_1, inverse_1, gain_1)
    grad_x = (grad_hidden + from_first).astype(BF16)

    back = jnp.concatenate([mixed, grad_x], axis=1).reshape(N, MB * piece, 2 * D)
    back = lax.all_to_all(back, "fsdp", split_axis=0, concat_axis=0, tiled=True).reshape(N, MB, piece, 2 * D)
    back = jnp.stack([jnp.take(back[:, m], deal[m, f], axis=0).swapaxes(0, 1) for m in range(MB)]).reshape(MB, T, 2 * D)
    mixed, grad_tokens = back[..., :D], back[..., D:].astype(F32)

    g_in = lax.psum_scatter(g_in.astype(BF16).reshape(S, N * own, 3 * width), "fsdp", scatter_dimension=1, tiled=True)
    g_in = lax.all_to_all(g_in, "seq", split_axis=0, concat_axis=0, tiled=True)
    g_in = g_in.reshape(S, own, 3, width).transpose(1, 2, 0, 3).reshape(own, 3 * D).astype(F32)
    g_out = lax.psum_scatter(g_out.astype(BF16), "fsdp", scatter_dimension=0, tiled=True).astype(F32)
    g_bias = jnp.where(jnp.arange(S)[None, :, None] == s, g_bias.reshape(3, 1, width), 0.0)
    count = S * N
    small = jnp.concatenate(
        [
            g_gain_1.reshape(count, own), g_gain_2.reshape(count, own), g_router.reshape(count, own * E),
            g_shared.reshape(count, own), g_bias.reshape(count, 3 * own),
        ],
        axis=1,
    )
    small = lax.psum_scatter(small, ("seq", "fsdp"), scatter_dimension=0, tiled=True)[0]
    cuts = (own, 2 * own, 2 * own + own * E, 3 * own + own * E)
    return (
        mixed, grad_tokens, g_in, small[cuts[3] :], g_out, small[: cuts[0]], small[cuts[0] : cuts[1]],
        small[cuts[1] : cuts[2]].reshape(own, E), small[cuts[2] : cuts[3]],
        g_eg[None], g_eu[None], grad_b[:FE][None], g_sg, g_su, grad_b[FE:],
    )


def solution(mesh):
    both = ("seq", "fsdp")
    in_specs = (
        P(None, both, None), P(None, both, None), P(None, both, None), P(), P(), P(both, None), P(both), P(both, None),
        P(both), P(both), P(both, None), P(both), P("fsdp", "seq", None), P("fsdp", "seq", None),
        P("fsdp", None, "seq"), P("seq", "fsdp"), P("seq", "fsdp"), P("fsdp", "seq"),
    )
    out_specs = (
        P(None, both, None), P(None, both, None), P(both, None), P(both), P(both, None), P(both), P(both),
        P(both, None), P(both), P("fsdp", "seq", None), P("fsdp", "seq", None), P("fsdp", None, "seq"),
        P("seq", "fsdp"), P("seq", "fsdp"), P("fsdp", "seq"),
    )
    return jax.shard_map(shards, mesh=mesh, in_specs=in_specs, out_specs=out_specs, check_vma=False)
```

```python
import functools

import jax
import jax.numpy as jnp
from jax import lax
from jax.experimental import pallas as pl
from jax.experimental.pallas import tpu as pltpu
from jax.sharding import PartitionSpec as P

H = 16
HD = 128
TOP = 4
EPS = 1e-06
THETA = 1000000.0
MASKED = -1e30
F32 = jnp.float32
BF16 = jnp.bfloat16
MESH = pl.DeviceIdType.MESH
VMEM_LIMIT = 61 * 2**20

ORDER = ((0, 0), (0, 1), (2, 0), (1, 1), (1, 0), (3, 0), (2, 1), (3, 1))


def dot(a, b):
    return jnp.dot(a, b, preferred_element_type=F32)


def dot_t(a, b):
    return lax.dot_general(a, b, (((0,), (0,)), ((), ())), preferred_element_type=F32)


def dot_nt(a, b):
    return lax.dot_general(a, b, (((1,), (1,)), ((), ())), preferred_element_type=F32)


def turn(u):
    half = u.shape[-1] // 2
    return jnp.concatenate([-u[..., half:], u[..., :half]], axis=-1)


def turn_back(u):
    half = u.shape[-1] // 2
    return jnp.concatenate([u[..., half:], -u[..., :half]], axis=-1)


def rms_forward(values):
    inverse = lax.rsqrt(jnp.mean(values * values, axis=-1, keepdims=True) + EPS)
    return values * inverse, inverse


def rms_backward(grad, unit, inverse, gain):
    scaled = grad * gain
    grad_gain = jnp.sum(grad * unit, axis=tuple(range(grad.ndim - 1)))
    return inverse * (scaled - unit * jnp.mean(scaled * unit, axis=-1, keepdims=True)), grad_gain


def across(a, which):
    return lax.ppermute(a, "seq", [(i, i ^ which) for i in range(4)])


def split3(v):
    hi = lax.reduce_precision(v, 8, 7)
    mid = lax.reduce_precision(v - hi, 8, 7)
    low = lax.reduce_precision(v - hi - mid, 8, 7)
    return hi, mid, low


def swiglu_back(grad_act, gate, up):
    sig = jax.nn.sigmoid(gate)
    grad_gate = (grad_act * up * sig * (1.0 + gate * (1.0 - sig))).astype(BF16)
    grad_up = (grad_act * gate * sig).astype(BF16)
    return grad_gate, grad_up


def partners(s):
    return s + 1 - 2 * lax.rem(s, 2), lax.rem(s + 2, 4), 3 - s


def greet(s, f, S, N):
    barrier = pltpu.get_barrier_semaphore()
    for other in partners(s):
        pl.semaphore_signal(barrier, inc=1, device_id=(other, f), device_id_type=MESH)
    for step in range(1, N):
        pl.semaphore_signal(barrier, inc=1, device_id=(s, lax.rem(f + step, N)), device_id_type=MESH)
    pl.semaphore_wait(barrier, S - 1 + N - 1)


class Line:
    def __init__(self, s, f, N, block, move_send, move_recv, side_send, side_recv):
        self.s, self.chip, self.core, self.n = s, f // 2, lax.rem(f, 2), N // 2
        self.block = block
        self.move_send, self.move_recv = move_send, move_recv
        self.side_send, self.side_recv = side_send, side_recv

    def move(self, way, step, origin, to):
        ref = self.block(2 * origin + self.core)
        return pltpu.make_async_remote_copy(
            ref, ref, self.move_send.at[way, step], self.move_recv.at[way, step],
            device_id=(self.s, 2 * to + self.core), device_id_type=MESH,
        )

    def side(self, origin, core):
        ref = self.block(2 * origin + core)
        return pltpu.make_async_remote_copy(
            ref, ref, self.side_send.at[origin], self.side_recv.at[origin],
            device_id=(self.s, 2 * self.chip + 1 - self.core), device_id_type=MESH,
        )

    def send(self, step, act):
        q, n = self.chip, self.n

        @pl.when((q - step >= 0) & (q + 1 < n))
        def _():
            act(self.move(0, step, jnp.maximum(q - step, 0), jnp.minimum(q + 1, n - 1)))

        @pl.when((q + step < n) & (q >= 1))
        def _():
            act(self.move(1, step, jnp.minimum(q + step, n - 1), jnp.maximum(q - 1, 0)))

    def begin(self):
        self.send(0, lambda copy: copy.start())
        self.side(self.chip, self.core).start()

    def step(self, step):
        q, n = self.chip, self.n

        @pl.when(q - 1 - step >= 0)
        def _():
            origin = jnp.maximum(q - 1 - step, 0)
            self.move(0, step, origin, jnp.maximum(q - 1, 0)).wait_recv()
            if step + 1 < n - 1:

                @pl.when(q + 1 < n)
                def _():
                    self.move(0, step + 1, origin, jnp.minimum(q + 1, n - 1)).start()

            self.side(origin, self.core).start()

        @pl.when(q + 1 + step < n)
        def _():
            origin = jnp.minimum(q + 1 + step, n - 1)
            self.move(1, step, origin, jnp.minimum(q + 1, n - 1)).wait_recv()
            if step + 1 < n - 1:

                @pl.when(q >= 1)
                def _():
                    self.move(1, step + 1, origin, jnp.maximum(q - 1, 0)).start()

            self.side(origin, self.core).start()

    def arrive(self):
        for origin in range(self.n):
            self.side(origin, 1 - self.core).wait_recv()

    def drain(self):
        for step in range(self.n - 1):
            self.send(step, lambda copy: copy.wait_send())
        for origin in range(self.n):
            self.side(origin, self.core).wait_send()


PLACE = {key: i for i, key in enumerate(ORDER)}


def gather_vector(small, row, length, own, N):
    per = 128 // own
    for block in range(length // 128):
        total = None
        for i in range(block * per, (block + 1) * per):
            part = small[i % N, i // N, row : row + 1, :]
            total = part if total is None else total + part
        yield block, total


def forward_kernel(S, N, sizes, *refs):
    MB, piece, D, own, heads = sizes
    tok, cot, wq, wo, small, *refs = refs
    shards_in, refs = refs[:6], refs[6:]
    cos, sin, first, place, place_row, *refs = refs
    x_rows, g_all, w_in, w_back, small_all, normed_out, qkv_out, ctx_out, hid_out, x_all, *refs = refs
    fulls, refs = refs[:6], refs[6:]
    cot_by, shard_by, refs = refs[0], refs[1:7], refs[7:]
    small_v, tok_v, w_v, wb_v, x_v, gain_v, bias_v, na_v, qkv_v, ctx_v, part_send, part_recv, hid_v, n2_v, xo_v, *refs = refs
    (local_sem, deal_send, deal_recv, seq_send, seq_recv, small_send, small_recv, half_send, half_recv, part_sems,
     part_semr, norm_sems, norm_semr, out_sem, *line_sems) = refs
    s, f = lax.axis_index("seq"), lax.axis_index("fsdp")
    px, py, pd = partners(s)
    eighth = D // 8
    pr = MB * piece
    L = pr * N
    R = S * L
    width = heads * HD

    def spot(full, i, where):
        cut = pl.ds(where * eighth, eighth)
        return full.at[cut] if i < 2 else full.at[:, cut]

    def own_half(shard, i, half):
        cut = pl.ds(half * eighth, eighth)
        return shard.at[cut] if i < 2 else shard.at[:, cut]

    def remote(src, dst, send, recv, device):
        return pltpu.make_async_remote_copy(src, dst, send, recv, device_id=device, device_id_type=MESH)

    pairs = [
        (small, small_v.at[f, s]), (wq.at[s], w_v.at[s, f]), (wo, wb_v.at[f]), (tok.at[f], tok_v.at[f]), (cot.at[f], cot_by),
    ] + list(zip(shards_in, shard_by))
    take = [pltpu.make_async_copy(a, b, local_sem.at[i]) for i, (a, b) in enumerate(pairs)]
    put = [pltpu.make_async_copy(cot_by, g_all.at[f, f], local_sem.at[4])]
    for i in range(6):
        cut = pl.ds(0, 2 * eighth)
        target = fulls[i].at[cut] if i < 2 else fulls[i].at[:, cut]
        put.append(pltpu.make_async_copy(shard_by[i], target, local_sem.at[5 + i]))
    for copy in take:
        copy.start()
    greet(s, f, S, N)

    over_seq = []
    for k, other in enumerate((px, py, pd)):
        over_seq.append(remote(small, small_v.at[f, s], seq_send.at[0, k], seq_recv.at[0, k], (other, f)))
        over_seq.append(remote(wq.at[other], w_v.at[s, f], seq_send.at[1, k], seq_recv.at[1, k], (other, f)))
    for copy in over_seq:
        copy.start()
    deal_tok, deal_cot, to_all = [], [], []
    for k in range(1, N):
        to = lax.rem(f + k, N)
        deal_tok.append(remote(tok.at[to], tok_v.at[f], deal_send.at[0, k - 1], deal_recv.at[0, k - 1], (s, to)))
        deal_cot.append(remote(cot.at[to], g_all.at[to, f], deal_send.at[1, k - 1], deal_recv.at[1, k - 1], (s, to)))
        to_all.append(remote(small_v.at[f], small_v.at[f], small_send.at[k - 1], small_recv.at[k - 1], (s, to)))
    for copy in deal_tok:
        copy.start()

    def half_copy(i, k):
        where, rel, half = ((px, 1, 0), (py, 2, 1), (py, 2, 0), (px, 1, 1))[k]
        return remote(
            own_half(shards_in[i], i, half), spot(fulls[i], i, PLACE[rel, half]), half_send.at[i, k], half_recv.at[i, k],
            (where, f),
        )

    def pass_copy(i, k):
        where, rel, half = ((py, 1, 0), (px, 2, 1))[k]
        return remote(
            spot(fulls[i], i, PLACE[rel, half]), spot(fulls[i], i, PLACE[3, half]), half_send.at[i, 4 + k],
            half_recv.at[i, 4 + k], (where, f),
        )

    def give(i):
        for k in range(4):
            half_copy(i, k).start()

    def pass_on(i):
        for k in range(2):
            half_copy(i, k).wait_recv()
            pass_copy(i, k).start()

    give(0)
    for copy in take:
        copy.wait()
    for copy in put:
        copy.start()
    for copy in over_seq:
        copy.wait_recv()
    for copy in to_all:
        copy.start()
    w_line = Line(s, f, N, lambda j: w_v.at[:, j], *line_sems[0:4])
    b_line = Line(s, f, N, lambda j: wb_v.at[j], *line_sems[4:8])
    g_line = Line(s, f, N, lambda j: g_all.at[j], *line_sems[8:12])
    x_line = Line(s, f, N, lambda j: x_all.at[j], *line_sems[12:16])
    w_line.begin()
    b_line.begin()

    for copy in deal_tok + to_all:
        copy.wait_recv()
    for row in range(2):
        for block, part in gather_vector(small_v, row, D, own, N):
            gain_v[row : row + 1, block * 128 : (block + 1) * 128] = part
    nb = 3 * own
    for line in range(3 * D // 128):
        total = None
        for i in range(S * N):
            for half in range(2):
                if (i * nb) // 128 + half == line and (half == 0 or (i * nb) % 128 + nb > 128):
                    part = small_v[i % N, i // N, 2 + half : 3 + half, :]
                    total = part if total is None else total + part
        bias_v[line : line + 1, :] = total
    for j in range(N):
        x_v[j * pr : (j + 1) * pr, :] = tok_v[j].astype(F32)
    x = x_v[...]
    inverse = lax.rsqrt(jnp.mean(x * x, axis=-1, keepdims=True) + EPS)
    na_v[s] = (x * inverse * gain_v[0:1, :]).astype(BF16)
    spread = [
        remote(na_v.at[s], na_v.at[s], norm_sems.at[k], norm_semr.at[k], (other, f)) for k, other in enumerate((px, py, pd))
    ]
    for copy in spread:
        copy.start()
    for copy in deal_cot:
        copy.start()
    give(1)
    chips = N // 2
    for step in range(chips - 1):
        w_line.step(step)
        b_line.step(step)
        if step == 0:
            give(4)
        if step == 1:
            pass_on(0)
    pass_on(1)
    give(2)
    for copy in deal_cot:
        copy.wait_recv()
    for copy in put:
        copy.wait()
    g_line.begin()
    w_line.arrive()
    b_line.arrive()
    for copy in spread:
        copy.wait_recv()

    for t in range(3):

        def project(pair, carry, t=t):
            column = pl.multiple_of(t * width + pair * 2 * HD, 2 * HD)
            w = w_v[:, :, :, pl.ds(column, 2 * HD)].reshape(D, 2 * HD)
            out = dot(na_v[...].reshape(R, D), w)
            for k in range(2):
                u = out[:, k * HD : (k + 1) * HD]
                u = u + bias_v[pl.ds(t * (D // 128) + s * heads + 2 * pair + k, 1), :]
                if t < 2:
                    u = u * cos[...] + pltpu.roll(u, HD // 2, 1) * sin[...]
                qkv_v[t * heads + 2 * pair + k] = u.astype(BF16)
            return carry

        lax.fori_loop(0, heads // 2, project, 0)
    g_line.step(0)

    def attend(h, carry):
        rows = R // 4
        for block in range(4):
            cut = pl.ds(block * rows, rows)
            raw = dot_nt(qkv_v[h, cut, :], qkv_v[heads + h])
            ok = (first[cut, :] <= place_row[...]) & (place_row[...] <= place[cut, :])
            scores = jnp.where(ok, raw * HD**-0.5, MASKED)
            weights = jnp.exp(scores - jnp.max(scores, axis=-1, keepdims=True))
            chance = (weights / jnp.sum(weights, axis=-1, keepdims=True)).astype(BF16)
            ctx_v[cut, pl.ds(pl.multiple_of(h * HD, HD), HD)] = dot(chance, qkv_v[2 * heads + h]).astype(BF16)
        return carry

    lax.fori_loop(0, heads, attend, 0)
    for step in range(1, chips - 1):
        g_line.step(step)
        if step == 1:
            give(3)
            give(5)

    wb = wb_v[...].reshape(width, D)
    exchange = []
    for k, other in enumerate((px, py, pd)):
        rows = pl.ds(pl.multiple_of(other * L, L), L)
        part_send[k] = dot(ctx_v[rows, :], wb).astype(BF16)
        exchange.append(remote(part_send.at[k], part_recv.at[k], part_sems.at[k], part_semr.at[k], (other, f)))
        exchange[-1].start()
    pass_on(4)
    hid_v[...] = x_v[...] + dot(ctx_v[pl.ds(pl.multiple_of(s * L, L), L), :], wb)
    outs = [
        (tok_v, x_rows), (w_v, w_in), (wb_v, w_back), (small_v, small_all), (na_v, normed_out), (qkv_v, qkv_out),
        (ctx_v, ctx_out), (hid_v, hid_out), (xo_v, x_all.at[f]),
    ]
    outs = [pltpu.make_async_copy(a, b, out_sem.at[i]) for i, (a, b) in enumerate(outs)]
    for k in range(3):
        exchange[k].wait_recv()
        hid_v[...] += part_recv[k].astype(F32)
    hidden = hid_v[...]
    inverse = lax.rsqrt(jnp.mean(hidden * hidden, axis=-1, keepdims=True) + EPS)
    n2_v[...] = (hidden * inverse * gain_v[1:2, :]).astype(BF16)
    owners = (s, px, py, pd)
    for i, (rel, half) in enumerate(ORDER):
        column = pl.multiple_of((owners[rel] * 2 + half) * eighth, eighth)
        xo_v[:, i * eighth : (i + 1) * eighth] = n2_v[:, pl.ds(column, eighth)]
    outs[8].start()
    outs[8].wait()
    x_line.begin()
    pass_on(2)
    for step in range(chips - 1):
        x_line.step(step)
    pass_on(3)
    pass_on(5)
    for line in (w_line, b_line):
        line.drain()
    for copy in over_seq + to_all + spread:
        copy.wait_send()
    for copy in outs[:8]:
        copy.start()
    for i in range(6):
        for k in range(2, 4):
            half_copy(i, k).wait_recv()
        for k in range(2):
            pass_copy(i, k).wait_recv()
    for i in range(6):
        for k in range(4):
            half_copy(i, k).wait_send()
        for k in range(2):
            pass_copy(i, k).wait_send()
    for line in (g_line, x_line):
        line.arrive()
        line.drain()
    for copy in deal_tok + deal_cot + exchange:
        copy.wait_send()
    for copy in outs[:8]:
        copy.wait()


def forward(S, N, MB, tok, cot, wq, wo, small, shards_in, tables):
    own, D = wo.shape
    pr = tok.shape[1]
    L = pr * N
    R = S * L
    heads = H // S
    width = heads * HD
    chips = N // 2
    dma = pltpu.SemaphoreType.DMA
    line = [dma((2, chips - 1)), dma((2, chips - 1)), dma((chips,)), dma((chips,))]
    shape = jax.ShapeDtypeStruct
    w_shape, wb_shape, small_shape = (S, N) + wq.shape[1:], (N,) + wo.shape, (N, S) + small.shape
    out = [
        shape(tok.shape, BF16), shape((N,) + cot.shape, BF16), shape(w_shape, BF16), shape(wb_shape, BF16),
        shape(small_shape, F32), shape((S, L, D), BF16), shape((3 * heads, R, HD), BF16), shape((R, width), BF16),
        shape((L, D), F32), shape((N, L, D), BF16),
    ]
    for i, shard in enumerate(shards_in):
        rows, columns = shard.shape
        out.append(shape((4 * rows, columns) if i < 2 else (rows, 4 * columns), BF16))
    anywhere = pl.BlockSpec(memory_space=pl.ANY)
    in_vmem = pl.BlockSpec(memory_space=pltpu.VMEM)
    vmem = pltpu.VMEM
    return pl.pallas_call(
        functools.partial(forward_kernel, S, N, (MB, pr // MB, D, own, heads)),
        out_shape=out,
        in_specs=[anywhere] * 11 + [in_vmem] * 5,
        out_specs=[anywhere] * 16,
        scratch_shapes=[vmem(u.shape, u.dtype) for u in (cot[0], *shards_in)]
        + [
            vmem(small_shape, F32), vmem(tok.shape, BF16), vmem(w_shape, BF16), vmem(wb_shape, BF16), vmem((L, D), F32),
            vmem((8, D), F32), vmem((3 * D // 128, 128), F32), vmem((S, L, D), BF16), vmem((3 * heads, R, HD), BF16),
            vmem((R, width), BF16), vmem((3, L, D), BF16), vmem((3, L, D), BF16), vmem((L, D), F32), vmem((L, D), BF16),
            vmem((L, D), BF16),
            dma((11,)), dma((2, N - 1)), dma((2, N - 1)), dma((2, 3)), dma((2, 3)), dma((N - 1,)), dma((N - 1,)),
            dma((6, 6)), dma((6, 6)), dma((3,)), dma((3,)), dma((3,)), dma((3,)), dma((9,)),
        ] + line * 4,
        compiler_params=pltpu.CompilerParams(collective_id=0, has_side_effects=True, vmem_limit_bytes=VMEM_LIMIT),
        name="forward",
    )(tok, cot, wq, wo, small, *shards_in, *tables)


def backward_kernel(S, N, sizes, *refs):
    D, own, heads = sizes
    to_x, to_y, from_x, from_y, keep, refs = refs[:2], refs[2:4], refs[4:8], refs[8:12], refs[12:18], refs[18:]
    w_in, w_back, normed_all, qkv, mixed, gh, unit, inverse, gain_row, ready, ctx, cos, sin, first, place, place_row, *refs = refs
    grads, refs = refs[:6], refs[6:]
    mixed_out, gx_out, gin_out, gout_out, small_out, bias_out, vec_far, gin_buf, gout_buf, gin_pair, gout_pair, *refs = refs
    from_x, from_y, refs = (*refs[:2], *from_x), (*refs[2:4], *from_y), refs[4:]
    then_y, then_x, pair_y, pair_x, refs = refs[:6], refs[6:12], refs[12:18], refs[18:24], refs[24:]
    loads, sums, refs = refs[:3], refs[3:6], refs[6:]
    w_v, wb_v, ga_v, na_v, qkv_v, gc_v, gk_v, gv_v, part_send, part_recv, gn_v, gi_v, go_v, *refs = refs
    in_mine, in_pair, in_stage, in_far, out_mine, out_pair, out_stage, out_far, *refs = refs
    vec_v, vec_tmp, vec_sum, vec_near, mixed_v, gx_v, *refs = refs
    (step_send, step_recv, load_sem, ga_send, ga_recv, part_sems, part_semr, pair_send, pair_recv, far_send, far_recv,
     last_send, last_recv, vec_sems, vec_semr, near_sems, near_semr, home_send, home_recv, local_sem) = refs
    s, f = lax.axis_index("seq"), lax.axis_index("fsdp")
    px, py, pd = partners(s)
    chip, core, chips = f // 2, lax.rem(f, 2), N // 2
    eighth = D // 8
    L = gh.shape[0]
    R = S * L
    width = heads * HD
    pr = L // N
    kind = (0, 0, 1, 1, 2, 1)

    def remote(src, dst, send, recv, device):
        return pltpu.make_async_remote_copy(src, dst, send, recv, device_id=device, device_id_type=MESH)

    def part(ref, i, k):
        cut = pl.ds(k * eighth, eighth)
        return ref.at[cut] if i < 2 else ref.at[:, cut]

    def give_copy(i, way):
        a, b, to = ((to_x, from_x, px), (to_y, from_y, py))[way]
        return remote(a[i], b[i], step_send.at[i, way], step_recv.at[i, way], (to, f))

    def then_copy(i, way):
        a, b, to = ((pair_y, then_y, py), (pair_x, then_x, px))[way]
        return remote(a[i], b[i], step_send.at[i, 2 + way], step_recv.at[i, 2 + way], (to, f))

    def give(i):
        for way in range(2):
            give_copy(i, way).start()

    def fetch(i, sources):
        copies = [pltpu.make_async_copy(u, loads[kind[i]].at[k], load_sem.at[k]) for k, u in enumerate(sources)]
        for copy in copies:
            copy.start()
        for copy in copies:
            copy.wait()

    def second(i):
        buf = loads[kind[i]]
        for way, (place_in_keep, arrived) in enumerate(((2, from_x[i]), (3, from_y[i]))):
            if i < 2:
                give_copy(i, way).wait_recv()
            fetch(i, (part(keep[i], i, place_in_keep), part(arrived, i, 1)))
            buf[0] = (buf[0].astype(F32) + buf[1].astype(F32)).astype(BF16)
            copy = pltpu.make_async_copy(buf.at[0], (pair_y, pair_x)[way][i], load_sem.at[0])
            copy.start()
            copy.wait()
            then_copy(i, way).start()

    def third(i):
        buf, total = loads[kind[i]], sums[kind[i]]
        for way, (arrived, last) in enumerate(((from_x[i], then_y[i]), (from_y[i], then_x[i]))):
            then_copy(i, way).wait_recv()
            fetch(i, (part(keep[i], i, way), part(arrived, i, 0), last))
            total[...] = buf[0].astype(F32) + buf[1].astype(F32) + buf[2].astype(F32)
            copy = pltpu.make_async_copy(total, part(grads[i], i, way), load_sem.at[0])
            copy.start()
            copy.wait()

    def reducer(block, pair, mine, other, stage, far, k):
        def pair_copy(q):
            return remote(block(2 * q + 1 - core), pair.at[q], pair_send.at[k, q], pair_recv.at[k, q], (s, 2 * chip + 1 - core))

        def far_copy(d):
            to = lax.rem(chip + d, chips)
            return remote(stage.at[d], far.at[d - 1], far_send.at[k, d - 1], far_recv.at[k, d - 1], (s, 2 * to + core))

        def begin():
            for q in range(chips):
                pair_copy(q).start()

        def middle():
            for q in range(chips):
                pair_copy(q).wait_recv()
            for d in range(1, chips + 1):
                d = d % chips
                q = lax.rem(chip + d, chips)
                copies = (
                    pltpu.make_async_copy(block(2 * q + core), mine, load_sem.at[0]),
                    pltpu.make_async_copy(pair.at[q], other, load_sem.at[1]),
                )
                for copy in copies:
                    copy.start()
                for copy in copies:
                    copy.wait()
                stage[d] = (mine[...].astype(F32) + other[...].astype(F32)).astype(BF16)
                if d:
                    far_copy(d).start()

        def end():
            total = stage[0].astype(F32)
            for d in range(1, chips):
                far_copy(d).wait_recv()
                total = total + far[d - 1].astype(F32)
            return total

        def drain():
            for q in range(chips):
                pair_copy(q).wait_send()
            for d in range(1, chips):
                far_copy(d).wait_send()

        return begin, middle, end, drain

    in_begin, in_middle, in_end, in_drain = reducer(
        lambda j: gin_buf.at[:, j], gin_pair, in_mine, in_pair, in_stage, in_far, 0)
    out_begin, out_middle, out_end, out_drain = reducer(
        lambda j: gout_buf.at[j], gout_pair, out_mine, out_pair, out_stage, out_far, 1)

    begin = [
        pltpu.make_async_copy(w_back, wb_v, local_sem.at[0]), pltpu.make_async_copy(w_in, w_v, local_sem.at[1]),
        pltpu.make_async_copy(qkv, qkv_v, local_sem.at[2]), pltpu.make_async_copy(normed_all, na_v, local_sem.at[3]),
        pltpu.make_async_copy(mixed.at[f], mixed_v, local_sem.at[4]),
    ]
    for copy in begin:
        copy.start()
    ga_v[s] = gh[...].astype(BF16)
    greet(s, f, S, N)
    spread = [
        remote(ga_v.at[s], ga_v.at[s], ga_send.at[k], ga_recv.at[k], (other, f)) for k, other in enumerate((px, py, pd))
    ]
    for copy in spread:
        copy.start()
    give(0)
    homing = []
    for k in range(1, N):
        to = lax.rem(f + k, N)
        homing.append(remote(mixed.at[to], mixed_out.at[f], home_send.at[0, k - 1], home_recv.at[0, k - 1], (s, to)))
        homing[-1].start()
    for copy in begin:
        copy.wait()
    done = [pltpu.make_async_copy(mixed_v, mixed_out.at[f], local_sem.at[4 + N])]
    done[0].start()
    for copy in spread:
        copy.wait_recv()
    give(1)

    def project(pair, carry):
        out = dot_nt(ga_v[...].reshape(R, D), wb_v.at[pl.ds(pair * (N * 2 // heads), N * 2 // heads)][...].reshape(2 * HD, D))
        gc_v[2 * pair] = out[:, :HD].astype(BF16)
        gc_v[2 * pair + 1] = out[:, HD:].astype(BF16)
        return carry

    lax.fori_loop(0, heads // 2, project, 0)

    def out_grad(column, carry):
        cut = pl.ds(pl.multiple_of(column * 2 * eighth, 2 * eighth), 2 * eighth)
        go_v[:, cut] = dot_t(ctx[...], ga_v[:, :, cut].reshape(R, 2 * eighth)).astype(BF16)
        return carry

    lax.fori_loop(0, 4, out_grad, 0)
    second(4)
    for j in range(N):
        pltpu.make_async_copy(go_v.at[pl.ds(j * own, own)], gout_buf.at[j], local_sem.at[4 + j]).start()
    for j in range(N):
        pltpu.make_async_copy(go_v.at[pl.ds(j * own, own)], gout_buf.at[j], local_sem.at[4 + j]).wait()
    out_begin()

    def attend(h, carry):
        rows = R // 4
        gk_v[...] = jnp.zeros_like(gk_v)
        gv_v[...] = jnp.zeros_like(gv_v)
        for block in range(4):
            cut = pl.ds(block * rows, rows)
            q, gc = qkv_v[h, cut, :], gc_v[h, cut, :]
            raw = dot_nt(q, qkv_v[heads + h])
            ok = (first[cut, :] <= place_row[...]) & (place_row[...] <= place[cut, :])
            scores = jnp.where(ok, raw * HD**-0.5, MASKED)
            weights = jnp.exp(scores - jnp.max(scores, axis=-1, keepdims=True))
            chance = weights / jnp.sum(weights, axis=-1, keepdims=True)
            grad_chance = dot_nt(gc, qkv_v[2 * heads + h])
            delta = jnp.sum(chance * grad_chance, axis=-1, keepdims=True)
            grad_raw = (chance * (grad_chance - delta) * HD**-0.5).astype(BF16)
            gk_v[...] += dot_t(grad_raw, q)
            gv_v[...] += dot_t(chance.astype(BF16), gc)
            gq = dot(grad_raw, qkv_v[heads + h]).astype(BF16).astype(F32)
            gq = gq * cos[cut, :] + pltpu.roll(gq * sin[cut, :], HD // 2, 1)
            qkv_v[h, cut, :] = gq.astype(BF16)
        gk = gk_v[...].astype(BF16).astype(F32)
        gk = gk * cos[...] + pltpu.roll(gk * sin[...], HD // 2, 1)
        qkv_v[heads + h] = gk.astype(BF16)
        qkv_v[2 * heads + h] = gv_v[...].astype(BF16)
        return carry

    lax.fori_loop(0, heads, attend, 0)
    for c in range(3 * heads):
        vec_v[D // 128 + c : D // 128 + c + 1, :] = jnp.sum(qkv_v[c].astype(F32), axis=0, keepdims=True)

    def partial(rows):
        cut = pl.ds(pl.multiple_of(rows * L, L), L)
        left = jnp.concatenate([qkv_v[c, cut, :] for c in range(3 * heads)], axis=1)
        return dot_nt(left, w_v[...].reshape(D, 3 * width))

    exchange = []
    for k, other in enumerate((px, py, pd)):
        part_send[k] = partial(other).astype(BF16)
        exchange.append(remote(part_send.at[k], part_recv.at[k], part_sems.at[k], part_semr.at[k], (other, f)))
        exchange[-1].start()
    gn_v[...] = partial(s)
    second(5)
    second(2)

    def in_grad(i, carry):
        cut = pl.ds(pl.multiple_of(i * 2 * eighth, 2 * eighth), 2 * eighth)
        left = na_v[:, :, cut].reshape(R, 2 * eighth)
        for c in range(0, 3 * heads, 2):
            right = jnp.concatenate([qkv_v[c], qkv_v[c + 1]], axis=1)
            gi_v[:, :, c * HD : (c + 2) * HD] = dot_t(left, right).astype(BF16).reshape(N, own, 2 * HD)
        copy = pltpu.make_async_copy(gi_v, gin_buf.at[i], local_sem.at[0])
        copy.start()
        copy.wait()
        return carry

    lax.fori_loop(0, S, in_grad, 0)
    in_begin()
    out_middle()
    second(3)
    in_middle()
    for k in range(3):
        exchange[k].wait_recv()
        gn_v[...] += part_recv[k].astype(F32)
    scaled = gn_v[...] * gain_row[...]
    scaled = scaled - unit[...] * jnp.mean(scaled * unit[...], axis=-1, keepdims=True)
    gx = (gh[...] + inverse[...] * scaled).astype(BF16)
    for j in range(N):
        gx_v[j] = gx[j * pr : (j + 1) * pr, :]
    done.append(pltpu.make_async_copy(gx_v.at[f], gx_out.at[f], local_sem.at[5 + N]))
    done[1].start()
    for k in range(1, N):
        to = lax.rem(f + k, N)
        homing.append(remote(gx_v.at[to], gx_out.at[f], home_send.at[1, k - 1], home_recv.at[1, k - 1], (s, to)))
        homing[-1].start()
    gain = jnp.sum(gn_v[...] * unit[...], axis=0, keepdims=True)
    for line in range(D // 128):
        vec_v[line : line + 1, :] = gain[:, line * 128 : (line + 1) * 128]
    vec_v[D // 128 + 16 :, :] = ready[...]
    small = []
    for k in range(1, N):
        to = lax.rem(f + k, N)
        small.append(remote(vec_v, vec_far.at[k - 1], vec_sems.at[k - 1], vec_semr.at[k - 1], (s, to)))
        small[-1].start()
    second(0)
    second(1)
    vec_sum[...] = vec_v[...]
    for k in range(1, N):
        small[k - 1].wait_recv()
        copy = pltpu.make_async_copy(vec_far.at[k - 1], vec_tmp, local_sem.at[2])
        copy.start()
        copy.wait()
        vec_sum[...] += vec_tmp[...]
    for k, other in enumerate((px, py, pd)):
        small.append(remote(vec_sum, vec_near.at[k], near_sems.at[k], near_semr.at[k], (other, f)))
        small[-1].start()
    gout_out[...] = out_end()
    in_stage[0] = in_end().astype(BF16)
    last = [
        remote(in_stage.at[0, other], gin_out.at[s], last_send.at[k], last_recv.at[k], (other, f))
        for k, other in enumerate((px, py, pd))
    ]
    for copy in last:
        copy.start()
    done.append(pltpu.make_async_copy(in_stage.at[0, s], gin_out.at[s], local_sem.at[1]))
    done[2].start()
    for i in (4, 5, 2, 3, 0, 1):
        third(i)
    for i in range(6):
        for way in range(2):
            if i < 2:
                give_copy(i, way).wait_send()
            then_copy(i, way).wait_send()
    in_drain()
    out_drain()
    for copy in spread + exchange + small:
        copy.wait_send()
    for copy in last + homing:
        copy.wait()
    bias_out[s] = vec_sum[D // 128 : D // 128 + 16, :]
    for k, other in enumerate((px, py, pd)):
        small[N - 1 + k].wait_recv()
        bias_out[other] = vec_near[k, D // 128 : D // 128 + 16, :]
    small_out[...] = vec_sum[...] + vec_near[0] + vec_near[1] + vec_near[2]
    for copy in done:
        copy.wait()


def backward(S, N, to_x, to_y, from_x, from_y, keep, w_in, w_back, normed_all, qkv, mixed, gh, unit, inverse, gain_row, ready, ctx, tables):
    own, D = w_back.shape[1:]
    L = gh.shape[0]
    R = S * L
    heads = H // S
    width = heads * HD
    chips = N // 2
    dma = pltpu.SemaphoreType.DMA
    shape = jax.ShapeDtypeStruct
    vmem = pltpu.VMEM
    eighth = D // 8
    blocks = [(eighth, u.shape[1]) if i < 2 else (u.shape[0], eighth) for i, u in enumerate(keep)]
    wholes = [(2 * eighth, u.shape[1]) if i < 2 else (u.shape[0], 2 * eighth) for i, u in enumerate(keep)]
    kinds = [blocks[i] for i in (0, 2, 4)]
    in_block, out_block = (S, own, 3 * width), (own, D)
    vec = (D // 128 + 16 + ready.shape[0], 128)
    out = [shape(w, F32) for w in wholes] + [
        shape(mixed.shape, BF16), shape(mixed.shape, BF16), shape(in_block, BF16), shape(out_block, F32), shape(vec, F32),
        shape((S, 16, 128), F32),
        shape((N - 1,) + vec, F32),
        shape((S, N) + in_block[1:], BF16), shape((N,) + out_block, BF16), shape((chips,) + in_block, BF16),
        shape((chips,) + out_block, BF16),
    ]
    out += [shape(w, BF16) for w in wholes[:2] * 2] + [shape(b, BF16) for b in blocks * 4]
    anywhere = pl.BlockSpec(memory_space=pl.ANY)
    in_vmem = pl.BlockSpec(memory_space=vmem)
    result = pl.pallas_call(
        functools.partial(backward_kernel, S, N, (D, own, heads)),
        out_shape=out,
        in_specs=[anywhere] * 23 + [in_vmem] * 11,
        out_specs=[anywhere] * 9 + [in_vmem] * 3 + [anywhere] * (len(out) - 12),
        scratch_shapes=[vmem((3,) + k, BF16) for k in kinds] + [vmem(k, F32) for k in kinds]
        + [
            vmem(w_in.shape, BF16), vmem(w_back.shape, BF16), vmem((S, L, D), BF16), vmem((S, L, D), BF16),
            vmem(qkv.shape, BF16), vmem((heads, R, HD), BF16), vmem((R, HD), F32), vmem((R, HD), F32),
            vmem((3, L, D), BF16), vmem((3, L, D), BF16), vmem((L, D), F32), vmem((N, own, 3 * width), BF16),
            vmem((width, D), BF16),
            vmem(in_block, BF16), vmem(in_block, BF16), vmem((chips,) + in_block, BF16), vmem((chips - 1,) + in_block, BF16),
            vmem(out_block, BF16), vmem(out_block, BF16), vmem((chips,) + out_block, BF16),
            vmem((chips - 1,) + out_block, BF16),
            vmem(vec, F32), vmem(vec, F32), vmem(vec, F32), vmem((3,) + vec, F32),
            vmem(mixed.shape[1:], BF16), vmem(mixed.shape, BF16),
            dma((6, 4)), dma((6, 4)), dma((3,)), dma((3,)), dma((3,)), dma((3,)), dma((3,)), dma((2, chips)),
            dma((2, chips)), dma((2, chips - 1)), dma((2, chips - 1)), dma((3,)), dma((3,)), dma((N - 1,)), dma((N - 1,)),
            dma((3,)), dma((3,)), dma((2, N - 1)), dma((2, N - 1)), dma((6 + N,)),
        ],
        compiler_params=pltpu.CompilerParams(collective_id=1, has_side_effects=True, vmem_limit_bytes=VMEM_LIMIT),
        name="backward",
    )(*to_x, *to_y, *from_x, *from_y, *keep, w_in, w_back, normed_all, qkv, mixed, gh, unit, inverse, gain_row, ready, ctx, *tables)
    return result[:12]


def shards(
    tokens, cotangent, ids, deal, lengths, w_qkv, b_qkv, w_out, gain_attn, gain_ffn, w_router,
    w_shared_gate, e_gate, e_up, e_down, s_gate, s_up, s_down,
):
    S, N = lax.axis_size("seq"), lax.axis_size("fsdp")
    s, f = lax.axis_index("seq"), lax.axis_index("fsdp")
    MB, T, D = tokens.shape
    E = w_router.shape[1]
    assert S == 4 and e_gate.shape[0] == 1 and E == N
    FE, FS = e_gate.shape[2], s_gate.shape[1]
    piece = T // N
    pack = T * S
    heads = H // S
    width = heads * HD
    rows = N * MB * T
    own = w_out.shape[0]

    order = jnp.stack([jnp.bitwise_xor(s, rel) * 2 + half for rel, half in ORDER])
    inverse_order = jnp.argsort(order)

    def arrange(u, by):
        return jnp.take(u.reshape(u.shape[:-1] + (8, D // 8)), by, axis=u.ndim - 1).reshape(u.shape)

    inverse_deal = jnp.argsort(deal, axis=2)

    def deal_out(u):
        u = u.reshape(MB, piece, N, D)
        u = jnp.stack([jnp.take(u[m], inverse_deal[m, f], axis=1) for m in range(MB)])
        return u.transpose(2, 0, 1, 3).reshape(N, MB * piece, D)

    index = s * N + f

    def placed(u, length):
        return lax.dynamic_update_slice(jnp.zeros((length,), F32), u.astype(F32), ((index * u.shape[0]) % 128,))

    parts = [placed(gain_attn, 128), placed(gain_ffn, 128), placed(b_qkv, 256), placed(w_shared_gate, 128)]
    for u in (w_router.reshape(-1), ids.reshape(-1)):
        parts.append(jnp.pad(u.astype(F32), (0, -u.shape[0] % 128)))
    r_line = 5
    i_line = r_line + parts[4].shape[0] // 128
    small = jnp.concatenate(parts)
    small = jnp.pad(small, (0, -small.shape[0] % 1024)).reshape(-1, 128)

    spots = ((jnp.arange(S)[:, None, None] * piece + jnp.arange(piece)[None, None, :]) * N + jnp.arange(N)[None, :, None])
    spots = jnp.broadcast_to(spots[:, :, None, :], (S, N, MB, piece)).astype(jnp.int32)
    micro = jnp.arange(MB, dtype=jnp.int32)[None, None, :, None]
    my_lengths = lengths[:, f]
    ends = jnp.cumsum(my_lengths, axis=1)
    past = ends[None, None, :, None, :] <= spots[..., None]
    start = jnp.sum(jnp.where(past, my_lengths[None, None, :, None, :], 0), axis=4)
    frequency = THETA ** (-jnp.arange(0, HD, 2, dtype=F32) / HD)
    angle = (spots - start).astype(F32).reshape(-1, 1) * frequency
    cosine, sine = jnp.cos(angle), jnp.sin(angle)
    cosine = jnp.concatenate([cosine, cosine], axis=1)
    sine = jnp.concatenate([-sine, sine], axis=1)
    place = (spots + pack * micro).reshape(-1)
    first = (start + pack * micro).reshape(-1)
    tables = (cosine, sine, first[:, None], place[:, None], place[None, :])

    wq = w_qkv.reshape(own, 3, S, width).transpose(2, 0, 1, 3).reshape(S, own, 3 * width)
    x_rows, g_all, w_in, w_back, small, normed_all, qkv, context, hidden, x_all, *fulls = forward(
        S, N, MB, deal_out(tokens), deal_out(arrange(cotangent, order)), wq, w_out, small,
        (e_gate[0], e_up[0], s_gate.T, s_up.T, e_down[0], s_down), tables,
    )
    L, R = MB * T, MB * pack

    def vector(row):
        return small[:, :, row].swapaxes(0, 1).reshape(D // 128, 128 // own, 128).sum(1).reshape(D)

    gain_1, gain_2, shared_w = vector(0), vector(1), vector(4).astype(BF16)
    router_w = small[:, :, r_line:i_line].swapaxes(0, 1).reshape(S * N, -1)[:, : own * E].reshape(D, E).astype(BF16)
    all_ids = small[:, :, i_line:].reshape(N, S, -1)[:, :, : MB * T * TOP]
    eg, eu, sg, su, ed, sd = fulls
    x0 = x_rows.reshape(L, D).astype(F32)
    cot = arrange(lax.dynamic_index_in_dim(g_all, f, 0, keepdims=False).reshape(L, D), inverse_order)
    g_rows = g_all.reshape(rows, D)
    all_ids = lax.dynamic_index_in_dim(all_ids, s, 1, keepdims=False).reshape(N, MB, piece, N, TOP)
    where = inverse_deal.transpose(2, 1, 0)
    chosen = jnp.take_along_axis(
        all_ids[None], where[:, :, :, None, None, None], axis=4
    ).reshape(N, L, TOP).astype(jnp.int32)
    own_ids = lax.dynamic_index_in_dim(chosen, f, 0, keepdims=False)
    chosen = chosen.reshape(rows, TOP)
    x = x_all.reshape(rows, D)
    x_own = lax.dynamic_index_in_dim(x_all, f, 0, keepdims=False)
    unit_1, inverse_1 = rms_forward(x0)
    unit_2, inverse_2 = rms_forward(hidden)

    lead = jnp.concatenate([router_w, shared_w[:, None]], axis=1)
    lead_order = jnp.take(lead.reshape(8, D // 8, E + 1), order, axis=0).reshape(D, E + 1)
    logits = dot(x, lead_order)
    shifted = jnp.exp(logits[:, :E] - jnp.max(logits[:, :E], axis=-1, keepdims=True))
    router_f = jnp.sum(jnp.where(jnp.arange(E) == f, shifted, 0.0), axis=1) / jnp.sum(shifted, axis=1)
    gate_f = jnp.where(jnp.any(chosen == f, axis=1), router_f, 0.0)[:, None]
    sigma_rows = jax.nn.sigmoid(logits[:, E])[:, None]
    g32 = g_rows.astype(F32)
    geo = (gate_f * g32).astype(BF16)
    gso = (sigma_rows * g32).astype(BF16)

    gate, up = dot(x, eg), dot(x, eu)
    act = (jax.nn.silu(gate) * up).astype(BF16)
    out_e = dot(act, ed).astype(BF16).astype(F32)
    sgate, sup = dot_nt(x, sg), dot_nt(x, su)
    sact = (jax.nn.silu(sgate) * sup).astype(BF16)
    out_s = dot(sact, sd)
    y = (gate_f * out_e + sigma_rows * out_s).astype(BF16)
    y = lax.psum_scatter(y, "fsdp", scatter_dimension=0, tiled=True)
    gg = jnp.sum(g32 * out_e, axis=1)
    gs = jnp.sum(g32 * out_s, axis=1)

    grad_gate, grad_up = swiglu_back(dot_nt(geo, ed), gate, up)
    grad_sgate, grad_sup = swiglu_back(dot_nt(gso, sd), sgate, sup)
    dx_e = (dot_nt(grad_gate, eg) + dot_nt(grad_up, eu)).astype(BF16).astype(F32)
    dx = dx_e + dot(grad_sgate, sg) + dot(grad_sup, su)
    mine = (jnp.arange(N) == f).astype(F32)
    notes = [part[:, None] * mine for value in (gg, gs) for part in split3(value)]
    note_pad = -(6 * N) % 128
    payload = jnp.concatenate([dx] + notes + [jnp.zeros((rows, note_pad), F32)], axis=1).astype(BF16)
    dx = lax.psum_scatter(payload, "fsdp", scatter_dimension=0, tiled=True).astype(F32)

    half = D // 8
    cuts = (slice(4 * half, 6 * half), slice(6 * half, 8 * half), slice(0, 4 * half))

    def by_columns(cut):
        return (
            dot_t(grad_sgate, x[:, cut]).astype(BF16), dot_t(grad_sup, x[:, cut]).astype(BF16),
            dot_t(act, geo[:, cut]).astype(BF16), dot_t(sact, gso[:, cut]).astype(BF16),
        )

    def by_rows(cut):
        return dot_t(x[:, cut], grad_gate).astype(BF16), dot_t(x[:, cut], grad_up).astype(BF16)

    from_x = [across(u, 1) for u in by_columns(cuts[0])]
    from_y = [across(u, 2) for u in by_columns(cuts[1])]
    to_x, to_y = by_rows(cuts[0]), by_rows(cuts[1])
    keep = by_rows(cuts[2]) + by_columns(cuts[2])

    mixed = (hidden + arrange(y, inverse_order).astype(F32)).astype(BF16)
    base = D
    gg_own = sum(dx[:, base + i * N : base + (i + 1) * N] for i in range(3))
    gs_own = jnp.sum(dx[:, base + 3 * N : base + 6 * N], axis=1)
    grad_normed2 = arrange(dx[:, :D], inverse_order)
    flat2 = arrange(x_own, inverse_order)
    logits = dot(x_own, lead_order)
    shifted = jnp.exp(logits[:, :E] - jnp.max(logits[:, :E], axis=-1, keepdims=True))
    router = shifted / jnp.sum(shifted, axis=-1, keepdims=True)
    sigma = jax.nn.sigmoid(logits[:, E])
    picked = jnp.any(own_ids[:, :, None] == jnp.arange(E)[None, None, :], axis=1)
    grad_router = jnp.where(picked, gg_own, 0.0)
    grad_logits = (router * (grad_router - jnp.sum(router * grad_router, axis=-1, keepdims=True))).astype(BF16)
    grad_sigma = gs_own * sigma * (1.0 - sigma)
    grad_normed2 = grad_normed2 + dot_nt(grad_logits, router_w) + grad_sigma[:, None] * shared_w.astype(F32)[None, :]
    g_router = dot_t(flat2, grad_logits)
    g_shared = jnp.sum(grad_sigma[:, None] * flat2.astype(F32), axis=0)
    from_norm, g_gain_2 = rms_backward(grad_normed2, unit_2, inverse_2, gain_2)
    grad_hidden = cot.astype(F32) + from_norm

    ready = jnp.concatenate([g_gain_2, g_shared, g_router.reshape(-1)]).reshape(-1, 128)
    *expert_grads, mixed, grad_x, g_in, g_out, small, g_bias = backward(
        S, N, to_x, to_y, from_x, from_y, keep, w_in, w_back, normed_all, qkv, mixed.reshape(N, MB * piece, D), grad_hidden, unit_1,
        inverse_1, gain_1[None], ready, context, tables,
    )
    def take_home(u):
        u = u.reshape(N, MB, piece, D)
        return jnp.stack([jnp.take(u[:, m], deal[m, f], axis=0).swapaxes(0, 1) for m in range(MB)]).reshape(MB, T, D)

    mixed, grad_tokens = take_home(mixed), take_home(grad_x).astype(F32)

    g_in = g_in.reshape(S, own, 3, width).transpose(1, 2, 0, 3).reshape(own, 3 * D).astype(F32)
    g_bias = g_bias[:, : 3 * heads].reshape(S, 3, width).swapaxes(0, 1).reshape(-1)

    def mine(u):
        return lax.dynamic_slice_in_dim(u, index * (u.shape[0] // (S * N)), u.shape[0] // (S * N))

    small = small.reshape(-1)
    after = D + 16 * 128
    g_gain_1, g_gain_2, g_shared = mine(small[:D]), mine(small[after : after + D]), mine(small[after + D : after + 2 * D])
    g_router = mine(small[after + 2 * D :]).reshape(own, E)
    return (
        mixed, grad_tokens, g_in, mine(g_bias), g_out, g_gain_1, g_gain_2, g_router, g_shared,
        expert_grads[0][None], expert_grads[1][None], expert_grads[4][None], expert_grads[2].T, expert_grads[3].T, expert_grads[5],
    )


def solution(mesh):
    both = ("seq", "fsdp")
    in_specs = (
        P(None, both, None), P(None, both, None), P(None, both, None), P(), P(), P(both, None), P(both), P(both, None),
        P(both), P(both), P(both, None), P(both), P("fsdp", "seq", None), P("fsdp", "seq", None),
        P("fsdp", None, "seq"), P("seq", "fsdp"), P("seq", "fsdp"), P("fsdp", "seq"),
    )
    out_specs = (
        P(None, both, None), P(None, both, None), P(both, None), P(both), P(both, None), P(both), P(both),
        P(both, None), P(both), P("fsdp", "seq", None), P("fsdp", "seq", None), P("fsdp", None, "seq"),
        P("seq", "fsdp"), P("seq", "fsdp"), P("fsdp", "seq"),
    )
    return jax.shard_map(shards, mesh=mesh, in_specs=in_specs, out_specs=out_specs, check_vma=False)
```

```python
import functools

import jax
import jax.numpy as jnp
from jax import lax
from jax.experimental import pallas as pl
from jax.experimental.pallas import tpu as pltpu
from jax.sharding import PartitionSpec as P

H = 16
HD = 128
TOP = 4
EPS = 1e-06
THETA = 1000000.0
MASKED = -1e30
F32 = jnp.float32
BF16 = jnp.bfloat16
MESH = pl.DeviceIdType.MESH
VMEM_LIMIT = 61 * 2**20

ORDER = ((0, 0), (0, 1), (2, 0), (1, 1), (1, 0), (3, 0), (2, 1), (3, 1))


def dot(a, b):
    return jnp.dot(a, b, preferred_element_type=F32)


def dot_t(a, b):
    return lax.dot_general(a, b, (((0,), (0,)), ((), ())), preferred_element_type=F32)


def dot_nt(a, b):
    return lax.dot_general(a, b, (((1,), (1,)), ((), ())), preferred_element_type=F32)


def turn(u):
    half = u.shape[-1] // 2
    return jnp.concatenate([-u[..., half:], u[..., :half]], axis=-1)


def turn_back(u):
    half = u.shape[-1] // 2
    return jnp.concatenate([u[..., half:], -u[..., :half]], axis=-1)


def rms_forward(values):
    inverse = lax.rsqrt(jnp.mean(values * values, axis=-1, keepdims=True) + EPS)
    return values * inverse, inverse


def rms_backward(grad, unit, inverse, gain):
    scaled = grad * gain
    grad_gain = jnp.sum(grad * unit, axis=tuple(range(grad.ndim - 1)))
    return inverse * (scaled - unit * jnp.mean(scaled * unit, axis=-1, keepdims=True)), grad_gain


def across(a, which):
    return lax.ppermute(a, "seq", [(i, i ^ which) for i in range(4)])


def split3(v):
    hi = lax.reduce_precision(v, 8, 7)
    mid = lax.reduce_precision(v - hi, 8, 7)
    low = lax.reduce_precision(v - hi - mid, 8, 7)
    return hi, mid, low


def swiglu_back(grad_act, gate, up):
    sig = jax.nn.sigmoid(gate)
    grad_gate = (grad_act * up * sig * (1.0 + gate * (1.0 - sig))).astype(BF16)
    grad_up = (grad_act * gate * sig).astype(BF16)
    return grad_gate, grad_up


def partners(s):
    return s + 1 - 2 * lax.rem(s, 2), lax.rem(s + 2, 4), 3 - s


def greet(s, f, S, N):
    barrier = pltpu.get_barrier_semaphore()
    for other in partners(s):
        pl.semaphore_signal(barrier, inc=1, device_id=(other, f), device_id_type=MESH)
    for step in range(1, N):
        pl.semaphore_signal(barrier, inc=1, device_id=(s, lax.rem(f + step, N)), device_id_type=MESH)
    pl.semaphore_wait(barrier, S - 1 + N - 1)


class Line:
    def __init__(self, s, f, N, block, move_send, move_recv, side_send, side_recv):
        self.s, self.chip, self.core, self.n = s, f // 2, lax.rem(f, 2), N // 2
        self.block = block
        self.move_send, self.move_recv = move_send, move_recv
        self.side_send, self.side_recv = side_send, side_recv

    def move(self, way, step, origin, to):
        ref = self.block(2 * origin + self.core)
        return pltpu.make_async_remote_copy(
            ref, ref, self.move_send.at[way, step], self.move_recv.at[way, step],
            device_id=(self.s, 2 * to + self.core), device_id_type=MESH,
        )

    def side(self, origin, core):
        ref = self.block(2 * origin + core)
        return pltpu.make_async_remote_copy(
            ref, ref, self.side_send.at[origin], self.side_recv.at[origin],
            device_id=(self.s, 2 * self.chip + 1 - self.core), device_id_type=MESH,
        )

    def send(self, step, act):
        q, n = self.chip, self.n

        @pl.when((q - step >= 0) & (q + 1 < n))
        def _():
            act(self.move(0, step, jnp.maximum(q - step, 0), jnp.minimum(q + 1, n - 1)))

        @pl.when((q + step < n) & (q >= 1))
        def _():
            act(self.move(1, step, jnp.minimum(q + step, n - 1), jnp.maximum(q - 1, 0)))

    def begin(self):
        self.send(0, lambda copy: copy.start())
        self.side(self.chip, self.core).start()

    def step(self, step):
        q, n = self.chip, self.n

        @pl.when(q - 1 - step >= 0)
        def _():
            origin = jnp.maximum(q - 1 - step, 0)
            self.move(0, step, origin, jnp.maximum(q - 1, 0)).wait_recv()
            if step + 1 < n - 1:

                @pl.when(q + 1 < n)
                def _():
                    self.move(0, step + 1, origin, jnp.minimum(q + 1, n - 1)).start()

            self.side(origin, self.core).start()

        @pl.when(q + 1 + step < n)
        def _():
            origin = jnp.minimum(q + 1 + step, n - 1)
            self.move(1, step, origin, jnp.minimum(q + 1, n - 1)).wait_recv()
            if step + 1 < n - 1:

                @pl.when(q >= 1)
                def _():
                    self.move(1, step + 1, origin, jnp.maximum(q - 1, 0)).start()

            self.side(origin, self.core).start()

    def arrive(self):
        for origin in range(self.n):
            self.side(origin, 1 - self.core).wait_recv()

    def drain(self):
        for step in range(self.n - 1):
            self.send(step, lambda copy: copy.wait_send())
        for origin in range(self.n):
            self.side(origin, self.core).wait_send()


PLACE = {key: i for i, key in enumerate(ORDER)}


def gather_vector(small, row, length, own, N):
    per = 128 // own
    for block in range(length // 128):
        total = None
        for i in range(block * per, (block + 1) * per):
            part = small[i % N, i // N, row : row + 1, :]
            total = part if total is None else total + part
        yield block, total


def forward_kernel(S, N, sizes, *refs):
    MB, piece, D, own, heads = sizes
    tok, cot, wq, wo, small, *refs = refs
    shards_in, refs = refs[:6], refs[6:]
    cos, sin, first, place, place_row, *refs = refs
    x_rows, g_all, w_in, w_back, small_all, normed_out, qkv_out, ctx_out, hid_out, x_all, *refs = refs
    fulls, refs = refs[:6], refs[6:]
    cot_by, shard_by, refs = refs[0], refs[1:7], refs[7:]
    small_v, tok_v, w_v, wb_v, x_v, gain_v, bias_v, na_v, qkv_v, ctx_v, part_send, part_recv, hid_v, n2_v, xo_v, *refs = refs
    (local_sem, deal_send, deal_recv, seq_send, seq_recv, small_send, small_recv, half_send, half_recv, part_sems,
     part_semr, norm_sems, norm_semr, out_sem, *line_sems) = refs
    s, f = lax.axis_index("seq"), lax.axis_index("fsdp")
    px, py, pd = partners(s)
    eighth = D // 8
    pr = MB * piece
    L = pr * N
    R = S * L
    width = heads * HD

    def spot(full, i, where):
        cut = pl.ds(where * eighth, eighth)
        return full.at[cut] if i < 2 else full.at[:, cut]

    def own_half(shard, i, half):
        cut = pl.ds(half * eighth, eighth)
        return shard.at[cut] if i < 2 else shard.at[:, cut]

    def remote(src, dst, send, recv, device):
        return pltpu.make_async_remote_copy(src, dst, send, recv, device_id=device, device_id_type=MESH)

    pairs = [
        (small, small_v.at[f, s]), (wq.at[s], w_v.at[s, f]), (wo, wb_v.at[f]), (tok.at[f], tok_v.at[f]), (cot.at[f], cot_by),
    ] + list(zip(shards_in, shard_by))
    take = [pltpu.make_async_copy(a, b, local_sem.at[i]) for i, (a, b) in enumerate(pairs)]
    put = [pltpu.make_async_copy(cot_by, g_all.at[f, f], local_sem.at[4])]
    for i in range(6):
        cut = pl.ds(0, 2 * eighth)
        target = fulls[i].at[cut] if i < 2 else fulls[i].at[:, cut]
        put.append(pltpu.make_async_copy(shard_by[i], target, local_sem.at[5 + i]))
    for copy in take:
        copy.start()
    greet(s, f, S, N)

    over_seq = []
    for k, other in enumerate((px, py, pd)):
        over_seq.append(remote(small, small_v.at[f, s], seq_send.at[0, k], seq_recv.at[0, k], (other, f)))
        over_seq.append(remote(wq.at[other], w_v.at[s, f], seq_send.at[1, k], seq_recv.at[1, k], (other, f)))
    for copy in over_seq:
        copy.start()
    deal_tok, deal_cot, to_all = [], [], []
    for k in range(1, N):
        to = lax.rem(f + k, N)
        deal_tok.append(remote(tok.at[to], tok_v.at[f], deal_send.at[0, k - 1], deal_recv.at[0, k - 1], (s, to)))
        deal_cot.append(remote(cot.at[to], g_all.at[to, f], deal_send.at[1, k - 1], deal_recv.at[1, k - 1], (s, to)))
        to_all.append(remote(small_v.at[f], small_v.at[f], small_send.at[k - 1], small_recv.at[k - 1], (s, to)))
    for copy in deal_tok:
        copy.start()

    def half_copy(i, k):
        where, rel, half = ((px, 1, 0), (py, 2, 1), (py, 2, 0), (px, 1, 1))[k]
        return remote(
            own_half(shards_in[i], i, half), spot(fulls[i], i, PLACE[rel, half]), half_send.at[i, k], half_recv.at[i, k],
            (where, f),
        )

    def pass_copy(i, k):
        where, rel, half = ((py, 1, 0), (px, 2, 1))[k]
        return remote(
            spot(fulls[i], i, PLACE[rel, half]), spot(fulls[i], i, PLACE[3, half]), half_send.at[i, 4 + k],
            half_recv.at[i, 4 + k], (where, f),
        )

    def give(i):
        for k in range(4):
            half_copy(i, k).start()

    def pass_on(i):
        for k in range(2):
            half_copy(i, k).wait_recv()
            pass_copy(i, k).start()

    give(0)
    for copy in take:
        copy.wait()
    for copy in put:
        copy.start()
    for copy in over_seq:
        copy.wait_recv()
    for copy in to_all:
        copy.start()
    w_line = Line(s, f, N, lambda j: w_v.at[:, j], *line_sems[0:4])
    b_line = Line(s, f, N, lambda j: wb_v.at[j], *line_sems[4:8])
    g_line = Line(s, f, N, lambda j: g_all.at[j], *line_sems[8:12])
    x_line = Line(s, f, N, lambda j: x_all.at[j], *line_sems[12:16])
    w_line.begin()
    b_line.begin()

    for copy in deal_tok + to_all:
        copy.wait_recv()
    for row in range(2):
        for block, part in gather_vector(small_v, row, D, own, N):
            gain_v[row : row + 1, block * 128 : (block + 1) * 128] = part
    nb = 3 * own
    for line in range(3 * D // 128):
        total = None
        for i in range(S * N):
            for half in range(2):
                if (i * nb) // 128 + half == line and (half == 0 or (i * nb) % 128 + nb > 128):
                    part = small_v[i % N, i // N, 2 + half : 3 + half, :]
                    total = part if total is None else total + part
        bias_v[line : line + 1, :] = total
    for j in range(N):
        x_v[j * pr : (j + 1) * pr, :] = tok_v[j].astype(F32)
    x = x_v[...]
    inverse = lax.rsqrt(jnp.mean(x * x, axis=-1, keepdims=True) + EPS)
    na_v[s] = (x * inverse * gain_v[0:1, :]).astype(BF16)
    spread = [
        remote(na_v.at[s], na_v.at[s], norm_sems.at[k], norm_semr.at[k], (other, f)) for k, other in enumerate((px, py, pd))
    ]
    for copy in spread:
        copy.start()
    for copy in deal_cot:
        copy.start()
    give(1)
    chips = N // 2
    for step in range(chips - 1):
        w_line.step(step)
        b_line.step(step)
        if step == 0:
            give(4)
        if step == 1:
            pass_on(0)
    pass_on(1)
    give(2)
    for copy in deal_cot:
        copy.wait_recv()
    for copy in put:
        copy.wait()
    g_line.begin()
    w_line.arrive()
    b_line.arrive()
    for copy in spread:
        copy.wait_recv()

    for t in range(3):

        def project(pair, carry, t=t):
            column = pl.multiple_of(t * width + pair * 2 * HD, 2 * HD)
            w = w_v[:, :, :, pl.ds(column, 2 * HD)].reshape(D, 2 * HD)
            out = dot(na_v[...].reshape(R, D), w)
            for k in range(2):
                u = out[:, k * HD : (k + 1) * HD]
                u = u + bias_v[pl.ds(t * (D // 128) + s * heads + 2 * pair + k, 1), :]
                if t < 2:
                    u = u * cos[...] + pltpu.roll(u, HD // 2, 1) * sin[...]
                qkv_v[t * heads + 2 * pair + k] = u.astype(BF16)
            return carry

        lax.fori_loop(0, heads // 2, project, 0)
    g_line.step(0)

    def attend(h, carry):
        rows = R // 4
        for block in range(4):
            cut = pl.ds(block * rows, rows)
            raw = dot_nt(qkv_v[h, cut, :], qkv_v[heads + h])
            ok = (first[cut, :] <= place_row[...]) & (place_row[...] <= place[cut, :])
            scores = jnp.where(ok, raw * HD**-0.5, MASKED)
            weights = jnp.exp(scores - jnp.max(scores, axis=-1, keepdims=True))
            chance = (weights / jnp.sum(weights, axis=-1, keepdims=True)).astype(BF16)
            ctx_v[cut, pl.ds(pl.multiple_of(h * HD, HD), HD)] = dot(chance, qkv_v[2 * heads + h]).astype(BF16)
        return carry

    lax.fori_loop(0, heads, attend, 0)
    for step in range(1, chips - 1):
        g_line.step(step)
        if step == 1:
            give(3)
            give(5)

    wb = wb_v[...].reshape(width, D)
    exchange = []
    for k, other in enumerate((px, py, pd)):
        rows = pl.ds(pl.multiple_of(other * L, L), L)
        part_send[k] = dot(ctx_v[rows, :], wb).astype(BF16)
        exchange.append(remote(part_send.at[k], part_recv.at[k], part_sems.at[k], part_semr.at[k], (other, f)))
        exchange[-1].start()
    pass_on(4)
    hid_v[...] = x_v[...] + dot(ctx_v[pl.ds(pl.multiple_of(s * L, L), L), :], wb)
    outs = [
        (tok_v, x_rows), (w_v, w_in), (wb_v, w_back), (small_v, small_all), (na_v, normed_out), (qkv_v, qkv_out),
        (ctx_v, ctx_out), (hid_v, hid_out), (xo_v, x_all.at[f]),
    ]
    outs = [pltpu.make_async_copy(a, b, out_sem.at[i]) for i, (a, b) in enumerate(outs)]
    for k in range(3):
        exchange[k].wait_recv()
        hid_v[...] += part_recv[k].astype(F32)
    hidden = hid_v[...]
    inverse = lax.rsqrt(jnp.mean(hidden * hidden, axis=-1, keepdims=True) + EPS)
    n2_v[...] = (hidden * inverse * gain_v[1:2, :]).astype(BF16)
    owners = (s, px, py, pd)
    for i, (rel, half) in enumerate(ORDER):
        column = pl.multiple_of((owners[rel] * 2 + half) * eighth, eighth)
        xo_v[:, i * eighth : (i + 1) * eighth] = n2_v[:, pl.ds(column, eighth)]
    outs[8].start()
    outs[8].wait()
    x_line.begin()
    pass_on(2)
    for step in range(chips - 1):
        x_line.step(step)
    pass_on(3)
    pass_on(5)
    for line in (w_line, b_line):
        line.drain()
    for copy in over_seq + to_all + spread:
        copy.wait_send()
    for copy in outs[:8]:
        copy.start()
    for i in range(6):
        for k in range(2, 4):
            half_copy(i, k).wait_recv()
        for k in range(2):
            pass_copy(i, k).wait_recv()
    for i in range(6):
        for k in range(4):
            half_copy(i, k).wait_send()
        for k in range(2):
            pass_copy(i, k).wait_send()
    for line in (g_line, x_line):
        line.arrive()
        line.drain()
    for copy in deal_tok + deal_cot + exchange:
        copy.wait_send()
    for copy in outs[:8]:
        copy.wait()


def forward(S, N, MB, tok, cot, wq, wo, small, shards_in, tables):
    own, D = wo.shape
    pr = tok.shape[1]
    L = pr * N
    R = S * L
    heads = H // S
    width = heads * HD
    chips = N // 2
    dma = pltpu.SemaphoreType.DMA
    line = [dma((2, chips - 1)), dma((2, chips - 1)), dma((chips,)), dma((chips,))]
    shape = jax.ShapeDtypeStruct
    w_shape, wb_shape, small_shape = (S, N) + wq.shape[1:], (N,) + wo.shape, (N, S) + small.shape
    out = [
        shape(tok.shape, BF16), shape((N,) + cot.shape, BF16), shape(w_shape, BF16), shape(wb_shape, BF16),
        shape(small_shape, F32), shape((S, L, D), BF16), shape((3 * heads, R, HD), BF16), shape((R, width), BF16),
        shape((L, D), F32), shape((N, L, D), BF16),
    ]
    for i, shard in enumerate(shards_in):
        rows, columns = shard.shape
        out.append(shape((4 * rows, columns) if i < 2 else (rows, 4 * columns), BF16))
    anywhere = pl.BlockSpec(memory_space=pl.ANY)
    in_vmem = pl.BlockSpec(memory_space=pltpu.VMEM)
    vmem = pltpu.VMEM
    return pl.pallas_call(
        functools.partial(forward_kernel, S, N, (MB, pr // MB, D, own, heads)),
        out_shape=out,
        in_specs=[anywhere] * 11 + [in_vmem] * 5,
        out_specs=[anywhere] * 16,
        scratch_shapes=[vmem(u.shape, u.dtype) for u in (cot[0], *shards_in)]
        + [
            vmem(small_shape, F32), vmem(tok.shape, BF16), vmem(w_shape, BF16), vmem(wb_shape, BF16), vmem((L, D), F32),
            vmem((8, D), F32), vmem((3 * D // 128, 128), F32), vmem((S, L, D), BF16), vmem((3 * heads, R, HD), BF16),
            vmem((R, width), BF16), vmem((3, L, D), BF16), vmem((3, L, D), BF16), vmem((L, D), F32), vmem((L, D), BF16),
            vmem((L, D), BF16),
            dma((11,)), dma((2, N - 1)), dma((2, N - 1)), dma((2, 3)), dma((2, 3)), dma((N - 1,)), dma((N - 1,)),
            dma((6, 6)), dma((6, 6)), dma((3,)), dma((3,)), dma((3,)), dma((3,)), dma((9,)),
        ] + line * 4,
        compiler_params=pltpu.CompilerParams(collective_id=0, has_side_effects=True, vmem_limit_bytes=VMEM_LIMIT),
        name="forward",
    )(tok, cot, wq, wo, small, *shards_in, *tables)


def experts_kernel(N, E, *refs):
    x, g, picked, lead, *refs = refs
    weights, refs = refs[:6], refs[6:]
    y, dx, geo, gso, grad_gate, grad_up, grad_sgate, grad_sup, act, sact, *refs = refs
    held, sems = refs[:6], refs[6]
    eg, eu, sg, su, ed, sd = held
    f = lax.axis_index("fsdp")
    D = x.shape[1]
    copies = [pltpu.make_async_copy(a, b, sems.at[i]) for i, (a, b) in enumerate(zip(weights, held))]
    opening = pl.program_id(0) == 0

    @pl.when(opening)
    def _():
        for i in (0, 1, 4, 2, 3, 5):
            copies[i].start()

    def need(i):
        @pl.when(opening)
        def _():
            copies[i].wait()

    rows = x[...]
    logits = dot(rows, lead[...])
    lane = lax.broadcasted_iota(jnp.int32, logits.shape, 1)
    scores = jnp.where(lane < E, logits, MASKED)
    shifted = jnp.exp(scores - jnp.max(scores, axis=-1, keepdims=True))
    share = jnp.sum(jnp.where(lane == f, shifted, 0.0), axis=-1, keepdims=True)
    share = share / jnp.sum(jnp.where(lane < E, shifted, 0.0), axis=-1, keepdims=True)
    gate_f = jnp.where(picked[...] > 0.5, share, 0.0)
    sigma = jax.nn.sigmoid(jnp.sum(jnp.where(lane == E, logits, 0.0), axis=-1, keepdims=True))
    geo[...] = (gate_f * g[...].astype(F32)).astype(BF16)
    gso[...] = (sigma * g[...].astype(F32)).astype(BF16)

    need(0)
    gate = dot(rows, eg[...])
    need(1)
    up = dot(rows, eu[...])
    sig = jax.nn.sigmoid(gate)
    act[...] = (gate * sig * up).astype(BF16)
    need(4)
    grad_act = dot_nt(geo[...], ed[...])
    grad_gate[...] = (grad_act * up * sig * (1.0 + gate * (1.0 - sig))).astype(BF16)
    grad_up[...] = (grad_act * gate * sig).astype(BF16)
    out = dot(act[...], ed[...]).astype(BF16).astype(F32)
    note_e = jnp.sum(out * g[...].astype(F32), axis=-1, keepdims=True)
    out = gate_f * out
    back = (dot_nt(grad_gate[...], eg[...]) + dot_nt(grad_up[...], eu[...])).astype(BF16)

    need(2)
    gate = dot_nt(rows, sg[...])
    need(3)
    up = dot_nt(rows, su[...])
    sig = jax.nn.sigmoid(gate)
    sact[...] = (gate * sig * up).astype(BF16)
    need(5)
    grad_act = dot_nt(gso[...], sd[...])
    grad_sgate[...] = (grad_act * up * sig * (1.0 + gate * (1.0 - sig))).astype(BF16)
    grad_sup[...] = (grad_act * gate * sig).astype(BF16)
    out_s = dot(sact[...], sd[...])
    note_s = jnp.sum(out_s * g[...].astype(F32), axis=-1, keepdims=True)
    y[...] = (out + sigma * out_s).astype(BF16)
    back = back.astype(F32) + dot(grad_sgate[...], sg[...]) + dot(grad_sup[...], su[...])
    dx[:, :D] = back.astype(BF16)
    lane = lax.broadcasted_iota(jnp.int32, (rows.shape[0], dx.shape[1] - D), 1)
    notes = jnp.zeros(lane.shape, F32)
    i = 0
    for value in (note_e, note_s):
        for _ in range(3):
            part = value.astype(BF16).astype(F32)
            notes = jnp.where(lane == i * N + f, part, notes)
            value = value - part
            i += 1
    dx[:, D:] = notes.astype(BF16)


def experts(N, E, x, g, picked, lead, weights):
    rows, D = x.shape
    tile = 256
    FE, FS = weights[0].shape[1], weights[2].shape[0]
    wide = D + 6 * N + -(6 * N) % 128
    columns = (D, wide, D, D, FE, FE, FS, FS, FE, FS)
    once = dict(pipeline_mode=pl.Buffered(1))
    return pl.pallas_call(
        functools.partial(experts_kernel, N, E),
        grid=(rows // tile,),
        out_shape=[jax.ShapeDtypeStruct((rows, c), BF16) for c in columns],
        in_specs=[pl.BlockSpec((tile, c), lambda i: (i, 0)) for c in (D, D, 1)]
        + [pl.BlockSpec(lead.shape, lambda i: (0, 0), **once)] + [pl.BlockSpec(memory_space=pl.ANY)] * 6,
        out_specs=[pl.BlockSpec((tile, c), lambda i: (i, 0)) for c in columns],
        scratch_shapes=[pltpu.VMEM(w.shape, BF16) for w in weights] + [pltpu.SemaphoreType.DMA((6,))],
        compiler_params=pltpu.CompilerParams(
            dimension_semantics=("arbitrary",), vmem_limit_bytes=VMEM_LIMIT
        ),
        cost_estimate=pl.CostEstimate(
            flops=12 * rows * D * (FE + FS), bytes_accessed=40 * rows * D, transcendentals=rows * (FE + FS)
        ),
        name="experts",
    )(x, g, picked, lead, *weights)


def backward_kernel(S, N, sizes, *refs):
    D, own, heads = sizes
    to_x, to_y, stacked_x, stacked_y, keep, refs = refs[:2], refs[2:4], refs[4], refs[5], refs[6:12], refs[12:]
    from_x, from_y, line = [], [], 0
    for ref in keep[2:]:
        from_x.append(stacked_x.at[pl.ds(line, ref.shape[0])])
        from_y.append(stacked_y.at[pl.ds(line, ref.shape[0])])
        line += ref.shape[0]
    w_in, w_back, normed_all, qkv, mixed, gh, unit, inverse, gain_row, ready, ctx, cos, sin, first, place, place_row, *refs = refs
    mixed_out, gx_out, gin_out, gout_out, small_out, bias_out, vec_far, gin_buf, gout_buf, gin_pair, gout_pair, *refs = refs
    from_x, from_y, refs = (*refs[:2], *from_x), (*refs[2:4], *from_y), refs[4:]
    then_y, then_x, pair_y, pair_x, refs = refs[:6], refs[6:12], refs[12:18], refs[18:24], refs[24:]
    loads, refs = refs[:3], refs[3:]
    w_v, wb_v, ga_v, na_v, qkv_v, gc_v, gk_v, gv_v, part_send, part_recv, gn_v, gi_v, go_v, *refs = refs
    in_mine, in_pair, in_stage, in_far, out_mine, out_pair, out_stage, out_far, *refs = refs
    vec_v, vec_tmp, vec_sum, vec_near, mixed_v, gx_v, *refs = refs
    (step_send, step_recv, load_sem, ga_send, ga_recv, part_sems, part_semr, pair_send, pair_recv, far_send, far_recv,
     last_send, last_recv, vec_sems, vec_semr, near_sems, near_semr, home_send, home_recv, local_sem) = refs
    s, f = lax.axis_index("seq"), lax.axis_index("fsdp")
    px, py, pd = partners(s)
    chip, core, chips = f // 2, lax.rem(f, 2), N // 2
    eighth = D // 8
    L = gh.shape[0]
    R = S * L
    width = heads * HD
    pr = L // N
    kind = (0, 0, 1, 1, 2, 1)

    def remote(src, dst, send, recv, device):
        return pltpu.make_async_remote_copy(src, dst, send, recv, device_id=device, device_id_type=MESH)

    def part(ref, i, k):
        cut = pl.ds(k * eighth, eighth)
        return ref.at[cut] if i < 2 else ref.at[:, cut]

    def give_copy(i, way):
        a, b, to = ((to_x, from_x, px), (to_y, from_y, py))[way]
        return remote(a[i], b[i], step_send.at[i, way], step_recv.at[i, way], (to, f))

    def then_copy(i, way):
        a, b, to = ((pair_y, then_y, py), (pair_x, then_x, px))[way]
        return remote(a[i], b[i], step_send.at[i, 2 + way], step_recv.at[i, 2 + way], (to, f))

    def give(i):
        for way in range(2):
            give_copy(i, way).start()

    def fetch(i, sources):
        copies = [pltpu.make_async_copy(u, loads[kind[i]].at[k], load_sem.at[k]) for k, u in enumerate(sources)]
        for copy in copies:
            copy.start()
        for copy in copies:
            copy.wait()

    def second(i):
        buf = loads[kind[i]]
        for way, (place_in_keep, arrived) in enumerate(((2, from_x[i]), (3, from_y[i]))):
            if i < 2:
                give_copy(i, way).wait_recv()
            fetch(i, (part(keep[i], i, place_in_keep), part(arrived, i, 1)))
            buf[0] = (buf[0].astype(F32) + buf[1].astype(F32)).astype(BF16)
            copy = pltpu.make_async_copy(buf.at[0], (pair_y, pair_x)[way][i], load_sem.at[0])
            copy.start()
            copy.wait()
            then_copy(i, way).start()

    def reducer(block, pair, mine, other, stage, far, k):
        def pair_copy(q):
            return remote(block(2 * q + 1 - core), pair.at[q], pair_send.at[k, q], pair_recv.at[k, q], (s, 2 * chip + 1 - core))

        def far_copy(d):
            to = lax.rem(chip + d, chips)
            return remote(stage.at[d], far.at[d - 1], far_send.at[k, d - 1], far_recv.at[k, d - 1], (s, 2 * to + core))

        def begin():
            for q in range(chips):
                pair_copy(q).start()

        def middle():
            for q in range(chips):
                pair_copy(q).wait_recv()
            for d in range(1, chips + 1):
                d = d % chips
                q = lax.rem(chip + d, chips)
                copies = (
                    pltpu.make_async_copy(block(2 * q + core), mine, load_sem.at[0]),
                    pltpu.make_async_copy(pair.at[q], other, load_sem.at[1]),
                )
                for copy in copies:
                    copy.start()
                for copy in copies:
                    copy.wait()
                stage[d] = (mine[...].astype(F32) + other[...].astype(F32)).astype(BF16)
                if d:
                    far_copy(d).start()

        def end():
            total = stage[0].astype(F32)
            for d in range(1, chips):
                far_copy(d).wait_recv()
                total = total + far[d - 1].astype(F32)
            return total

        def drain():
            for q in range(chips):
                pair_copy(q).wait_send()
            for d in range(1, chips):
                far_copy(d).wait_send()

        return begin, middle, end, drain

    in_begin, in_middle, in_end, in_drain = reducer(
        lambda j: gin_buf.at[:, j], gin_pair, in_mine, in_pair, in_stage, in_far, 0)
    out_begin, out_middle, out_end, out_drain = reducer(
        lambda j: gout_buf.at[j], gout_pair, out_mine, out_pair, out_stage, out_far, 1)

    begin = [
        pltpu.make_async_copy(w_back, wb_v, local_sem.at[0]), pltpu.make_async_copy(w_in, w_v, local_sem.at[1]),
        pltpu.make_async_copy(qkv, qkv_v, local_sem.at[2]), pltpu.make_async_copy(normed_all, na_v, local_sem.at[3]),
        pltpu.make_async_copy(mixed.at[f], mixed_v, local_sem.at[4]),
    ]
    for copy in begin:
        copy.start()
    ga_v[s] = gh[...].astype(BF16)
    greet(s, f, S, N)
    spread = [
        remote(ga_v.at[s], ga_v.at[s], ga_send.at[k], ga_recv.at[k], (other, f)) for k, other in enumerate((px, py, pd))
    ]
    for copy in spread:
        copy.start()
    give(0)
    homing = []
    for k in range(1, N):
        to = lax.rem(f + k, N)
        homing.append(remote(mixed.at[to], mixed_out.at[f], home_send.at[0, k - 1], home_recv.at[0, k - 1], (s, to)))
        homing[-1].start()
    for copy in begin:
        copy.wait()
    done = [pltpu.make_async_copy(mixed_v, mixed_out.at[f], local_sem.at[4 + N])]
    done[0].start()
    for copy in spread:
        copy.wait_recv()
    give(1)

    def project(pair, carry):
        out = dot_nt(ga_v[...].reshape(R, D), wb_v.at[pl.ds(pair * (N * 2 // heads), N * 2 // heads)][...].reshape(2 * HD, D))
        gc_v[2 * pair] = out[:, :HD].astype(BF16)
        gc_v[2 * pair + 1] = out[:, HD:].astype(BF16)
        return carry

    lax.fori_loop(0, heads // 2, project, 0)

    def out_grad(column, carry):
        cut = pl.ds(pl.multiple_of(column * 2 * eighth, 2 * eighth), 2 * eighth)
        go_v[:, cut] = dot_t(ctx[...], ga_v[:, :, cut].reshape(R, 2 * eighth)).astype(BF16)
        return carry

    lax.fori_loop(0, 4, out_grad, 0)
    second(4)
    for j in range(N):
        pltpu.make_async_copy(go_v.at[pl.ds(j * own, own)], gout_buf.at[j], local_sem.at[4 + j]).start()
    for j in range(N):
        pltpu.make_async_copy(go_v.at[pl.ds(j * own, own)], gout_buf.at[j], local_sem.at[4 + j]).wait()
    out_begin()

    def attend(h, carry):
        rows = R // 4
        gk_v[...] = jnp.zeros_like(gk_v)
        gv_v[...] = jnp.zeros_like(gv_v)
        for block in range(4):
            cut = pl.ds(block * rows, rows)
            q, gc = qkv_v[h, cut, :], gc_v[h, cut, :]
            raw = dot_nt(q, qkv_v[heads + h])
            ok = (first[cut, :] <= place_row[...]) & (place_row[...] <= place[cut, :])
            scores = jnp.where(ok, raw * HD**-0.5, MASKED)
            weights = jnp.exp(scores - jnp.max(scores, axis=-1, keepdims=True))
            chance = weights / jnp.sum(weights, axis=-1, keepdims=True)
            grad_chance = dot_nt(gc, qkv_v[2 * heads + h])
            delta = jnp.sum(chance * grad_chance, axis=-1, keepdims=True)
            grad_raw = (chance * (grad_chance - delta) * HD**-0.5).astype(BF16)
            gk_v[...] += dot_t(grad_raw, q)
            gv_v[...] += dot_t(chance.astype(BF16), gc)
            gq = dot(grad_raw, qkv_v[heads + h]).astype(BF16).astype(F32)
            gq = gq * cos[cut, :] + pltpu.roll(gq * sin[cut, :], HD // 2, 1)
            qkv_v[h, cut, :] = gq.astype(BF16)
        gk = gk_v[...].astype(BF16).astype(F32)
        gk = gk * cos[...] + pltpu.roll(gk * sin[...], HD // 2, 1)
        qkv_v[heads + h] = gk.astype(BF16)
        qkv_v[2 * heads + h] = gv_v[...].astype(BF16)
        return carry

    lax.fori_loop(0, heads, attend, 0)
    for c in range(3 * heads):
        vec_v[D // 128 + c : D // 128 + c + 1, :] = jnp.sum(qkv_v[c].astype(F32), axis=0, keepdims=True)

    def partial(rows):
        cut = pl.ds(pl.multiple_of(rows * L, L), L)
        left = jnp.concatenate([qkv_v[c, cut, :] for c in range(3 * heads)], axis=1)
        return dot_nt(left, w_v[...].reshape(D, 3 * width))

    exchange = []
    for k, other in enumerate((px, py, pd)):
        part_send[k] = partial(other).astype(BF16)
        exchange.append(remote(part_send.at[k], part_recv.at[k], part_sems.at[k], part_semr.at[k], (other, f)))
        exchange[-1].start()
    gn_v[...] = partial(s)
    second(5)
    second(2)

    def in_grad(i, carry):
        cut = pl.ds(pl.multiple_of(i * 2 * eighth, 2 * eighth), 2 * eighth)
        left = na_v[:, :, cut].reshape(R, 2 * eighth)
        for c in range(0, 3 * heads, 2):
            right = jnp.concatenate([qkv_v[c], qkv_v[c + 1]], axis=1)
            gi_v[:, :, c * HD : (c + 2) * HD] = dot_t(left, right).astype(BF16).reshape(N, own, 2 * HD)
        copy = pltpu.make_async_copy(gi_v, gin_buf.at[i], local_sem.at[0])
        copy.start()
        copy.wait()
        return carry

    lax.fori_loop(0, S, in_grad, 0)
    in_begin()
    out_middle()
    second(3)
    in_middle()
    for k in range(3):
        exchange[k].wait_recv()
        gn_v[...] += part_recv[k].astype(F32)
    scaled = gn_v[...] * gain_row[...]
    scaled = scaled - unit[...] * jnp.mean(scaled * unit[...], axis=-1, keepdims=True)
    gx = (gh[...] + inverse[...] * scaled).astype(BF16)
    for j in range(N):
        gx_v[j] = gx[j * pr : (j + 1) * pr, :]
    done.append(pltpu.make_async_copy(gx_v.at[f], gx_out.at[f], local_sem.at[5 + N]))
    done[1].start()
    for k in range(1, N):
        to = lax.rem(f + k, N)
        homing.append(remote(gx_v.at[to], gx_out.at[f], home_send.at[1, k - 1], home_recv.at[1, k - 1], (s, to)))
        homing[-1].start()
    gain = jnp.sum(gn_v[...] * unit[...], axis=0, keepdims=True)
    for line in range(D // 128):
        vec_v[line : line + 1, :] = gain[:, line * 128 : (line + 1) * 128]
    vec_v[D // 128 + 16 :, :] = ready[...]
    small = []
    for k in range(1, N):
        to = lax.rem(f + k, N)
        small.append(remote(vec_v, vec_far.at[k - 1], vec_sems.at[k - 1], vec_semr.at[k - 1], (s, to)))
        small[-1].start()
    second(0)
    second(1)
    vec_sum[...] = vec_v[...]
    for k in range(1, N):
        small[k - 1].wait_recv()
        copy = pltpu.make_async_copy(vec_far.at[k - 1], vec_tmp, local_sem.at[2])
        copy.start()
        copy.wait()
        vec_sum[...] += vec_tmp[...]
    for k, other in enumerate((px, py, pd)):
        small.append(remote(vec_sum, vec_near.at[k], near_sems.at[k], near_semr.at[k], (other, f)))
        small[-1].start()
    gout_out[...] = out_end()
    in_stage[0] = in_end().astype(BF16)
    last = [
        remote(in_stage.at[0, other], gin_out.at[s], last_send.at[k], last_recv.at[k], (other, f))
        for k, other in enumerate((px, py, pd))
    ]
    for copy in last:
        copy.start()
    done.append(pltpu.make_async_copy(in_stage.at[0, s], gin_out.at[s], local_sem.at[1]))
    done[2].start()
    for i in range(6):
        for way in range(2):
            then_copy(i, way).wait_recv()
            if i < 2:
                give_copy(i, way).wait_send()
            then_copy(i, way).wait_send()
    in_drain()
    out_drain()
    for copy in spread + exchange + small:
        copy.wait_send()
    for copy in last + homing:
        copy.wait()
    bias_out[s] = vec_sum[D // 128 : D // 128 + 16, :]
    for k, other in enumerate((px, py, pd)):
        small[N - 1 + k].wait_recv()
        bias_out[other] = vec_near[k, D // 128 : D // 128 + 16, :]
    small_out[...] = vec_sum[...] + vec_near[0] + vec_near[1] + vec_near[2]
    for copy in done:
        copy.wait()


def backward(S, N, to_x, to_y, from_x, from_y, keep, w_in, w_back, normed_all, qkv, mixed, gh, unit, inverse, gain_row, ready, ctx, tables):
    own, D = w_back.shape[1:]
    L = gh.shape[0]
    R = S * L
    heads = H // S
    width = heads * HD
    chips = N // 2
    dma = pltpu.SemaphoreType.DMA
    shape = jax.ShapeDtypeStruct
    vmem = pltpu.VMEM
    eighth = D // 8
    blocks = [(eighth, u.shape[1]) if i < 2 else (u.shape[0], eighth) for i, u in enumerate(keep)]
    wholes = [(2 * eighth, u.shape[1]) if i < 2 else (u.shape[0], 2 * eighth) for i, u in enumerate(keep)]
    kinds = [blocks[i] for i in (0, 2, 4)]
    in_block, out_block = (S, own, 3 * width), (own, D)
    vec = (D // 128 + 16 + ready.shape[0], 128)
    out = [
        shape(mixed.shape, BF16), shape(mixed.shape, BF16), shape(in_block, BF16), shape(out_block, F32), shape(vec, F32),
        shape((S, 16, 128), F32),
        shape((N - 1,) + vec, F32),
        shape((S, N) + in_block[1:], BF16), shape((N,) + out_block, BF16), shape((chips,) + in_block, BF16),
        shape((chips,) + out_block, BF16),
    ]
    out += [shape(w, BF16) for w in wholes[:2] * 2] + [shape(b, BF16) for b in blocks * 4]
    anywhere = pl.BlockSpec(memory_space=pl.ANY)
    in_vmem = pl.BlockSpec(memory_space=vmem)
    result = pl.pallas_call(
        functools.partial(backward_kernel, S, N, (D, own, heads)),
        out_shape=out,
        in_specs=[anywhere] * 17 + [in_vmem] * 11,
        out_specs=[anywhere] * 3 + [in_vmem] * 3 + [anywhere] * (len(out) - 6),
        scratch_shapes=[vmem((2,) + k, BF16) for k in kinds]
        + [
            vmem(w_in.shape, BF16), vmem(w_back.shape, BF16), vmem((S, L, D), BF16), vmem((S, L, D), BF16),
            vmem(qkv.shape, BF16), vmem((heads, R, HD), BF16), vmem((R, HD), F32), vmem((R, HD), F32),
            vmem((3, L, D), BF16), vmem((3, L, D), BF16), vmem((L, D), F32), vmem((N, own, 3 * width), BF16),
            vmem((width, D), BF16),
            vmem(in_block, BF16), vmem(in_block, BF16), vmem((chips,) + in_block, BF16), vmem((chips - 1,) + in_block, BF16),
            vmem(out_block, BF16), vmem(out_block, BF16), vmem((chips,) + out_block, BF16),
            vmem((chips - 1,) + out_block, BF16),
            vmem(vec, F32), vmem(vec, F32), vmem(vec, F32), vmem((3,) + vec, F32),
            vmem(mixed.shape[1:], BF16), vmem(mixed.shape, BF16),
            dma((6, 4)), dma((6, 4)), dma((3,)), dma((3,)), dma((3,)), dma((3,)), dma((3,)), dma((2, chips)),
            dma((2, chips)), dma((2, chips - 1)), dma((2, chips - 1)), dma((3,)), dma((3,)), dma((N - 1,)), dma((N - 1,)),
            dma((3,)), dma((3,)), dma((2, N - 1)), dma((2, N - 1)), dma((6 + N,)),
        ],
        compiler_params=pltpu.CompilerParams(collective_id=1, has_side_effects=True, vmem_limit_bytes=VMEM_LIMIT),
        name="backward",
    )(*to_x, *to_y, from_x, from_y, *keep, w_in, w_back, normed_all, qkv, mixed, gh, unit, inverse, gain_row, ready, ctx, *tables)
    first_x, first_y, then_y, then_x = result[11:13], result[13:15], result[15:21], result[21:27]
    grads, line = [], 0
    for i, block in enumerate(keep):
        if i < 2:
            sources = (first_x[i][:eighth], first_y[i][:eighth])
            halves = (block[:eighth], block[eighth : 2 * eighth])
        else:
            lines = slice(line, line + block.shape[0])
            sources = (from_x[lines, :eighth], from_y[lines, :eighth])
            halves = (block[:, :eighth], block[:, eighth : 2 * eighth])
            line += block.shape[0]
        sums = [
            a.astype(F32) + b.astype(F32) + c.astype(F32)
            for a, b, c in zip(halves, sources, (then_y[i], then_x[i]))
        ]
        grads.append(jnp.concatenate(sums, axis=min(i // 2, 1)))
    return grads, result[:6]


def shards(
    tokens, cotangent, ids, deal, lengths, w_qkv, b_qkv, w_out, gain_attn, gain_ffn, w_router,
    w_shared_gate, e_gate, e_up, e_down, s_gate, s_up, s_down,
):
    S, N = lax.axis_size("seq"), lax.axis_size("fsdp")
    s, f = lax.axis_index("seq"), lax.axis_index("fsdp")
    MB, T, D = tokens.shape
    E = w_router.shape[1]
    assert S == 4 and e_gate.shape[0] == 1 and E == N
    FE, FS = e_gate.shape[2], s_gate.shape[1]
    piece = T // N
    pack = T * S
    heads = H // S
    width = heads * HD
    rows = N * MB * T
    own = w_out.shape[0]

    order = jnp.stack([jnp.bitwise_xor(s, rel) * 2 + half for rel, half in ORDER])
    inverse_order = jnp.argsort(order)

    def arrange(u, by):
        return jnp.take(u.reshape(u.shape[:-1] + (8, D // 8)), by, axis=u.ndim - 1).reshape(u.shape)

    inverse_deal = jnp.argsort(deal, axis=2)

    def deal_out(u):
        u = u.reshape(MB, piece, N, D)
        u = jnp.stack([jnp.take(u[m], inverse_deal[m, f], axis=1) for m in range(MB)])
        return u.transpose(2, 0, 1, 3).reshape(N, MB * piece, D)

    index = s * N + f

    def placed(u, length):
        return lax.dynamic_update_slice(jnp.zeros((length,), F32), u.astype(F32), ((index * u.shape[0]) % 128,))

    parts = [placed(gain_attn, 128), placed(gain_ffn, 128), placed(b_qkv, 256), placed(w_shared_gate, 128)]
    for u in (w_router.reshape(-1), ids.reshape(-1)):
        parts.append(jnp.pad(u.astype(F32), (0, -u.shape[0] % 128)))
    r_line = 5
    i_line = r_line + parts[4].shape[0] // 128
    small = jnp.concatenate(parts)
    small = jnp.pad(small, (0, -small.shape[0] % 1024)).reshape(-1, 128)

    spots = ((jnp.arange(S)[:, None, None] * piece + jnp.arange(piece)[None, None, :]) * N + jnp.arange(N)[None, :, None])
    spots = jnp.broadcast_to(spots[:, :, None, :], (S, N, MB, piece)).astype(jnp.int32)
    micro = jnp.arange(MB, dtype=jnp.int32)[None, None, :, None]
    my_lengths = lengths[:, f]
    ends = jnp.cumsum(my_lengths, axis=1)
    past = ends[None, None, :, None, :] <= spots[..., None]
    start = jnp.sum(jnp.where(past, my_lengths[None, None, :, None, :], 0), axis=4)
    frequency = THETA ** (-jnp.arange(0, HD, 2, dtype=F32) / HD)
    angle = (spots - start).astype(F32).reshape(-1, 1) * frequency
    cosine, sine = jnp.cos(angle), jnp.sin(angle)
    cosine = jnp.concatenate([cosine, cosine], axis=1)
    sine = jnp.concatenate([-sine, sine], axis=1)
    place = (spots + pack * micro).reshape(-1)
    first = (start + pack * micro).reshape(-1)
    tables = (cosine, sine, first[:, None], place[:, None], place[None, :])

    wq = w_qkv.reshape(own, 3, S, width).transpose(2, 0, 1, 3).reshape(S, own, 3 * width)
    x_rows, g_all, w_in, w_back, small, normed_all, qkv, context, hidden, x_all, *fulls = forward(
        S, N, MB, deal_out(tokens), deal_out(arrange(cotangent, order)), wq, w_out, small,
        (e_gate[0], e_up[0], s_gate.T, s_up.T, e_down[0], s_down), tables,
    )
    L, R = MB * T, MB * pack

    def vector(row):
        return small[:, :, row].swapaxes(0, 1).reshape(D // 128, 128 // own, 128).sum(1).reshape(D)

    gain_1, gain_2, shared_w = vector(0), vector(1), vector(4).astype(BF16)
    router_w = small[:, :, r_line:i_line].swapaxes(0, 1).reshape(S * N, -1)[:, : own * E].reshape(D, E).astype(BF16)
    all_ids = small[:, :, i_line:].reshape(N, S, -1)[:, :, : MB * T * TOP]
    x0 = x_rows.reshape(L, D).astype(F32)
    cot = arrange(lax.dynamic_index_in_dim(g_all, f, 0, keepdims=False).reshape(L, D), inverse_order)
    g_rows = g_all.reshape(rows, D)
    all_ids = lax.dynamic_index_in_dim(all_ids, s, 1, keepdims=False).reshape(N, MB, piece, N, TOP)
    where = inverse_deal.transpose(2, 1, 0)
    chosen = jnp.take_along_axis(
        all_ids[None], where[:, :, :, None, None, None], axis=4
    ).reshape(N, L, TOP).astype(jnp.int32)
    own_ids = lax.dynamic_index_in_dim(chosen, f, 0, keepdims=False)
    chosen = chosen.reshape(rows, TOP)
    x = x_all.reshape(rows, D)
    x_own = lax.dynamic_index_in_dim(x_all, f, 0, keepdims=False)
    unit_1, inverse_1 = rms_forward(x0)
    unit_2, inverse_2 = rms_forward(hidden)

    lead = jnp.concatenate([router_w, shared_w[:, None]], axis=1)
    lead_order = jnp.take(lead.reshape(8, D // 8, E + 1), order, axis=0).reshape(D, E + 1)
    picked_rows = jnp.any(chosen == f, axis=1, keepdims=True).astype(F32)
    y, dx, geo, gso, grad_gate, grad_up, grad_sgate, grad_sup, act, sact = experts(
        N, E, x, g_rows, picked_rows, jnp.pad(lead_order, ((0, 0), (0, 127 - E))), fulls
    )
    dx = lax.psum_scatter(dx, "fsdp", scatter_dimension=0, tiled=True)

    half = D // 8
    cuts = (slice(4 * half, 6 * half), slice(6 * half, 8 * half), slice(0, 4 * half))

    def by_columns(cut):
        return (
            dot_t(grad_sgate, x[:, cut]).astype(BF16), dot_t(grad_sup, x[:, cut]).astype(BF16),
            dot_t(act, geo[:, cut]).astype(BF16), dot_t(sact, gso[:, cut]).astype(BF16),
        )

    def by_rows(cut):
        return dot_t(x[:, cut], grad_gate).astype(BF16), dot_t(x[:, cut], grad_up).astype(BF16)

    by_x, by_y = jnp.concatenate(by_columns(cuts[0])), jnp.concatenate(by_columns(cuts[1]))
    x, y, by_x, by_y = lax.optimization_barrier((x, y, by_x, by_y))
    y = lax.psum_scatter(y, "fsdp", scatter_dimension=0, tiled=True)
    from_x, from_y = across(by_x, 1), across(by_y, 2)
    to_x, to_y = by_rows(cuts[0]), by_rows(cuts[1])
    keep = by_rows(cuts[2]) + by_columns(cuts[2])
    dx, from_x, from_y, to_x, to_y, keep = lax.optimization_barrier((dx, from_x, from_y, to_x, to_y, keep))
    dx = dx.astype(F32)

    mixed = (hidden + arrange(y, inverse_order).astype(F32)).astype(BF16)
    base = D
    gg_own = sum(dx[:, base + i * N : base + (i + 1) * N] for i in range(3))
    gs_own = jnp.sum(dx[:, base + 3 * N : base + 6 * N], axis=1)
    grad_normed2 = arrange(dx[:, :D], inverse_order)
    flat2 = arrange(x_own, inverse_order)
    logits = dot(x_own, lead_order)
    shifted = jnp.exp(logits[:, :E] - jnp.max(logits[:, :E], axis=-1, keepdims=True))
    router = shifted / jnp.sum(shifted, axis=-1, keepdims=True)
    sigma = jax.nn.sigmoid(logits[:, E])
    picked = jnp.any(own_ids[:, :, None] == jnp.arange(E)[None, None, :], axis=1)
    grad_router = jnp.where(picked, gg_own, 0.0)
    grad_logits = (router * (grad_router - jnp.sum(router * grad_router, axis=-1, keepdims=True))).astype(BF16)
    grad_sigma = gs_own * sigma * (1.0 - sigma)
    grad_normed2 = grad_normed2 + dot_nt(grad_logits, router_w) + grad_sigma[:, None] * shared_w.astype(F32)[None, :]
    g_router = dot_t(flat2, grad_logits)
    g_shared = jnp.sum(grad_sigma[:, None] * flat2.astype(F32), axis=0)
    from_norm, g_gain_2 = rms_backward(grad_normed2, unit_2, inverse_2, gain_2)
    grad_hidden = cot.astype(F32) + from_norm

    ready = jnp.concatenate([g_gain_2, g_shared, g_router.reshape(-1)]).reshape(-1, 128)
    expert_grads, (mixed, grad_x, g_in, g_out, small, g_bias) = backward(
        S, N, to_x, to_y, from_x, from_y, keep, w_in, w_back, normed_all, qkv, mixed.reshape(N, MB * piece, D), grad_hidden, unit_1,
        inverse_1, gain_1[None], ready, context, tables,
    )
    def take_home(u):
        u = u.reshape(N, MB, piece, D)
        return jnp.stack([jnp.take(u[:, m], deal[m, f], axis=0).swapaxes(0, 1) for m in range(MB)]).reshape(MB, T, D)

    mixed, grad_tokens = take_home(mixed), take_home(grad_x).astype(F32)

    g_in = g_in.reshape(S, own, 3, width).transpose(1, 2, 0, 3).reshape(own, 3 * D).astype(F32)
    g_bias = g_bias[:, : 3 * heads].reshape(S, 3, width).swapaxes(0, 1).reshape(-1)

    def mine(u):
        return lax.dynamic_slice_in_dim(u, index * (u.shape[0] // (S * N)), u.shape[0] // (S * N))

    small = small.reshape(-1)
    after = D + 16 * 128
    g_gain_1, g_gain_2, g_shared = mine(small[:D]), mine(small[after : after + D]), mine(small[after + D : after + 2 * D])
    g_router = mine(small[after + 2 * D :]).reshape(own, E)
    return (
        mixed, grad_tokens, g_in, mine(g_bias), g_out, g_gain_1, g_gain_2, g_router, g_shared,
        expert_grads[0][None], expert_grads[1][None], expert_grads[4][None], expert_grads[2].T, expert_grads[3].T, expert_grads[5],
    )


def solution(mesh):
    both = ("seq", "fsdp")
    in_specs = (
        P(None, both, None), P(None, both, None), P(None, both, None), P(), P(), P(both, None), P(both), P(both, None),
        P(both), P(both), P(both, None), P(both), P("fsdp", "seq", None), P("fsdp", "seq", None),
        P("fsdp", None, "seq"), P("seq", "fsdp"), P("seq", "fsdp"), P("fsdp", "seq"),
    )
    out_specs = (
        P(None, both, None), P(None, both, None), P(both, None), P(both), P(both, None), P(both), P(both),
        P(both, None), P(both), P("fsdp", "seq", None), P("fsdp", "seq", None), P("fsdp", None, "seq"),
        P("seq", "fsdp"), P("seq", "fsdp"), P("fsdp", "seq"),
    )
    return jax.shard_map(shards, mesh=mesh, in_specs=in_specs, out_specs=out_specs, check_vma=False)
```

```python
import functools

import jax
import jax.numpy as jnp
from jax import lax
from jax.experimental import pallas as pl
from jax.experimental.pallas import tpu as pltpu
from jax.sharding import PartitionSpec as P

H = 16
HD = 128
TOP = 4
EPS = 1e-06
THETA = 1000000.0
MASKED = -1e30
F32 = jnp.float32
BF16 = jnp.bfloat16
MESH = pl.DeviceIdType.MESH
VMEM_LIMIT = 61 * 2**20

ORDER = ((0, 0), (0, 1), (2, 0), (1, 1), (1, 0), (3, 0), (2, 1), (3, 1))


def dot(a, b):
    return jnp.dot(a, b, preferred_element_type=F32)


def dot_t(a, b):
    return lax.dot_general(a, b, (((0,), (0,)), ((), ())), preferred_element_type=F32)


def dot_nt(a, b):
    return lax.dot_general(a, b, (((1,), (1,)), ((), ())), preferred_element_type=F32)


def turn(u):
    half = u.shape[-1] // 2
    return jnp.concatenate([-u[..., half:], u[..., :half]], axis=-1)


def turn_back(u):
    half = u.shape[-1] // 2
    return jnp.concatenate([u[..., half:], -u[..., :half]], axis=-1)


def rms_forward(values):
    inverse = lax.rsqrt(jnp.mean(values * values, axis=-1, keepdims=True) + EPS)
    return values * inverse, inverse


def rms_backward(grad, unit, inverse, gain):
    scaled = grad * gain
    grad_gain = jnp.sum(grad * unit, axis=tuple(range(grad.ndim - 1)))
    return inverse * (scaled - unit * jnp.mean(scaled * unit, axis=-1, keepdims=True)), grad_gain


def across(a, which):
    return lax.ppermute(a, "seq", [(i, i ^ which) for i in range(4)])


def split3(v):
    hi = lax.reduce_precision(v, 8, 7)
    mid = lax.reduce_precision(v - hi, 8, 7)
    low = lax.reduce_precision(v - hi - mid, 8, 7)
    return hi, mid, low


def swiglu_back(grad_act, gate, up):
    sig = jax.nn.sigmoid(gate)
    grad_gate = (grad_act * up * sig * (1.0 + gate * (1.0 - sig))).astype(BF16)
    grad_up = (grad_act * gate * sig).astype(BF16)
    return grad_gate, grad_up


def partners(s):
    return s + 1 - 2 * lax.rem(s, 2), lax.rem(s + 2, 4), 3 - s


def greet(s, f, S, N):
    barrier = pltpu.get_barrier_semaphore()
    for other in partners(s):
        pl.semaphore_signal(barrier, inc=1, device_id=(other, f), device_id_type=MESH)
    for step in range(1, N):
        pl.semaphore_signal(barrier, inc=1, device_id=(s, lax.rem(f + step, N)), device_id_type=MESH)
    pl.semaphore_wait(barrier, S - 1 + N - 1)


class Line:
    def __init__(self, s, f, N, block, move_send, move_recv, side_send, side_recv):
        self.s, self.chip, self.core, self.n = s, f // 2, lax.rem(f, 2), N // 2
        self.block = block
        self.move_send, self.move_recv = move_send, move_recv
        self.side_send, self.side_recv = side_send, side_recv

    def move(self, way, step, origin, to):
        ref = self.block(2 * origin + self.core)
        return pltpu.make_async_remote_copy(
            ref, ref, self.move_send.at[way, step], self.move_recv.at[way, step],
            device_id=(self.s, 2 * to + self.core), device_id_type=MESH,
        )

    def side(self, origin, core):
        ref = self.block(2 * origin + core)
        return pltpu.make_async_remote_copy(
            ref, ref, self.side_send.at[origin], self.side_recv.at[origin],
            device_id=(self.s, 2 * self.chip + 1 - self.core), device_id_type=MESH,
        )

    def send(self, step, act):
        q, n = self.chip, self.n

        @pl.when((q - step >= 0) & (q + 1 < n))
        def _():
            act(self.move(0, step, jnp.maximum(q - step, 0), jnp.minimum(q + 1, n - 1)))

        @pl.when((q + step < n) & (q >= 1))
        def _():
            act(self.move(1, step, jnp.minimum(q + step, n - 1), jnp.maximum(q - 1, 0)))

    def begin(self):
        self.send(0, lambda copy: copy.start())
        self.side(self.chip, self.core).start()

    def step(self, step):
        q, n = self.chip, self.n

        @pl.when(q - 1 - step >= 0)
        def _():
            origin = jnp.maximum(q - 1 - step, 0)
            self.move(0, step, origin, jnp.maximum(q - 1, 0)).wait_recv()
            if step + 1 < n - 1:

                @pl.when(q + 1 < n)
                def _():
                    self.move(0, step + 1, origin, jnp.minimum(q + 1, n - 1)).start()

            self.side(origin, self.core).start()

        @pl.when(q + 1 + step < n)
        def _():
            origin = jnp.minimum(q + 1 + step, n - 1)
            self.move(1, step, origin, jnp.minimum(q + 1, n - 1)).wait_recv()
            if step + 1 < n - 1:

                @pl.when(q >= 1)
                def _():
                    self.move(1, step + 1, origin, jnp.maximum(q - 1, 0)).start()

            self.side(origin, self.core).start()

    def arrive(self):
        for origin in range(self.n):
            self.side(origin, 1 - self.core).wait_recv()

    def drain(self):
        for step in range(self.n - 1):
            self.send(step, lambda copy: copy.wait_send())
        for origin in range(self.n):
            self.side(origin, self.core).wait_send()


PLACE = {key: i for i, key in enumerate(ORDER)}


def gather_vector(small, row, length, own, N):
    per = 128 // own
    for block in range(length // 128):
        total = None
        for i in range(block * per, (block + 1) * per):
            part = small[i % N, i // N, row : row + 1, :]
            total = part if total is None else total + part
        yield block, total


def forward_kernel(S, N, sizes, *refs):
    MB, piece, D, own, heads = sizes
    tok, cot, wq, wo, small, *refs = refs
    shards_in, refs = refs[:6], refs[6:]
    cos, sin, first, place, place_row, *refs = refs
    x_rows, g_all, w_in, w_back, small_all, normed_out, qkv_out, ctx_out, hid_out, x_all, *refs = refs
    fulls, refs = refs[:6], refs[6:]
    cot_by, shard_by, refs = refs[0], refs[1:7], refs[7:]
    small_v, tok_v, w_v, wb_v, x_v, gain_v, bias_v, na_v, qkv_v, ctx_v, part_send, part_recv, hid_v, n2_v, xo_v, *refs = refs
    (local_sem, deal_send, deal_recv, seq_send, seq_recv, small_send, small_recv, half_send, half_recv, part_sems,
     part_semr, norm_sems, norm_semr, out_sem, *line_sems) = refs
    s, f = lax.axis_index("seq"), lax.axis_index("fsdp")
    px, py, pd = partners(s)
    eighth = D // 8
    pr = MB * piece
    L = pr * N
    R = S * L
    width = heads * HD

    def spot(full, i, where):
        cut = pl.ds(where * eighth, eighth)
        return full.at[cut] if i < 2 else full.at[:, cut]

    def own_half(shard, i, half):
        cut = pl.ds(half * eighth, eighth)
        return shard.at[cut] if i < 2 else shard.at[:, cut]

    def remote(src, dst, send, recv, device):
        return pltpu.make_async_remote_copy(src, dst, send, recv, device_id=device, device_id_type=MESH)

    pairs = [
        (small, small_v.at[f, s]), (wq.at[s], w_v.at[s, f]), (wo, wb_v.at[f]), (tok.at[f], tok_v.at[f]), (cot.at[f], cot_by),
    ] + list(zip(shards_in, shard_by))
    take = [pltpu.make_async_copy(a, b, local_sem.at[i]) for i, (a, b) in enumerate(pairs)]
    put = [pltpu.make_async_copy(cot_by, g_all.at[f, f], local_sem.at[4])]
    for i in range(6):
        cut = pl.ds(0, 2 * eighth)
        target = fulls[i].at[cut] if i < 2 else fulls[i].at[:, cut]
        put.append(pltpu.make_async_copy(shard_by[i], target, local_sem.at[5 + i]))
    for copy in take:
        copy.start()
    greet(s, f, S, N)

    over_seq = []
    for k, other in enumerate((px, py, pd)):
        over_seq.append(remote(small, small_v.at[f, s], seq_send.at[0, k], seq_recv.at[0, k], (other, f)))
        over_seq.append(remote(wq.at[other], w_v.at[s, f], seq_send.at[1, k], seq_recv.at[1, k], (other, f)))
    for copy in over_seq:
        copy.start()
    deal_tok, deal_cot, to_all = [], [], []
    for k in range(1, N):
        to = lax.rem(f + k, N)
        deal_tok.append(remote(tok.at[to], tok_v.at[f], deal_send.at[0, k - 1], deal_recv.at[0, k - 1], (s, to)))
        deal_cot.append(remote(cot.at[to], g_all.at[to, f], deal_send.at[1, k - 1], deal_recv.at[1, k - 1], (s, to)))
        to_all.append(remote(small_v.at[f], small_v.at[f], small_send.at[k - 1], small_recv.at[k - 1], (s, to)))
    for copy in deal_tok:
        copy.start()

    def half_copy(i, k):
        where, rel, half = ((px, 1, 0), (py, 2, 1), (py, 2, 0), (px, 1, 1))[k]
        return remote(
            own_half(shards_in[i], i, half), spot(fulls[i], i, PLACE[rel, half]), half_send.at[i, k], half_recv.at[i, k],
            (where, f),
        )

    def pass_copy(i, k):
        where, rel, half = ((py, 1, 0), (px, 2, 1))[k]
        return remote(
            spot(fulls[i], i, PLACE[rel, half]), spot(fulls[i], i, PLACE[3, half]), half_send.at[i, 4 + k],
            half_recv.at[i, 4 + k], (where, f),
        )

    def give(i):
        for k in range(4):
            half_copy(i, k).start()

    def pass_on(i):
        for k in range(2):
            half_copy(i, k).wait_recv()
            pass_copy(i, k).start()

    give(0)
    for copy in take:
        copy.wait()
    for copy in put:
        copy.start()
    for copy in over_seq:
        copy.wait_recv()
    for copy in to_all:
        copy.start()
    w_line = Line(s, f, N, lambda j: w_v.at[:, j], *line_sems[0:4])
    b_line = Line(s, f, N, lambda j: wb_v.at[j], *line_sems[4:8])
    g_line = Line(s, f, N, lambda j: g_all.at[j], *line_sems[8:12])
    x_line = Line(s, f, N, lambda j: x_all.at[j], *line_sems[12:16])
    w_line.begin()
    b_line.begin()

    for copy in deal_tok + to_all:
        copy.wait_recv()
    for row in range(2):
        for block, part in gather_vector(small_v, row, D, own, N):
            gain_v[row : row + 1, block * 128 : (block + 1) * 128] = part
    nb = 3 * own
    for line in range(3 * D // 128):
        total = None
        for i in range(S * N):
            for half in range(2):
                if (i * nb) // 128 + half == line and (half == 0 or (i * nb) % 128 + nb > 128):
                    part = small_v[i % N, i // N, 2 + half : 3 + half, :]
                    total = part if total is None else total + part
        bias_v[line : line + 1, :] = total
    for j in range(N):
        x_v[j * pr : (j + 1) * pr, :] = tok_v[j].astype(F32)
    x = x_v[...]
    inverse = lax.rsqrt(jnp.mean(x * x, axis=-1, keepdims=True) + EPS)
    na_v[s] = (x * inverse * gain_v[0:1, :]).astype(BF16)
    spread = [
        remote(na_v.at[s], na_v.at[s], norm_sems.at[k], norm_semr.at[k], (other, f)) for k, other in enumerate((px, py, pd))
    ]
    for copy in spread:
        copy.start()
    for copy in deal_cot:
        copy.start()
    give(1)
    chips = N // 2
    for step in range(chips - 1):
        w_line.step(step)
        b_line.step(step)
        if step == 0:
            give(4)
        if step == 1:
            pass_on(0)
    pass_on(1)
    give(2)
    for copy in deal_cot:
        copy.wait_recv()
    for copy in put:
        copy.wait()
    g_line.begin()
    w_line.arrive()
    b_line.arrive()
    for copy in spread:
        copy.wait_recv()

    for t in range(3):

        def project(pair, carry, t=t):
            column = pl.multiple_of(t * width + pair * 2 * HD, 2 * HD)
            w = w_v[:, :, :, pl.ds(column, 2 * HD)].reshape(D, 2 * HD)
            out = dot(na_v[...].reshape(R, D), w)
            for k in range(2):
                u = out[:, k * HD : (k + 1) * HD]
                u = u + bias_v[pl.ds(t * (D // 128) + s * heads + 2 * pair + k, 1), :]
                if t < 2:
                    u = u * cos[...] + pltpu.roll(u, HD // 2, 1) * sin[...]
                qkv_v[t * heads + 2 * pair + k] = u.astype(BF16)
            return carry

        lax.fori_loop(0, heads // 2, project, 0)
    g_line.step(0)

    def attend(h, carry):
        rows = R // 4
        for block in range(4):
            cut = pl.ds(block * rows, rows)
            raw = dot_nt(qkv_v[h, cut, :], qkv_v[heads + h])
            ok = (first[cut, :] <= place_row[...]) & (place_row[...] <= place[cut, :])
            scores = jnp.where(ok, raw * HD**-0.5, MASKED)
            weights = jnp.exp(scores - jnp.max(scores, axis=-1, keepdims=True))
            chance = (weights / jnp.sum(weights, axis=-1, keepdims=True)).astype(BF16)
            ctx_v[cut, pl.ds(pl.multiple_of(h * HD, HD), HD)] = dot(chance, qkv_v[2 * heads + h]).astype(BF16)
        return carry

    lax.fori_loop(0, heads, attend, 0)
    for step in range(1, chips - 1):
        g_line.step(step)
        if step == 1:
            give(3)
            give(5)

    wb = wb_v[...].reshape(width, D)
    exchange = []
    for k, other in enumerate((px, py, pd)):
        rows = pl.ds(pl.multiple_of(other * L, L), L)
        part_send[k] = dot(ctx_v[rows, :], wb).astype(BF16)
        exchange.append(remote(part_send.at[k], part_recv.at[k], part_sems.at[k], part_semr.at[k], (other, f)))
        exchange[-1].start()
    pass_on(4)
    hid_v[...] = x_v[...] + dot(ctx_v[pl.ds(pl.multiple_of(s * L, L), L), :], wb)
    outs = [
        (tok_v, x_rows), (w_v, w_in), (wb_v, w_back), (small_v, small_all), (na_v, normed_out), (qkv_v, qkv_out),
        (ctx_v, ctx_out), (hid_v, hid_out), (xo_v, x_all.at[f]),
    ]
    outs = [pltpu.make_async_copy(a, b, out_sem.at[i]) for i, (a, b) in enumerate(outs)]
    for k in range(3):
        exchange[k].wait_recv()
        hid_v[...] += part_recv[k].astype(F32)
    hidden = hid_v[...]
    inverse = lax.rsqrt(jnp.mean(hidden * hidden, axis=-1, keepdims=True) + EPS)
    n2_v[...] = (hidden * inverse * gain_v[1:2, :]).astype(BF16)
    owners = (s, px, py, pd)
    for i, (rel, half) in enumerate(ORDER):
        column = pl.multiple_of((owners[rel] * 2 + half) * eighth, eighth)
        xo_v[:, i * eighth : (i + 1) * eighth] = n2_v[:, pl.ds(column, eighth)]
    outs[8].start()
    outs[8].wait()
    x_line.begin()
    pass_on(2)
    for step in range(chips - 1):
        x_line.step(step)
    pass_on(3)
    pass_on(5)
    for line in (w_line, b_line):
        line.drain()
    for copy in over_seq + to_all + spread:
        copy.wait_send()
    for copy in outs[:8]:
        copy.start()
    for i in range(6):
        for k in range(2, 4):
            half_copy(i, k).wait_recv()
        for k in range(2):
            pass_copy(i, k).wait_recv()
    for i in range(6):
        for k in range(4):
            half_copy(i, k).wait_send()
        for k in range(2):
            pass_copy(i, k).wait_send()
    for line in (g_line, x_line):
        line.arrive()
        line.drain()
    for copy in deal_tok + deal_cot + exchange:
        copy.wait_send()
    for copy in outs[:8]:
        copy.wait()


def forward(S, N, MB, tok, cot, wq, wo, small, shards_in, tables):
    own, D = wo.shape
    pr = tok.shape[1]
    L = pr * N
    R = S * L
    heads = H // S
    width = heads * HD
    chips = N // 2
    dma = pltpu.SemaphoreType.DMA
    line = [dma((2, chips - 1)), dma((2, chips - 1)), dma((chips,)), dma((chips,))]
    shape = jax.ShapeDtypeStruct
    w_shape, wb_shape, small_shape = (S, N) + wq.shape[1:], (N,) + wo.shape, (N, S) + small.shape
    out = [
        shape(tok.shape, BF16), shape((N,) + cot.shape, BF16), shape(w_shape, BF16), shape(wb_shape, BF16),
        shape(small_shape, F32), shape((S, L, D), BF16), shape((3 * heads, R, HD), BF16), shape((R, width), BF16),
        shape((L, D), F32), shape((N, L, D), BF16),
    ]
    for i, shard in enumerate(shards_in):
        rows, columns = shard.shape
        out.append(shape((4 * rows, columns) if i < 2 else (rows, 4 * columns), BF16))
    anywhere = pl.BlockSpec(memory_space=pl.ANY)
    in_vmem = pl.BlockSpec(memory_space=pltpu.VMEM)
    vmem = pltpu.VMEM
    return pl.pallas_call(
        functools.partial(forward_kernel, S, N, (MB, pr // MB, D, own, heads)),
        out_shape=out,
        in_specs=[anywhere] * 11 + [in_vmem] * 5,
        out_specs=[anywhere] * 16,
        scratch_shapes=[vmem(u.shape, u.dtype) for u in (cot[0], *shards_in)]
        + [
            vmem(small_shape, F32), vmem(tok.shape, BF16), vmem(w_shape, BF16), vmem(wb_shape, BF16), vmem((L, D), F32),
            vmem((8, D), F32), vmem((3 * D // 128, 128), F32), vmem((S, L, D), BF16), vmem((3 * heads, R, HD), BF16),
            vmem((R, width), BF16), vmem((3, L, D), BF16), vmem((3, L, D), BF16), vmem((L, D), F32), vmem((L, D), BF16),
            vmem((L, D), BF16),
            dma((11,)), dma((2, N - 1)), dma((2, N - 1)), dma((2, 3)), dma((2, 3)), dma((N - 1,)), dma((N - 1,)),
            dma((6, 6)), dma((6, 6)), dma((3,)), dma((3,)), dma((3,)), dma((3,)), dma((9,)),
        ] + line * 4,
        compiler_params=pltpu.CompilerParams(collective_id=0, has_side_effects=True, vmem_limit_bytes=VMEM_LIMIT),
        name="forward",
    )(tok, cot, wq, wo, small, *shards_in, *tables)


def hold(weights, held, sems, order):
    copies = [pltpu.make_async_copy(a, b, sems.at[i]) for i, (a, b) in enumerate(zip(weights, held))]
    opening = pl.program_id(0) == 0

    @pl.when(opening)
    def _():
        for i in order:
            copies[i].start()

    def need(i):
        @pl.when(opening)
        def _():
            copies[i].wait()

    return need


def experts_forward_kernel(N, E, *refs):
    x, g, picked, lead, *refs = refs
    weights, refs = refs[:6], refs[6:]
    y, notes, geo, gso, gate_o, up_o, sgate_o, sup_o, act, sact, *refs = refs
    eg, eu, sg, su, ed, sd = refs[:6]
    need = hold(weights, refs[:6], refs[6], (0, 1, 4, 2, 3, 5))
    f = lax.axis_index("fsdp")
    rows = x[...]
    logits = dot(rows, lead[...])
    lane = lax.broadcasted_iota(jnp.int32, logits.shape, 1)
    scores = jnp.where(lane < E, logits, MASKED)
    shifted = jnp.exp(scores - jnp.max(scores, axis=-1, keepdims=True))
    share = jnp.sum(jnp.where(lane == f, shifted, 0.0), axis=-1, keepdims=True)
    share = share / jnp.sum(jnp.where(lane < E, shifted, 0.0), axis=-1, keepdims=True)
    gate_f = jnp.where(picked[...] > 0.5, share, 0.0)
    sigma = jax.nn.sigmoid(jnp.sum(jnp.where(lane == E, logits, 0.0), axis=-1, keepdims=True))
    geo[...] = (gate_f * g[...].astype(F32)).astype(BF16)
    gso[...] = (sigma * g[...].astype(F32)).astype(BF16)
    need(0)
    gate = dot(rows, eg[...])
    gate_o[...] = gate
    need(1)
    up = dot(rows, eu[...])
    up_o[...] = up
    act[...] = (gate * jax.nn.sigmoid(gate) * up).astype(BF16)
    need(4)
    out = dot(act[...], ed[...]).astype(BF16).astype(F32)
    note_e = jnp.sum(out * g[...].astype(F32), axis=-1, keepdims=True)
    out = gate_f * out
    need(2)
    gate = dot_nt(rows, sg[...])
    sgate_o[...] = gate
    need(3)
    up = dot_nt(rows, su[...])
    sup_o[...] = up
    sact[...] = (gate * jax.nn.sigmoid(gate) * up).astype(BF16)
    need(5)
    out_s = dot(sact[...], sd[...])
    note_s = jnp.sum(out_s * g[...].astype(F32), axis=-1, keepdims=True)
    y[...] = (out + sigma * out_s).astype(BF16)
    lane = lax.broadcasted_iota(jnp.int32, notes.shape, 1)
    total = jnp.zeros(notes.shape, F32)
    i = 0
    for value in (note_e, note_s):
        for _ in range(3):
            part = value.astype(BF16).astype(F32)
            total = jnp.where(lane == i * N + f, part, total)
            value = value - part
            i += 1
    notes[...] = total.astype(BF16)


def experts_backward_kernel(*refs):
    notes, geo, gso, gate_i, up_i, sgate_i, sup_i, *refs = refs
    weights, refs = refs[:6], refs[6:]
    dx, grad_gate, grad_up, grad_sgate, grad_sup, *refs = refs
    eg, eu, sg, su, ed, sd = refs[:6]
    need = hold(weights, refs[:6], refs[6], (4, 0, 1, 5, 2, 3))
    D = geo.shape[1]

    def local(grad_act, gate, up, gate_grad, up_grad):
        sig = jax.nn.sigmoid(gate[...])
        gate_grad[...] = (grad_act * up[...] * sig * (1.0 + gate[...] * (1.0 - sig))).astype(BF16)
        up_grad[...] = (grad_act * gate[...] * sig).astype(BF16)

    need(4)
    local(dot_nt(geo[...], ed[...]), gate_i, up_i, grad_gate, grad_up)
    need(0)
    need(1)
    back = (dot_nt(grad_gate[...], eg[...]) + dot_nt(grad_up[...], eu[...])).astype(BF16)
    need(5)
    local(dot_nt(gso[...], sd[...]), sgate_i, sup_i, grad_sgate, grad_sup)
    need(2)
    need(3)
    back = back.astype(F32) + dot(grad_sgate[...], sg[...]) + dot(grad_sup[...], su[...])
    dx[:, :D] = back.astype(BF16)
    dx[:, D:] = notes[...]


def experts_call(kernel, name, arrays, whole, weights, outs, products):
    rows = arrays[0].shape[0]
    tile = 256
    units = weights[0].shape[1] + weights[2].shape[0]
    return pl.pallas_call(
        kernel,
        grid=(rows // tile,),
        out_shape=[jax.ShapeDtypeStruct((rows, c), t) for c, t in outs],
        in_specs=[pl.BlockSpec((tile, u.shape[1]), lambda i: (i, 0)) for u in arrays]
        + [pl.BlockSpec(u.shape, lambda i: (0, 0), pipeline_mode=pl.Buffered(1)) for u in whole]
        + [pl.BlockSpec(memory_space=pl.ANY)] * 6,
        out_specs=[pl.BlockSpec((tile, c), lambda i: (i, 0)) for c, _ in outs],
        scratch_shapes=[pltpu.VMEM(w.shape, BF16) for w in weights] + [pltpu.SemaphoreType.DMA((6,))],
        compiler_params=pltpu.CompilerParams(dimension_semantics=("arbitrary",), vmem_limit_bytes=VMEM_LIMIT),
        cost_estimate=pl.CostEstimate(
            flops=2 * products * rows * arrays[1].shape[1] * units, bytes_accessed=16 * rows * (units + 2048),
            transcendentals=rows * units,
        ),
        name=name,
    )(*arrays, *whole, *weights)


def experts_forward(N, E, x, g, picked, lead, weights):
    D, FE, FS = x.shape[1], weights[0].shape[1], weights[2].shape[0]
    outs = [(D, BF16), (6 * N + -(6 * N) % 128, BF16), (D, BF16), (D, BF16)]
    outs += [(c, F32) for c in (FE, FE, FS, FS)] + [(FE, BF16), (FS, BF16)]
    kernel = functools.partial(experts_forward_kernel, N, E)
    return experts_call(kernel, "experts_forward", (x, g, picked), (lead,), weights, outs, 3)


def experts_backward(arrays, weights):
    D, FE, FS = arrays[1].shape[1], weights[0].shape[1], weights[2].shape[0]
    outs = [(c, BF16) for c in (D + arrays[0].shape[1], FE, FE, FS, FS)]
    return experts_call(experts_backward_kernel, "experts_backward", arrays, (), weights, outs, 3)


def backward_kernel(S, N, sizes, *refs):
    D, own, heads = sizes
    to_x, to_y, stacked_x, stacked_y, keep, refs = refs[:2], refs[2:4], refs[4], refs[5], refs[6:12], refs[12:]
    from_x, from_y, line = [], [], 0
    for ref in keep[2:]:
        from_x.append(stacked_x.at[pl.ds(line, ref.shape[0])])
        from_y.append(stacked_y.at[pl.ds(line, ref.shape[0])])
        line += ref.shape[0]
    w_in, w_back, normed_all, qkv, mixed, gh, unit, inverse, gain_row, ready, ctx, cos, sin, first, place, place_row, *refs = refs
    mixed_out, gx_out, gin_out, gout_out, small_out, bias_out, vec_far, gin_buf, gout_buf, gin_pair, gout_pair, *refs = refs
    from_x, from_y, refs = (*refs[:2], *from_x), (*refs[2:4], *from_y), refs[4:]
    then_y, then_x, pair_y, pair_x, refs = refs[:6], refs[6:12], refs[12:18], refs[18:24], refs[24:]
    loads, refs = refs[:3], refs[3:]
    w_v, wb_v, ga_v, na_v, qkv_v, gc_v, gk_v, gv_v, part_send, part_recv, gn_v, gi_v, go_v, *refs = refs
    in_mine, in_pair, in_stage, in_far, out_mine, out_pair, out_stage, out_far, *refs = refs
    vec_v, vec_tmp, vec_sum, vec_near, mixed_v, gx_v, *refs = refs
    (step_send, step_recv, load_sem, ga_send, ga_recv, part_sems, part_semr, pair_send, pair_recv, far_send, far_recv,
     last_send, last_recv, vec_sems, vec_semr, near_sems, near_semr, home_send, home_recv, local_sem) = refs
    s, f = lax.axis_index("seq"), lax.axis_index("fsdp")
    px, py, pd = partners(s)
    chip, core, chips = f // 2, lax.rem(f, 2), N // 2
    eighth = D // 8
    L = gh.shape[0]
    R = S * L
    width = heads * HD
    pr = L // N
    kind = (0, 0, 1, 1, 2, 1)

    def remote(src, dst, send, recv, device):
        return pltpu.make_async_remote_copy(src, dst, send, recv, device_id=device, device_id_type=MESH)

    def part(ref, i, k):
        cut = pl.ds(k * eighth, eighth)
        return ref.at[cut] if i < 2 else ref.at[:, cut]

    def give_copy(i, way):
        a, b, to = ((to_x, from_x, px), (to_y, from_y, py))[way]
        return remote(a[i], b[i], step_send.at[i, way], step_recv.at[i, way], (to, f))

    def then_copy(i, way):
        a, b, to = ((pair_y, then_y, py), (pair_x, then_x, px))[way]
        return remote(a[i], b[i], step_send.at[i, 2 + way], step_recv.at[i, 2 + way], (to, f))

    def give(i):
        for way in range(2):
            give_copy(i, way).start()

    def fetch(i, sources):
        copies = [pltpu.make_async_copy(u, loads[kind[i]].at[k], load_sem.at[k]) for k, u in enumerate(sources)]
        for copy in copies:
            copy.start()
        for copy in copies:
            copy.wait()

    def second(i):
        buf = loads[kind[i]]
        for way, (place_in_keep, arrived) in enumerate(((2, from_x[i]), (3, from_y[i]))):
            if i < 2:
                give_copy(i, way).wait_recv()
            fetch(i, (part(keep[i], i, place_in_keep), part(arrived, i, 1)))
            buf[0] = (buf[0].astype(F32) + buf[1].astype(F32)).astype(BF16)
            copy = pltpu.make_async_copy(buf.at[0], (pair_y, pair_x)[way][i], load_sem.at[0])
            copy.start()
            copy.wait()
            then_copy(i, way).start()

    def reducer(block, pair, mine, other, stage, far, k):
        def pair_copy(q):
            return remote(block(2 * q + 1 - core), pair.at[q], pair_send.at[k, q], pair_recv.at[k, q], (s, 2 * chip + 1 - core))

        def far_copy(d):
            to = lax.rem(chip + d, chips)
            return remote(stage.at[d], far.at[d - 1], far_send.at[k, d - 1], far_recv.at[k, d - 1], (s, 2 * to + core))

        def begin():
            for q in range(chips):
                pair_copy(q).start()

        def middle():
            for q in range(chips):
                pair_copy(q).wait_recv()
            for d in range(1, chips + 1):
                d = d % chips
                q = lax.rem(chip + d, chips)
                copies = (
                    pltpu.make_async_copy(block(2 * q + core), mine, load_sem.at[0]),
                    pltpu.make_async_copy(pair.at[q], other, load_sem.at[1]),
                )
                for copy in copies:
                    copy.start()
                for copy in copies:
                    copy.wait()
                stage[d] = (mine[...].astype(F32) + other[...].astype(F32)).astype(BF16)
                if d:
                    far_copy(d).start()

        def end():
            total = stage[0].astype(F32)
            for d in range(1, chips):
                far_copy(d).wait_recv()
                total = total + far[d - 1].astype(F32)
            return total

        def drain():
            for q in range(chips):
                pair_copy(q).wait_send()
            for d in range(1, chips):
                far_copy(d).wait_send()

        return begin, middle, end, drain

    in_begin, in_middle, in_end, in_drain = reducer(
        lambda j: gin_buf.at[:, j], gin_pair, in_mine, in_pair, in_stage, in_far, 0)
    out_begin, out_middle, out_end, out_drain = reducer(
        lambda j: gout_buf.at[j], gout_pair, out_mine, out_pair, out_stage, out_far, 1)

    begin = [
        pltpu.make_async_copy(w_back, wb_v, local_sem.at[0]), pltpu.make_async_copy(w_in, w_v, local_sem.at[1]),
        pltpu.make_async_copy(qkv, qkv_v, local_sem.at[2]), pltpu.make_async_copy(normed_all, na_v, local_sem.at[3]),
        pltpu.make_async_copy(mixed.at[f], mixed_v, local_sem.at[4]),
    ]
    for copy in begin:
        copy.start()
    ga_v[s] = gh[...].astype(BF16)
    greet(s, f, S, N)
    spread = [
        remote(ga_v.at[s], ga_v.at[s], ga_send.at[k], ga_recv.at[k], (other, f)) for k, other in enumerate((px, py, pd))
    ]
    for copy in spread:
        copy.start()
    give(0)
    homing = []
    for k in range(1, N):
        to = lax.rem(f + k, N)
        homing.append(remote(mixed.at[to], mixed_out.at[f], home_send.at[0, k - 1], home_recv.at[0, k - 1], (s, to)))
        homing[-1].start()
    for copy in begin:
        copy.wait()
    done = [pltpu.make_async_copy(mixed_v, mixed_out.at[f], local_sem.at[4 + N])]
    done[0].start()
    for copy in spread:
        copy.wait_recv()
    give(1)

    def project(pair, carry):
        out = dot_nt(ga_v[...].reshape(R, D), wb_v.at[pl.ds(pair * (N * 2 // heads), N * 2 // heads)][...].reshape(2 * HD, D))
        gc_v[2 * pair] = out[:, :HD].astype(BF16)
        gc_v[2 * pair + 1] = out[:, HD:].astype(BF16)
        return carry

    lax.fori_loop(0, heads // 2, project, 0)

    def out_grad(column, carry):
        cut = pl.ds(pl.multiple_of(column * 2 * eighth, 2 * eighth), 2 * eighth)
        go_v[:, cut] = dot_t(ctx[...], ga_v[:, :, cut].reshape(R, 2 * eighth)).astype(BF16)
        return carry

    lax.fori_loop(0, 4, out_grad, 0)
    second(4)
    for j in range(N):
        pltpu.make_async_copy(go_v.at[pl.ds(j * own, own)], gout_buf.at[j], local_sem.at[4 + j]).start()
    for j in range(N):
        pltpu.make_async_copy(go_v.at[pl.ds(j * own, own)], gout_buf.at[j], local_sem.at[4 + j]).wait()
    out_begin()

    def attend(h, carry):
        rows = R // 4
        gk_v[...] = jnp.zeros_like(gk_v)
        gv_v[...] = jnp.zeros_like(gv_v)
        for block in range(4):
            cut = pl.ds(block * rows, rows)
            q, gc = qkv_v[h, cut, :], gc_v[h, cut, :]
            raw = dot_nt(q, qkv_v[heads + h])
            ok = (first[cut, :] <= place_row[...]) & (place_row[...] <= place[cut, :])
            scores = jnp.where(ok, raw * HD**-0.5, MASKED)
            weights = jnp.exp(scores - jnp.max(scores, axis=-1, keepdims=True))
            chance = weights / jnp.sum(weights, axis=-1, keepdims=True)
            grad_chance = dot_nt(gc, qkv_v[2 * heads + h])
            delta = jnp.sum(chance * grad_chance, axis=-1, keepdims=True)
            grad_raw = (chance * (grad_chance - delta) * HD**-0.5).astype(BF16)
            gk_v[...] += dot_t(grad_raw, q)
            gv_v[...] += dot_t(chance.astype(BF16), gc)
            gq = dot(grad_raw, qkv_v[heads + h]).astype(BF16).astype(F32)
            gq = gq * cos[cut, :] + pltpu.roll(gq * sin[cut, :], HD // 2, 1)
            qkv_v[h, cut, :] = gq.astype(BF16)
        gk = gk_v[...].astype(BF16).astype(F32)
        gk = gk * cos[...] + pltpu.roll(gk * sin[...], HD // 2, 1)
        qkv_v[heads + h] = gk.astype(BF16)
        qkv_v[2 * heads + h] = gv_v[...].astype(BF16)
        return carry

    lax.fori_loop(0, heads, attend, 0)
    for c in range(3 * heads):
        vec_v[D // 128 + c : D // 128 + c + 1, :] = jnp.sum(qkv_v[c].astype(F32), axis=0, keepdims=True)

    def partial(rows):
        cut = pl.ds(pl.multiple_of(rows * L, L), L)
        left = jnp.concatenate([qkv_v[c, cut, :] for c in range(3 * heads)], axis=1)
        return dot_nt(left, w_v[...].reshape(D, 3 * width))

    exchange = []
    for k, other in enumerate((px, py, pd)):
        part_send[k] = partial(other).astype(BF16)
        exchange.append(remote(part_send.at[k], part_recv.at[k], part_sems.at[k], part_semr.at[k], (other, f)))
        exchange[-1].start()
    gn_v[...] = partial(s)
    second(5)
    second(2)

    def in_grad(i, carry):
        cut = pl.ds(pl.multiple_of(i * 2 * eighth, 2 * eighth), 2 * eighth)
        left = na_v[:, :, cut].reshape(R, 2 * eighth)
        for c in range(0, 3 * heads, 2):
            right = jnp.concatenate([qkv_v[c], qkv_v[c + 1]], axis=1)
            gi_v[:, :, c * HD : (c + 2) * HD] = dot_t(left, right).astype(BF16).reshape(N, own, 2 * HD)
        copy = pltpu.make_async_copy(gi_v, gin_buf.at[i], local_sem.at[0])
        copy.start()
        copy.wait()
        return carry

    lax.fori_loop(0, S, in_grad, 0)
    in_begin()
    out_middle()
    second(3)
    in_middle()
    for k in range(3):
        exchange[k].wait_recv()
        gn_v[...] += part_recv[k].astype(F32)
    scaled = gn_v[...] * gain_row[...]
    scaled = scaled - unit[...] * jnp.mean(scaled * unit[...], axis=-1, keepdims=True)
    gx = (gh[...] + inverse[...] * scaled).astype(BF16)
    for j in range(N):
        gx_v[j] = gx[j * pr : (j + 1) * pr, :]
    done.append(pltpu.make_async_copy(gx_v.at[f], gx_out.at[f], local_sem.at[5 + N]))
    done[1].start()
    for k in range(1, N):
        to = lax.rem(f + k, N)
        homing.append(remote(gx_v.at[to], gx_out.at[f], home_send.at[1, k - 1], home_recv.at[1, k - 1], (s, to)))
        homing[-1].start()
    gain = jnp.sum(gn_v[...] * unit[...], axis=0, keepdims=True)
    for line in range(D // 128):
        vec_v[line : line + 1, :] = gain[:, line * 128 : (line + 1) * 128]
    vec_v[D // 128 + 16 :, :] = ready[...]
    small = []
    for k in range(1, N):
        to = lax.rem(f + k, N)
        small.append(remote(vec_v, vec_far.at[k - 1], vec_sems.at[k - 1], vec_semr.at[k - 1], (s, to)))
        small[-1].start()
    second(0)
    second(1)
    vec_sum[...] = vec_v[...]
    for k in range(1, N):
        small[k - 1].wait_recv()
        copy = pltpu.make_async_copy(vec_far.at[k - 1], vec_tmp, local_sem.at[2])
        copy.start()
        copy.wait()
        vec_sum[...] += vec_tmp[...]
    for k, other in enumerate((px, py, pd)):
        small.append(remote(vec_sum, vec_near.at[k], near_sems.at[k], near_semr.at[k], (other, f)))
        small[-1].start()
    gout_out[...] = out_end()
    in_stage[0] = in_end().astype(BF16)
    last = [
        remote(in_stage.at[0, other], gin_out.at[s], last_send.at[k], last_recv.at[k], (other, f))
        for k, other in enumerate((px, py, pd))
    ]
    for copy in last:
        copy.start()
    done.append(pltpu.make_async_copy(in_stage.at[0, s], gin_out.at[s], local_sem.at[1]))
    done[2].start()
    for i in range(6):
        for way in range(2):
            then_copy(i, way).wait_recv()
            if i < 2:
                give_copy(i, way).wait_send()
            then_copy(i, way).wait_send()
    in_drain()
    out_drain()
    for copy in spread + exchange + small:
        copy.wait_send()
    for copy in last + homing:
        copy.wait()
    bias_out[s] = vec_sum[D // 128 : D // 128 + 16, :]
    for k, other in enumerate((px, py, pd)):
        small[N - 1 + k].wait_recv()
        bias_out[other] = vec_near[k, D // 128 : D // 128 + 16, :]
    small_out[...] = vec_sum[...] + vec_near[0] + vec_near[1] + vec_near[2]
    for copy in done:
        copy.wait()


def backward(S, N, to_x, to_y, from_x, from_y, keep, w_in, w_back, normed_all, qkv, mixed, gh, unit, inverse, gain_row, ready, ctx, tables):
    own, D = w_back.shape[1:]
    L = gh.shape[0]
    R = S * L
    heads = H // S
    width = heads * HD
    chips = N // 2
    dma = pltpu.SemaphoreType.DMA
    shape = jax.ShapeDtypeStruct
    vmem = pltpu.VMEM
    eighth = D // 8
    blocks = [(eighth, u.shape[1]) if i < 2 else (u.shape[0], eighth) for i, u in enumerate(keep)]
    wholes = [(2 * eighth, u.shape[1]) if i < 2 else (u.shape[0], 2 * eighth) for i, u in enumerate(keep)]
    kinds = [blocks[i] for i in (0, 2, 4)]
    in_block, out_block = (S, own, 3 * width), (own, D)
    vec = (D // 128 + 16 + ready.shape[0], 128)
    out = [
        shape(mixed.shape, BF16), shape(mixed.shape, BF16), shape(in_block, BF16), shape(out_block, F32), shape(vec, F32),
        shape((S, 16, 128), F32),
        shape((N - 1,) + vec, F32),
        shape((S, N) + in_block[1:], BF16), shape((N,) + out_block, BF16), shape((chips,) + in_block, BF16),
        shape((chips,) + out_block, BF16),
    ]
    out += [shape(w, BF16) for w in wholes[:2] * 2] + [shape(b, BF16) for b in blocks * 4]
    anywhere = pl.BlockSpec(memory_space=pl.ANY)
    in_vmem = pl.BlockSpec(memory_space=vmem)
    result = pl.pallas_call(
        functools.partial(backward_kernel, S, N, (D, own, heads)),
        out_shape=out,
        in_specs=[anywhere] * 17 + [in_vmem] * 11,
        out_specs=[anywhere] * 3 + [in_vmem] * 3 + [anywhere] * (len(out) - 6),
        scratch_shapes=[vmem((2,) + k, BF16) for k in kinds]
        + [
            vmem(w_in.shape, BF16), vmem(w_back.shape, BF16), vmem((S, L, D), BF16), vmem((S, L, D), BF16),
            vmem(qkv.shape, BF16), vmem((heads, R, HD), BF16), vmem((R, HD), F32), vmem((R, HD), F32),
            vmem((3, L, D), BF16), vmem((3, L, D), BF16), vmem((L, D), F32), vmem((N, own, 3 * width), BF16),
            vmem((width, D), BF16),
            vmem(in_block, BF16), vmem(in_block, BF16), vmem((chips,) + in_block, BF16), vmem((chips - 1,) + in_block, BF16),
            vmem(out_block, BF16), vmem(out_block, BF16), vmem((chips,) + out_block, BF16),
            vmem((chips - 1,) + out_block, BF16),
            vmem(vec, F32), vmem(vec, F32), vmem(vec, F32), vmem((3,) + vec, F32),
            vmem(mixed.shape[1:], BF16), vmem(mixed.shape, BF16),
            dma((6, 4)), dma((6, 4)), dma((3,)), dma((3,)), dma((3,)), dma((3,)), dma((3,)), dma((2, chips)),
            dma((2, chips)), dma((2, chips - 1)), dma((2, chips - 1)), dma((3,)), dma((3,)), dma((N - 1,)), dma((N - 1,)),
            dma((3,)), dma((3,)), dma((2, N - 1)), dma((2, N - 1)), dma((6 + N,)),
        ],
        compiler_params=pltpu.CompilerParams(collective_id=1, has_side_effects=True, vmem_limit_bytes=VMEM_LIMIT),
        name="backward",
    )(*to_x, *to_y, from_x, from_y, *keep, w_in, w_back, normed_all, qkv, mixed, gh, unit, inverse, gain_row, ready, ctx, *tables)
    first_x, first_y, then_y, then_x = result[11:13], result[13:15], result[15:21], result[21:27]
    grads, line = [], 0
    for i, block in enumerate(keep):
        if i < 2:
            sources = (first_x[i][:eighth], first_y[i][:eighth])
            halves = (block[:eighth], block[eighth : 2 * eighth])
        else:
            lines = slice(line, line + block.shape[0])
            sources = (from_x[lines, :eighth], from_y[lines, :eighth])
            halves = (block[:, :eighth], block[:, eighth : 2 * eighth])
            line += block.shape[0]
        sums = [
            a.astype(F32) + b.astype(F32) + c.astype(F32)
            for a, b, c in zip(halves, sources, (then_y[i], then_x[i]))
        ]
        grads.append(jnp.concatenate(sums, axis=min(i // 2, 1)))
    return grads, result[:6]


def shards(
    tokens, cotangent, ids, deal, lengths, w_qkv, b_qkv, w_out, gain_attn, gain_ffn, w_router,
    w_shared_gate, e_gate, e_up, e_down, s_gate, s_up, s_down,
):
    S, N = lax.axis_size("seq"), lax.axis_size("fsdp")
    s, f = lax.axis_index("seq"), lax.axis_index("fsdp")
    MB, T, D = tokens.shape
    E = w_router.shape[1]
    assert S == 4 and e_gate.shape[0] == 1 and E == N
    FE, FS = e_gate.shape[2], s_gate.shape[1]
    piece = T // N
    pack = T * S
    heads = H // S
    width = heads * HD
    rows = N * MB * T
    own = w_out.shape[0]

    order = jnp.stack([jnp.bitwise_xor(s, rel) * 2 + half for rel, half in ORDER])
    inverse_order = jnp.argsort(order)

    def arrange(u, by):
        return jnp.take(u.reshape(u.shape[:-1] + (8, D // 8)), by, axis=u.ndim - 1).reshape(u.shape)

    inverse_deal = jnp.argsort(deal, axis=2)

    def deal_out(u):
        u = u.reshape(MB, piece, N, D)
        u = jnp.stack([jnp.take(u[m], inverse_deal[m, f], axis=1) for m in range(MB)])
        return u.transpose(2, 0, 1, 3).reshape(N, MB * piece, D)

    index = s * N + f

    def placed(u, length):
        return lax.dynamic_update_slice(jnp.zeros((length,), F32), u.astype(F32), ((index * u.shape[0]) % 128,))

    parts = [placed(gain_attn, 128), placed(gain_ffn, 128), placed(b_qkv, 256), placed(w_shared_gate, 128)]
    for u in (w_router.reshape(-1), ids.reshape(-1)):
        parts.append(jnp.pad(u.astype(F32), (0, -u.shape[0] % 128)))
    r_line = 5
    i_line = r_line + parts[4].shape[0] // 128
    small = jnp.concatenate(parts)
    small = jnp.pad(small, (0, -small.shape[0] % 1024)).reshape(-1, 128)

    spots = ((jnp.arange(S)[:, None, None] * piece + jnp.arange(piece)[None, None, :]) * N + jnp.arange(N)[None, :, None])
    spots = jnp.broadcast_to(spots[:, :, None, :], (S, N, MB, piece)).astype(jnp.int32)
    micro = jnp.arange(MB, dtype=jnp.int32)[None, None, :, None]
    my_lengths = lengths[:, f]
    ends = jnp.cumsum(my_lengths, axis=1)
    past = ends[None, None, :, None, :] <= spots[..., None]
    start = jnp.sum(jnp.where(past, my_lengths[None, None, :, None, :], 0), axis=4)
    frequency = THETA ** (-jnp.arange(0, HD, 2, dtype=F32) / HD)
    angle = (spots - start).astype(F32).reshape(-1, 1) * frequency
    cosine, sine = jnp.cos(angle), jnp.sin(angle)
    cosine = jnp.concatenate([cosine, cosine], axis=1)
    sine = jnp.concatenate([-sine, sine], axis=1)
    place = (spots + pack * micro).reshape(-1)
    first = (start + pack * micro).reshape(-1)
    tables = (cosine, sine, first[:, None], place[:, None], place[None, :])

    wq = w_qkv.reshape(own, 3, S, width).transpose(2, 0, 1, 3).reshape(S, own, 3 * width)
    x_rows, g_all, w_in, w_back, small, normed_all, qkv, context, hidden, x_all, *fulls = forward(
        S, N, MB, deal_out(tokens), deal_out(arrange(cotangent, order)), wq, w_out, small,
        (e_gate[0], e_up[0], s_gate.T, s_up.T, e_down[0], s_down), tables,
    )
    L, R = MB * T, MB * pack

    def vector(row):
        return small[:, :, row].swapaxes(0, 1).reshape(D // 128, 128 // own, 128).sum(1).reshape(D)

    gain_1, gain_2, shared_w = vector(0), vector(1), vector(4).astype(BF16)
    router_w = small[:, :, r_line:i_line].swapaxes(0, 1).reshape(S * N, -1)[:, : own * E].reshape(D, E).astype(BF16)
    all_ids = small[:, :, i_line:].reshape(N, S, -1)[:, :, : MB * T * TOP]
    x0 = x_rows.reshape(L, D).astype(F32)
    cot = arrange(lax.dynamic_index_in_dim(g_all, f, 0, keepdims=False).reshape(L, D), inverse_order)
    g_rows = g_all.reshape(rows, D)
    all_ids = lax.dynamic_index_in_dim(all_ids, s, 1, keepdims=False).reshape(N, MB, piece, N, TOP)
    where = inverse_deal.transpose(2, 1, 0)
    chosen = jnp.take_along_axis(
        all_ids[None], where[:, :, :, None, None, None], axis=4
    ).reshape(N, L, TOP).astype(jnp.int32)
    own_ids = lax.dynamic_index_in_dim(chosen, f, 0, keepdims=False)
    chosen = chosen.reshape(rows, TOP)
    x = x_all.reshape(rows, D)
    x_own = lax.dynamic_index_in_dim(x_all, f, 0, keepdims=False)
    unit_1, inverse_1 = rms_forward(x0)
    unit_2, inverse_2 = rms_forward(hidden)

    lead = jnp.concatenate([router_w, shared_w[:, None]], axis=1)
    lead_order = jnp.take(lead.reshape(8, D // 8, E + 1), order, axis=0).reshape(D, E + 1)
    picked_rows = jnp.any(chosen == f, axis=1, keepdims=True).astype(F32)
    y, *saved, act, sact = experts_forward(
        N, E, x, g_rows, picked_rows, jnp.pad(lead_order, ((0, 0), (0, 127 - E))), fulls
    )
    y = lax.psum_scatter(y, "fsdp", scatter_dimension=0, tiled=True)
    geo, gso = saved[1:3]
    dx, grad_gate, grad_up, grad_sgate, grad_sup = experts_backward(saved, fulls)
    dx = lax.psum_scatter(dx, "fsdp", scatter_dimension=0, tiled=True)

    half = D // 8
    cuts = (slice(4 * half, 6 * half), slice(6 * half, 8 * half), slice(0, 4 * half))

    def by_columns(cut):
        return (
            dot_t(grad_sgate, x[:, cut]).astype(BF16), dot_t(grad_sup, x[:, cut]).astype(BF16),
            dot_t(act, geo[:, cut]).astype(BF16), dot_t(sact, gso[:, cut]).astype(BF16),
        )

    def by_rows(cut):
        return dot_t(x[:, cut], grad_gate).astype(BF16), dot_t(x[:, cut], grad_up).astype(BF16)

    by_x, by_y = jnp.concatenate(by_columns(cuts[0])), jnp.concatenate(by_columns(cuts[1]))
    x, by_x, by_y = lax.optimization_barrier((x, by_x, by_y))
    from_x, from_y = across(by_x, 1), across(by_y, 2)
    to_x, to_y = by_rows(cuts[0]), by_rows(cuts[1])
    keep = by_rows(cuts[2]) + by_columns(cuts[2])
    dx, from_x, from_y, to_x, to_y, keep = lax.optimization_barrier((dx, from_x, from_y, to_x, to_y, keep))
    dx = dx.astype(F32)

    mixed = (hidden + arrange(y, inverse_order).astype(F32)).astype(BF16)
    base = D
    gg_own = sum(dx[:, base + i * N : base + (i + 1) * N] for i in range(3))
    gs_own = jnp.sum(dx[:, base + 3 * N : base + 6 * N], axis=1)
    grad_normed2 = arrange(dx[:, :D], inverse_order)
    flat2 = arrange(x_own, inverse_order)
    logits = dot(x_own, lead_order)
    shifted = jnp.exp(logits[:, :E] - jnp.max(logits[:, :E], axis=-1, keepdims=True))
    router = shifted / jnp.sum(shifted, axis=-1, keepdims=True)
    sigma = jax.nn.sigmoid(logits[:, E])
    picked = jnp.any(own_ids[:, :, None] == jnp.arange(E)[None, None, :], axis=1)
    grad_router = jnp.where(picked, gg_own, 0.0)
    grad_logits = (router * (grad_router - jnp.sum(router * grad_router, axis=-1, keepdims=True))).astype(BF16)
    grad_sigma = gs_own * sigma * (1.0 - sigma)
    grad_normed2 = grad_normed2 + dot_nt(grad_logits, router_w) + grad_sigma[:, None] * shared_w.astype(F32)[None, :]
    g_router = dot_t(flat2, grad_logits)
    g_shared = jnp.sum(grad_sigma[:, None] * flat2.astype(F32), axis=0)
    from_norm, g_gain_2 = rms_backward(grad_normed2, unit_2, inverse_2, gain_2)
    grad_hidden = cot.astype(F32) + from_norm

    ready = jnp.concatenate([g_gain_2, g_shared, g_router.reshape(-1)]).reshape(-1, 128)
    expert_grads, (mixed, grad_x, g_in, g_out, small, g_bias) = backward(
        S, N, to_x, to_y, from_x, from_y, keep, w_in, w_back, normed_all, qkv, mixed.reshape(N, MB * piece, D), grad_hidden, unit_1,
        inverse_1, gain_1[None], ready, context, tables,
    )
    def take_home(u):
        u = u.reshape(N, MB, piece, D)
        return jnp.stack([jnp.take(u[:, m], deal[m, f], axis=0).swapaxes(0, 1) for m in range(MB)]).reshape(MB, T, D)

    mixed, grad_tokens = take_home(mixed), take_home(grad_x).astype(F32)

    g_in = g_in.reshape(S, own, 3, width).transpose(1, 2, 0, 3).reshape(own, 3 * D).astype(F32)
    g_bias = g_bias[:, : 3 * heads].reshape(S, 3, width).swapaxes(0, 1).reshape(-1)

    def mine(u):
        return lax.dynamic_slice_in_dim(u, index * (u.shape[0] // (S * N)), u.shape[0] // (S * N))

    small = small.reshape(-1)
    after = D + 16 * 128
    g_gain_1, g_gain_2, g_shared = mine(small[:D]), mine(small[after : after + D]), mine(small[after + D : after + 2 * D])
    g_router = mine(small[after + 2 * D :]).reshape(own, E)
    return (
        mixed, grad_tokens, g_in, mine(g_bias), g_out, g_gain_1, g_gain_2, g_router, g_shared,
        expert_grads[0][None], expert_grads[1][None], expert_grads[4][None], expert_grads[2].T, expert_grads[3].T, expert_grads[5],
    )


def solution(mesh):
    both = ("seq", "fsdp")
    in_specs = (
        P(None, both, None), P(None, both, None), P(None, both, None), P(), P(), P(both, None), P(both), P(both, None),
        P(both), P(both), P(both, None), P(both), P("fsdp", "seq", None), P("fsdp", "seq", None),
        P("fsdp", None, "seq"), P("seq", "fsdp"), P("seq", "fsdp"), P("fsdp", "seq"),
    )
    out_specs = (
        P(None, both, None), P(None, both, None), P(both, None), P(both), P(both, None), P(both), P(both),
        P(both, None), P(both), P("fsdp", "seq", None), P("fsdp", "seq", None), P("fsdp", None, "seq"),
        P("seq", "fsdp"), P("seq", "fsdp"), P("fsdp", "seq"),
    )
    return jax.shard_map(shards, mesh=mesh, in_specs=in_specs, out_specs=out_specs, check_vma=False)
```

```python
import functools

import jax
import jax.numpy as jnp
from jax import lax
from jax.experimental import pallas as pl
from jax.experimental.pallas import tpu as pltpu
from jax.sharding import PartitionSpec as P

H = 16
HD = 128
TOP = 4
EPS = 1e-06
THETA = 1000000.0
MASKED = -1e30
F32 = jnp.float32
BF16 = jnp.bfloat16
MESH = pl.DeviceIdType.MESH
VMEM_LIMIT = 61 * 2**20

ORDER = ((0, 0), (0, 1), (2, 0), (1, 1), (1, 0), (3, 0), (2, 1), (3, 1))


def dot(a, b):
    return jnp.dot(a, b, preferred_element_type=F32)


def dot_t(a, b):
    return lax.dot_general(a, b, (((0,), (0,)), ((), ())), preferred_element_type=F32)


def dot_nt(a, b):
    return lax.dot_general(a, b, (((1,), (1,)), ((), ())), preferred_element_type=F32)


def turn(u):
    half = u.shape[-1] // 2
    return jnp.concatenate([-u[..., half:], u[..., :half]], axis=-1)


def turn_back(u):
    half = u.shape[-1] // 2
    return jnp.concatenate([u[..., half:], -u[..., :half]], axis=-1)


def rms_forward(values):
    inverse = lax.rsqrt(jnp.mean(values * values, axis=-1, keepdims=True) + EPS)
    return values * inverse, inverse


def rms_backward(grad, unit, inverse, gain):
    scaled = grad * gain
    grad_gain = jnp.sum(grad * unit, axis=tuple(range(grad.ndim - 1)))
    return inverse * (scaled - unit * jnp.mean(scaled * unit, axis=-1, keepdims=True)), grad_gain


def across(a, which):
    return lax.ppermute(a, "seq", [(i, i ^ which) for i in range(4)])


def split3(v):
    hi = lax.reduce_precision(v, 8, 7)
    mid = lax.reduce_precision(v - hi, 8, 7)
    low = lax.reduce_precision(v - hi - mid, 8, 7)
    return hi, mid, low


def swiglu_back(grad_act, gate, up):
    sig = jax.nn.sigmoid(gate)
    grad_gate = (grad_act * up * sig * (1.0 + gate * (1.0 - sig))).astype(BF16)
    grad_up = (grad_act * gate * sig).astype(BF16)
    return grad_gate, grad_up


def partners(s):
    return s + 1 - 2 * lax.rem(s, 2), lax.rem(s + 2, 4), 3 - s


def greet(s, f, S, N):
    barrier = pltpu.get_barrier_semaphore()
    for other in partners(s):
        pl.semaphore_signal(barrier, inc=1, device_id=(other, f), device_id_type=MESH)
    for step in range(1, N):
        pl.semaphore_signal(barrier, inc=1, device_id=(s, lax.rem(f + step, N)), device_id_type=MESH)
    pl.semaphore_wait(barrier, S - 1 + N - 1)


class Line:
    def __init__(self, s, f, N, block, move_send, move_recv, side_send, side_recv):
        self.s, self.chip, self.core, self.n = s, f // 2, lax.rem(f, 2), N // 2
        self.block = block
        self.move_send, self.move_recv = move_send, move_recv
        self.side_send, self.side_recv = side_send, side_recv

    def move(self, way, step, origin, to):
        ref = self.block(2 * origin + self.core)
        return pltpu.make_async_remote_copy(
            ref, ref, self.move_send.at[way, step], self.move_recv.at[way, step],
            device_id=(self.s, 2 * to + self.core), device_id_type=MESH,
        )

    def side(self, origin, core):
        ref = self.block(2 * origin + core)
        return pltpu.make_async_remote_copy(
            ref, ref, self.side_send.at[origin], self.side_recv.at[origin],
            device_id=(self.s, 2 * self.chip + 1 - self.core), device_id_type=MESH,
        )

    def send(self, step, act):
        q, n = self.chip, self.n

        @pl.when((q - step >= 0) & (q + 1 < n))
        def _():
            act(self.move(0, step, jnp.maximum(q - step, 0), jnp.minimum(q + 1, n - 1)))

        @pl.when((q + step < n) & (q >= 1))
        def _():
            act(self.move(1, step, jnp.minimum(q + step, n - 1), jnp.maximum(q - 1, 0)))

    def begin(self):
        self.send(0, lambda copy: copy.start())
        self.side(self.chip, self.core).start()

    def step(self, step):
        q, n = self.chip, self.n

        @pl.when(q - 1 - step >= 0)
        def _():
            origin = jnp.maximum(q - 1 - step, 0)
            self.move(0, step, origin, jnp.maximum(q - 1, 0)).wait_recv()
            if step + 1 < n - 1:

                @pl.when(q + 1 < n)
                def _():
                    self.move(0, step + 1, origin, jnp.minimum(q + 1, n - 1)).start()

            self.side(origin, self.core).start()

        @pl.when(q + 1 + step < n)
        def _():
            origin = jnp.minimum(q + 1 + step, n - 1)
            self.move(1, step, origin, jnp.minimum(q + 1, n - 1)).wait_recv()
            if step + 1 < n - 1:

                @pl.when(q >= 1)
                def _():
                    self.move(1, step + 1, origin, jnp.maximum(q - 1, 0)).start()

            self.side(origin, self.core).start()

    def arrive(self):
        for origin in range(self.n):
            self.side(origin, 1 - self.core).wait_recv()

    def drain(self):
        for step in range(self.n - 1):
            self.send(step, lambda copy: copy.wait_send())
        for origin in range(self.n):
            self.side(origin, self.core).wait_send()


PLACE = {key: i for i, key in enumerate(ORDER)}


def gather_vector(small, row, length, own, N):
    per = 128 // own
    for block in range(length // 128):
        total = None
        for i in range(block * per, (block + 1) * per):
            part = small[i % N, i // N, row : row + 1, :]
            total = part if total is None else total + part
        yield block, total


def forward_kernel(S, N, sizes, *refs):
    MB, piece, D, own, heads = sizes
    tok, cot, wq, wo, small, *refs = refs
    shards_in, refs = refs[:6], refs[6:]
    cos, sin, first, place, place_row, *refs = refs
    x_rows, g_all, w_in, w_back, small_all, normed_out, qkv_out, ctx_out, hid_out, x_all, *refs = refs
    fulls, refs = refs[:6], refs[6:]
    cot_by, shard_by, refs = refs[0], refs[1:7], refs[7:]
    small_v, tok_v, w_v, wb_v, x_v, gain_v, bias_v, na_v, qkv_v, ctx_v, part_send, part_recv, hid_v, n2_v, xo_v, *refs = refs
    (local_sem, deal_send, deal_recv, seq_send, seq_recv, small_send, small_recv, half_send, half_recv, part_sems,
     part_semr, norm_sems, norm_semr, out_sem, *line_sems) = refs
    s, f = lax.axis_index("seq"), lax.axis_index("fsdp")
    px, py, pd = partners(s)
    eighth = D // 8
    pr = MB * piece
    L = pr * N
    R = S * L
    width = heads * HD

    def spot(full, i, where):
        cut = pl.ds(where * eighth, eighth)
        return full.at[cut] if i < 2 else full.at[:, cut]

    def own_half(shard, i, half):
        cut = pl.ds(half * eighth, eighth)
        return shard.at[cut] if i < 2 else shard.at[:, cut]

    def remote(src, dst, send, recv, device):
        return pltpu.make_async_remote_copy(src, dst, send, recv, device_id=device, device_id_type=MESH)

    pairs = [
        (small, small_v.at[f, s]), (wq.at[s], w_v.at[s, f]), (wo, wb_v.at[f]), (tok.at[f], tok_v.at[f]), (cot.at[f], cot_by),
    ] + list(zip(shards_in, shard_by))
    take = [pltpu.make_async_copy(a, b, local_sem.at[i]) for i, (a, b) in enumerate(pairs)]
    put = [pltpu.make_async_copy(cot_by, g_all.at[f, f], local_sem.at[4])]
    for i in range(6):
        cut = pl.ds(0, 2 * eighth)
        target = fulls[i].at[cut] if i < 2 else fulls[i].at[:, cut]
        put.append(pltpu.make_async_copy(shard_by[i], target, local_sem.at[5 + i]))
    for copy in take:
        copy.start()
    greet(s, f, S, N)

    over_seq = []
    for k, other in enumerate((px, py, pd)):
        over_seq.append(remote(small, small_v.at[f, s], seq_send.at[0, k], seq_recv.at[0, k], (other, f)))
        over_seq.append(remote(wq.at[other], w_v.at[s, f], seq_send.at[1, k], seq_recv.at[1, k], (other, f)))
    for copy in over_seq:
        copy.start()
    deal_tok, deal_cot, to_all = [], [], []
    for k in range(1, N):
        to = lax.rem(f + k, N)
        deal_tok.append(remote(tok.at[to], tok_v.at[f], deal_send.at[0, k - 1], deal_recv.at[0, k - 1], (s, to)))
        deal_cot.append(remote(cot.at[to], g_all.at[to, f], deal_send.at[1, k - 1], deal_recv.at[1, k - 1], (s, to)))
        to_all.append(remote(small_v.at[f], small_v.at[f], small_send.at[k - 1], small_recv.at[k - 1], (s, to)))
    for copy in deal_tok:
        copy.start()

    def half_copy(i, k):
        where, rel, half = ((px, 1, 0), (py, 2, 1), (py, 2, 0), (px, 1, 1))[k]
        return remote(
            own_half(shards_in[i], i, half), spot(fulls[i], i, PLACE[rel, half]), half_send.at[i, k], half_recv.at[i, k],
            (where, f),
        )

    def pass_copy(i, k):
        where, rel, half = ((py, 1, 0), (px, 2, 1))[k]
        return remote(
            spot(fulls[i], i, PLACE[rel, half]), spot(fulls[i], i, PLACE[3, half]), half_send.at[i, 4 + k],
            half_recv.at[i, 4 + k], (where, f),
        )

    def give(i):
        for k in range(4):
            half_copy(i, k).start()

    def pass_on(i):
        for k in range(2):
            half_copy(i, k).wait_recv()
            pass_copy(i, k).start()

    give(0)
    for copy in take:
        copy.wait()
    for copy in put:
        copy.start()
    for copy in over_seq:
        copy.wait_recv()
    for copy in to_all:
        copy.start()
    w_line = Line(s, f, N, lambda j: w_v.at[:, j], *line_sems[0:4])
    b_line = Line(s, f, N, lambda j: wb_v.at[j], *line_sems[4:8])
    g_line = Line(s, f, N, lambda j: g_all.at[j], *line_sems[8:12])
    x_line = Line(s, f, N, lambda j: x_all.at[j], *line_sems[12:16])
    w_line.begin()
    b_line.begin()

    for copy in deal_tok + to_all:
        copy.wait_recv()
    for row in range(2):
        for block, part in gather_vector(small_v, row, D, own, N):
            gain_v[row : row + 1, block * 128 : (block + 1) * 128] = part
    nb = 3 * own
    for line in range(3 * D // 128):
        total = None
        for i in range(S * N):
            for half in range(2):
                if (i * nb) // 128 + half == line and (half == 0 or (i * nb) % 128 + nb > 128):
                    part = small_v[i % N, i // N, 2 + half : 3 + half, :]
                    total = part if total is None else total + part
        bias_v[line : line + 1, :] = total
    for j in range(N):
        x_v[j * pr : (j + 1) * pr, :] = tok_v[j].astype(F32)
    x = x_v[...]
    inverse = lax.rsqrt(jnp.mean(x * x, axis=-1, keepdims=True) + EPS)
    na_v[s] = (x * inverse * gain_v[0:1, :]).astype(BF16)
    spread = [
        remote(na_v.at[s], na_v.at[s], norm_sems.at[k], norm_semr.at[k], (other, f)) for k, other in enumerate((px, py, pd))
    ]
    for copy in spread:
        copy.start()
    for copy in deal_cot:
        copy.start()
    give(1)
    chips = N // 2
    for step in range(chips - 1):
        w_line.step(step)
        b_line.step(step)
        if step == 0:
            give(4)
        if step == 1:
            pass_on(0)
    pass_on(1)
    give(2)
    for copy in deal_cot:
        copy.wait_recv()
    for copy in put:
        copy.wait()
    g_line.begin()
    w_line.arrive()
    b_line.arrive()
    for copy in spread:
        copy.wait_recv()

    for t in range(3):

        def project(pair, carry, t=t):
            column = pl.multiple_of(t * width + pair * 2 * HD, 2 * HD)
            w = w_v[:, :, :, pl.ds(column, 2 * HD)].reshape(D, 2 * HD)
            out = dot(na_v[...].reshape(R, D), w)
            for k in range(2):
                u = out[:, k * HD : (k + 1) * HD]
                u = u + bias_v[pl.ds(t * (D // 128) + s * heads + 2 * pair + k, 1), :]
                if t < 2:
                    u = u * cos[...] + pltpu.roll(u, HD // 2, 1) * sin[...]
                qkv_v[t * heads + 2 * pair + k] = u.astype(BF16)
            return carry

        lax.fori_loop(0, heads // 2, project, 0)
    g_line.step(0)

    def attend(h, carry):
        rows = R // 4
        for block in range(4):
            cut = pl.ds(block * rows, rows)
            raw = dot_nt(qkv_v[h, cut, :], qkv_v[heads + h])
            ok = (first[cut, :] <= place_row[...]) & (place_row[...] <= place[cut, :])
            scores = jnp.where(ok, raw * HD**-0.5, MASKED)
            weights = jnp.exp(scores - jnp.max(scores, axis=-1, keepdims=True))
            chance = (weights / jnp.sum(weights, axis=-1, keepdims=True)).astype(BF16)
            ctx_v[cut, pl.ds(pl.multiple_of(h * HD, HD), HD)] = dot(chance, qkv_v[2 * heads + h]).astype(BF16)
        return carry

    lax.fori_loop(0, heads, attend, 0)
    for step in range(1, chips - 1):
        g_line.step(step)

    wb = wb_v[...].reshape(width, D)
    exchange = []
    for k, other in enumerate((px, py, pd)):
        rows = pl.ds(pl.multiple_of(other * L, L), L)
        part_send[k] = dot(ctx_v[rows, :], wb).astype(BF16)
        exchange.append(remote(part_send.at[k], part_recv.at[k], part_sems.at[k], part_semr.at[k], (other, f)))
        exchange[-1].start()
    hid_v[...] = x_v[...] + dot(ctx_v[pl.ds(pl.multiple_of(s * L, L), L), :], wb)
    outs = [
        (tok_v, x_rows), (w_v, w_in), (wb_v, w_back), (small_v, small_all), (na_v, normed_out), (qkv_v, qkv_out),
        (ctx_v, ctx_out), (hid_v, hid_out), (xo_v, x_all.at[f]),
    ]
    outs = [pltpu.make_async_copy(a, b, out_sem.at[i]) for i, (a, b) in enumerate(outs)]
    for k in range(3):
        exchange[k].wait_recv()
        hid_v[...] += part_recv[k].astype(F32)
    give(3)
    give(5)
    hidden = hid_v[...]
    inverse = lax.rsqrt(jnp.mean(hidden * hidden, axis=-1, keepdims=True) + EPS)
    n2_v[...] = (hidden * inverse * gain_v[1:2, :]).astype(BF16)
    owners = (s, px, py, pd)
    for i, (rel, half) in enumerate(ORDER):
        column = pl.multiple_of((owners[rel] * 2 + half) * eighth, eighth)
        xo_v[:, i * eighth : (i + 1) * eighth] = n2_v[:, pl.ds(column, eighth)]
    outs[8].start()
    outs[8].wait()
    x_line.begin()
    pass_on(4)
    pass_on(2)
    for step in range(chips - 1):
        x_line.step(step)
    pass_on(3)
    pass_on(5)
    for line in (w_line, b_line):
        line.drain()
    for copy in over_seq + to_all + spread:
        copy.wait_send()
    for copy in outs[:8]:
        copy.start()
    for i in range(6):
        for k in range(2, 4):
            half_copy(i, k).wait_recv()
        for k in range(2):
            pass_copy(i, k).wait_recv()
    for i in range(6):
        for k in range(4):
            half_copy(i, k).wait_send()
        for k in range(2):
            pass_copy(i, k).wait_send()
    for line in (g_line, x_line):
        line.arrive()
        line.drain()
    for copy in deal_tok + deal_cot + exchange:
        copy.wait_send()
    for copy in outs[:8]:
        copy.wait()


def forward(S, N, MB, tok, cot, wq, wo, small, shards_in, tables):
    own, D = wo.shape
    pr = tok.shape[1]
    L = pr * N
    R = S * L
    heads = H // S
    width = heads * HD
    chips = N // 2
    dma = pltpu.SemaphoreType.DMA
    line = [dma((2, chips - 1)), dma((2, chips - 1)), dma((chips,)), dma((chips,))]
    shape = jax.ShapeDtypeStruct
    w_shape, wb_shape, small_shape = (S, N) + wq.shape[1:], (N,) + wo.shape, (N, S) + small.shape
    out = [
        shape(tok.shape, BF16), shape((N,) + cot.shape, BF16), shape(w_shape, BF16), shape(wb_shape, BF16),
        shape(small_shape, F32), shape((S, L, D), BF16), shape((3 * heads, R, HD), BF16), shape((R, width), BF16),
        shape((L, D), F32), shape((N, L, D), BF16),
    ]
    for i, shard in enumerate(shards_in):
        rows, columns = shard.shape
        out.append(shape((4 * rows, columns) if i < 2 else (rows, 4 * columns), BF16))
    anywhere = pl.BlockSpec(memory_space=pl.ANY)
    in_vmem = pl.BlockSpec(memory_space=pltpu.VMEM)
    vmem = pltpu.VMEM
    return pl.pallas_call(
        functools.partial(forward_kernel, S, N, (MB, pr // MB, D, own, heads)),
        out_shape=out,
        in_specs=[anywhere] * 11 + [in_vmem] * 5,
        out_specs=[anywhere] * 16,
        scratch_shapes=[vmem(u.shape, u.dtype) for u in (cot[0], *shards_in)]
        + [
            vmem(small_shape, F32), vmem(tok.shape, BF16), vmem(w_shape, BF16), vmem(wb_shape, BF16), vmem((L, D), F32),
            vmem((8, D), F32), vmem((3 * D // 128, 128), F32), vmem((S, L, D), BF16), vmem((3 * heads, R, HD), BF16),
            vmem((R, width), BF16), vmem((3, L, D), BF16), vmem((3, L, D), BF16), vmem((L, D), F32), vmem((L, D), BF16),
            vmem((L, D), BF16),
            dma((11,)), dma((2, N - 1)), dma((2, N - 1)), dma((2, 3)), dma((2, 3)), dma((N - 1,)), dma((N - 1,)),
            dma((6, 6)), dma((6, 6)), dma((3,)), dma((3,)), dma((3,)), dma((3,)), dma((9,)),
        ] + line * 4,
        compiler_params=pltpu.CompilerParams(collective_id=0, has_side_effects=True, vmem_limit_bytes=VMEM_LIMIT),
        name="forward",
    )(tok, cot, wq, wo, small, *shards_in, *tables)


def hold(weights, held, sems, order):
    copies = [pltpu.make_async_copy(a, b, sems.at[i]) for i, (a, b) in enumerate(zip(weights, held))]
    opening = pl.program_id(0) == 0

    @pl.when(opening)
    def _():
        for i in order:
            copies[i].start()

    def need(i):
        @pl.when(opening)
        def _():
            copies[i].wait()

    return need


def experts_forward_kernel(N, E, *refs):
    x, g, picked, lead, *refs = refs
    weights, refs = refs[:6], refs[6:]
    y, notes, geo, gso, gate_o, up_o, sgate_o, sup_o, act, sact, *refs = refs
    eg, eu, sg, su, ed, sd = refs[:6]
    need = hold(weights, refs[:6], refs[6], (0, 1, 4, 2, 3, 5))
    f = lax.axis_index("fsdp")
    rows = x[...]
    logits = dot(rows, lead[...])
    lane = lax.broadcasted_iota(jnp.int32, logits.shape, 1)
    scores = jnp.where(lane < E, logits, MASKED)
    shifted = jnp.exp(scores - jnp.max(scores, axis=-1, keepdims=True))
    share = jnp.sum(jnp.where(lane == f, shifted, 0.0), axis=-1, keepdims=True)
    share = share / jnp.sum(jnp.where(lane < E, shifted, 0.0), axis=-1, keepdims=True)
    gate_f = jnp.where(picked[...] > 0.5, share, 0.0)
    sigma = jax.nn.sigmoid(jnp.sum(jnp.where(lane == E, logits, 0.0), axis=-1, keepdims=True))
    geo[...] = (gate_f * g[...].astype(F32)).astype(BF16)
    gso[...] = (sigma * g[...].astype(F32)).astype(BF16)
    need(0)
    gate = dot(rows, eg[...])
    gate_o[...] = gate
    need(1)
    up = dot(rows, eu[...])
    up_o[...] = up
    act[...] = (gate * jax.nn.sigmoid(gate) * up).astype(BF16)
    need(4)
    out = dot(act[...], ed[...]).astype(BF16).astype(F32)
    note_e = jnp.sum(out * g[...].astype(F32), axis=-1, keepdims=True)
    out = gate_f * out
    need(2)
    gate = dot_nt(rows, sg[...])
    sgate_o[...] = gate
    need(3)
    up = dot_nt(rows, su[...])
    sup_o[...] = up
    sact[...] = (gate * jax.nn.sigmoid(gate) * up).astype(BF16)
    need(5)
    out_s = dot(sact[...], sd[...])
    note_s = jnp.sum(out_s * g[...].astype(F32), axis=-1, keepdims=True)
    y[...] = (out + sigma * out_s).astype(BF16)
    lane = lax.broadcasted_iota(jnp.int32, notes.shape, 1)
    total = jnp.zeros(notes.shape, F32)
    i = 0
    for value in (note_e, note_s):
        for _ in range(3):
            part = value.astype(BF16).astype(F32)
            total = jnp.where(lane == i * N + f, part, total)
            value = value - part
            i += 1
    notes[...] = total.astype(BF16)


def experts_backward_kernel(*refs):
    notes, geo, gso, gate_i, up_i, sgate_i, sup_i, *refs = refs
    weights, refs = refs[:6], refs[6:]
    dx, grad_gate, grad_up, grad_sgate, grad_sup, *refs = refs
    eg, eu, sg, su, ed, sd = refs[:6]
    need = hold(weights, refs[:6], refs[6], (4, 0, 1, 5, 2, 3))
    D = geo.shape[1]

    def local(grad_act, gate, up, gate_grad, up_grad):
        sig = jax.nn.sigmoid(gate[...])
        gate_grad[...] = (grad_act * up[...] * sig * (1.0 + gate[...] * (1.0 - sig))).astype(BF16)
        up_grad[...] = (grad_act * gate[...] * sig).astype(BF16)

    need(4)
    local(dot_nt(geo[...], ed[...]), gate_i, up_i, grad_gate, grad_up)
    need(0)
    need(1)
    back = (dot_nt(grad_gate[...], eg[...]) + dot_nt(grad_up[...], eu[...])).astype(BF16)
    need(5)
    local(dot_nt(gso[...], sd[...]), sgate_i, sup_i, grad_sgate, grad_sup)
    need(2)
    need(3)
    back = back.astype(F32) + dot(grad_sgate[...], sg[...]) + dot(grad_sup[...], su[...])
    dx[:, :D] = back.astype(BF16)
    dx[:, D:] = notes[...]


def experts_call(kernel, name, arrays, whole, weights, outs, products):
    rows = arrays[0].shape[0]
    tile = 256
    units = weights[0].shape[1] + weights[2].shape[0]
    return pl.pallas_call(
        kernel,
        grid=(rows // tile,),
        out_shape=[jax.ShapeDtypeStruct((rows, c), t) for c, t in outs],
        in_specs=[pl.BlockSpec((tile, u.shape[1]), lambda i: (i, 0)) for u in arrays]
        + [pl.BlockSpec(u.shape, lambda i: (0, 0), pipeline_mode=pl.Buffered(1)) for u in whole]
        + [pl.BlockSpec(memory_space=pl.ANY)] * 6,
        out_specs=[pl.BlockSpec((tile, c), lambda i: (i, 0)) for c, _ in outs],
        scratch_shapes=[pltpu.VMEM(w.shape, BF16) for w in weights] + [pltpu.SemaphoreType.DMA((6,))],
        compiler_params=pltpu.CompilerParams(dimension_semantics=("arbitrary",), vmem_limit_bytes=VMEM_LIMIT),
        cost_estimate=pl.CostEstimate(
            flops=2 * products * rows * arrays[1].shape[1] * units, bytes_accessed=16 * rows * (units + 2048),
            transcendentals=rows * units,
        ),
        name=name,
    )(*arrays, *whole, *weights)


def experts_forward(N, E, x, g, picked, lead, weights):
    D, FE, FS = x.shape[1], weights[0].shape[1], weights[2].shape[0]
    outs = [(D, BF16), (6 * N + -(6 * N) % 128, BF16), (D, BF16), (D, BF16)]
    outs += [(c, F32) for c in (FE, FE, FS, FS)] + [(FE, BF16), (FS, BF16)]
    kernel = functools.partial(experts_forward_kernel, N, E)
    return experts_call(kernel, "experts_forward", (x, g, picked), (lead,), weights, outs, 3)


def experts_backward(arrays, weights):
    D, FE, FS = arrays[1].shape[1], weights[0].shape[1], weights[2].shape[0]
    outs = [(c, BF16) for c in (D + arrays[0].shape[1], FE, FE, FS, FS)]
    return experts_call(experts_backward_kernel, "experts_backward", arrays, (), weights, outs, 3)


def backward_kernel(S, N, sizes, *refs):
    D, own, heads = sizes
    to_x, to_y, stacked_x, stacked_y, keep, refs = refs[:2], refs[2:4], refs[4], refs[5], refs[6:12], refs[12:]
    from_x, from_y, line = [], [], 0
    for ref in keep[2:]:
        from_x.append(stacked_x.at[pl.ds(line, ref.shape[0])])
        from_y.append(stacked_y.at[pl.ds(line, ref.shape[0])])
        line += ref.shape[0]
    w_in, w_back, normed_all, qkv, mixed, gh, unit, inverse, gain_row, ready, ctx, cos, sin, first, place, place_row, *refs = refs
    mixed_out, gx_out, gin_out, gout_out, small_out, bias_out, vec_far, gin_buf, gout_buf, gin_pair, gout_pair, *refs = refs
    from_x, from_y, refs = (*refs[:2], *from_x), (*refs[2:4], *from_y), refs[4:]
    then_y, then_x, pair_y, pair_x, refs = refs[:6], refs[6:12], refs[12:18], refs[18:24], refs[24:]
    loads, refs = refs[:3], refs[3:]
    w_v, wb_v, ga_v, na_v, qkv_v, gc_v, gk_v, gv_v, part_send, part_recv, gn_v, gi_v, go_v, *refs = refs
    in_mine, in_pair, in_stage, in_far, out_mine, out_pair, out_stage, out_far, *refs = refs
    vec_v, vec_tmp, vec_sum, vec_near, mixed_v, gx_v, *refs = refs
    (step_send, step_recv, load_sem, ga_send, ga_recv, part_sems, part_semr, pair_send, pair_recv, far_send, far_recv,
     last_send, last_recv, vec_sems, vec_semr, near_sems, near_semr, home_send, home_recv, local_sem) = refs
    s, f = lax.axis_index("seq"), lax.axis_index("fsdp")
    px, py, pd = partners(s)
    chip, core, chips = f // 2, lax.rem(f, 2), N // 2
    eighth = D // 8
    L = gh.shape[0]
    R = S * L
    width = heads * HD
    pr = L // N
    kind = (0, 0, 1, 1, 2, 1)

    def remote(src, dst, send, recv, device):
        return pltpu.make_async_remote_copy(src, dst, send, recv, device_id=device, device_id_type=MESH)

    def part(ref, i, k):
        cut = pl.ds(k * eighth, eighth)
        return ref.at[cut] if i < 2 else ref.at[:, cut]

    def give_copy(i, way):
        a, b, to = ((to_x, from_x, px), (to_y, from_y, py))[way]
        return remote(a[i], b[i], step_send.at[i, way], step_recv.at[i, way], (to, f))

    def then_copy(i, way):
        a, b, to = ((pair_y, then_y, py), (pair_x, then_x, px))[way]
        return remote(a[i], b[i], step_send.at[i, 2 + way], step_recv.at[i, 2 + way], (to, f))

    def give(i):
        for way in range(2):
            give_copy(i, way).start()

    def fetch(i, sources):
        copies = [pltpu.make_async_copy(u, loads[kind[i]].at[k], load_sem.at[k]) for k, u in enumerate(sources)]
        for copy in copies:
            copy.start()
        for copy in copies:
            copy.wait()

    def second(i):
        buf = loads[kind[i]]
        for way, (place_in_keep, arrived) in enumerate(((2, from_x[i]), (3, from_y[i]))):
            if i < 2:
                give_copy(i, way).wait_recv()
            fetch(i, (part(keep[i], i, place_in_keep), part(arrived, i, 1)))
            buf[0] = (buf[0].astype(F32) + buf[1].astype(F32)).astype(BF16)
            copy = pltpu.make_async_copy(buf.at[0], (pair_y, pair_x)[way][i], load_sem.at[0])
            copy.start()
            copy.wait()
            then_copy(i, way).start()

    def reducer(block, pair, mine, other, stage, far, k):
        def pair_copy(q):
            return remote(block(2 * q + 1 - core), pair.at[q], pair_send.at[k, q], pair_recv.at[k, q], (s, 2 * chip + 1 - core))

        def far_copy(d):
            to = lax.rem(chip + d, chips)
            return remote(stage.at[d], far.at[d - 1], far_send.at[k, d - 1], far_recv.at[k, d - 1], (s, 2 * to + core))

        def begin():
            for q in range(chips):
                pair_copy(q).start()

        def middle():
            for q in range(chips):
                pair_copy(q).wait_recv()
            for d in range(1, chips + 1):
                d = d % chips
                q = lax.rem(chip + d, chips)
                copies = (
                    pltpu.make_async_copy(block(2 * q + core), mine, load_sem.at[0]),
                    pltpu.make_async_copy(pair.at[q], other, load_sem.at[1]),
                )
                for copy in copies:
                    copy.start()
                for copy in copies:
                    copy.wait()
                stage[d] = (mine[...].astype(F32) + other[...].astype(F32)).astype(BF16)
                if d:
                    far_copy(d).start()

        def end():
            total = stage[0].astype(F32)
            for d in range(1, chips):
                far_copy(d).wait_recv()
                total = total + far[d - 1].astype(F32)
            return total

        def drain():
            for q in range(chips):
                pair_copy(q).wait_send()
            for d in range(1, chips):
                far_copy(d).wait_send()

        return begin, middle, end, drain

    in_begin, in_middle, in_end, in_drain = reducer(
        lambda j: gin_buf.at[:, j], gin_pair, in_mine, in_pair, in_stage, in_far, 0)
    out_begin, out_middle, out_end, out_drain = reducer(
        lambda j: gout_buf.at[j], gout_pair, out_mine, out_pair, out_stage, out_far, 1)

    begin = [
        pltpu.make_async_copy(w_back, wb_v, local_sem.at[0]), pltpu.make_async_copy(w_in, w_v, local_sem.at[1]),
        pltpu.make_async_copy(qkv, qkv_v, local_sem.at[2]), pltpu.make_async_copy(normed_all, na_v, local_sem.at[3]),
        pltpu.make_async_copy(mixed.at[f], mixed_v, local_sem.at[4]),
    ]
    for copy in begin:
        copy.start()
    ga_v[s] = gh[...].astype(BF16)
    greet(s, f, S, N)
    spread = [
        remote(ga_v.at[s], ga_v.at[s], ga_send.at[k], ga_recv.at[k], (other, f)) for k, other in enumerate((px, py, pd))
    ]
    for copy in spread:
        copy.start()
    give(0)
    homing = []
    for k in range(1, N):
        to = lax.rem(f + k, N)
        homing.append(remote(mixed.at[to], mixed_out.at[f], home_send.at[0, k - 1], home_recv.at[0, k - 1], (s, to)))
        homing[-1].start()
    for copy in begin:
        copy.wait()
    done = [pltpu.make_async_copy(mixed_v, mixed_out.at[f], local_sem.at[4 + N])]
    done[0].start()
    for copy in spread:
        copy.wait_recv()
    give(1)

    def project(pair, carry):
        out = dot_nt(ga_v[...].reshape(R, D), wb_v.at[pl.ds(pair * (N * 2 // heads), N * 2 // heads)][...].reshape(2 * HD, D))
        gc_v[2 * pair] = out[:, :HD].astype(BF16)
        gc_v[2 * pair + 1] = out[:, HD:].astype(BF16)
        return carry

    lax.fori_loop(0, heads // 2, project, 0)

    def out_grad(column, carry):
        cut = pl.ds(pl.multiple_of(column * 2 * eighth, 2 * eighth), 2 * eighth)
        go_v[:, cut] = dot_t(ctx[...], ga_v[:, :, cut].reshape(R, 2 * eighth)).astype(BF16)
        return carry

    lax.fori_loop(0, 4, out_grad, 0)
    second(4)
    for j in range(N):
        pltpu.make_async_copy(go_v.at[pl.ds(j * own, own)], gout_buf.at[j], local_sem.at[4 + j]).start()
    for j in range(N):
        pltpu.make_async_copy(go_v.at[pl.ds(j * own, own)], gout_buf.at[j], local_sem.at[4 + j]).wait()
    out_begin()

    def attend(h, carry):
        rows = R // 4
        gk_v[...] = jnp.zeros_like(gk_v)
        gv_v[...] = jnp.zeros_like(gv_v)
        for block in range(4):
            cut = pl.ds(block * rows, rows)
            q, gc = qkv_v[h, cut, :], gc_v[h, cut, :]
            raw = dot_nt(q, qkv_v[heads + h])
            ok = (first[cut, :] <= place_row[...]) & (place_row[...] <= place[cut, :])
            scores = jnp.where(ok, raw * HD**-0.5, MASKED)
            weights = jnp.exp(scores - jnp.max(scores, axis=-1, keepdims=True))
            chance = weights / jnp.sum(weights, axis=-1, keepdims=True)
            grad_chance = dot_nt(gc, qkv_v[2 * heads + h])
            delta = jnp.sum(chance * grad_chance, axis=-1, keepdims=True)
            grad_raw = (chance * (grad_chance - delta) * HD**-0.5).astype(BF16)
            gk_v[...] += dot_t(grad_raw, q)
            gv_v[...] += dot_t(chance.astype(BF16), gc)
            gq = dot(grad_raw, qkv_v[heads + h]).astype(BF16).astype(F32)
            gq = gq * cos[cut, :] + pltpu.roll(gq * sin[cut, :], HD // 2, 1)
            qkv_v[h, cut, :] = gq.astype(BF16)
        gk = gk_v[...].astype(BF16).astype(F32)
        gk = gk * cos[...] + pltpu.roll(gk * sin[...], HD // 2, 1)
        qkv_v[heads + h] = gk.astype(BF16)
        qkv_v[2 * heads + h] = gv_v[...].astype(BF16)
        return carry

    lax.fori_loop(0, heads, attend, 0)
    for c in range(3 * heads):
        vec_v[D // 128 + c : D // 128 + c + 1, :] = jnp.sum(qkv_v[c].astype(F32), axis=0, keepdims=True)

    def partial(rows):
        cut = pl.ds(pl.multiple_of(rows * L, L), L)
        left = jnp.concatenate([qkv_v[c, cut, :] for c in range(3 * heads)], axis=1)
        return dot_nt(left, w_v[...].reshape(D, 3 * width))

    exchange = []
    for k, other in enumerate((px, py, pd)):
        part_send[k] = partial(other).astype(BF16)
        exchange.append(remote(part_send.at[k], part_recv.at[k], part_sems.at[k], part_semr.at[k], (other, f)))
        exchange[-1].start()
    gn_v[...] = partial(s)
    second(5)
    second(2)

    def in_grad(i, carry):
        cut = pl.ds(pl.multiple_of(i * 2 * eighth, 2 * eighth), 2 * eighth)
        left = na_v[:, :, cut].reshape(R, 2 * eighth)
        for c in range(0, 3 * heads, 2):
            right = jnp.concatenate([qkv_v[c], qkv_v[c + 1]], axis=1)
            gi_v[:, :, c * HD : (c + 2) * HD] = dot_t(left, right).astype(BF16).reshape(N, own, 2 * HD)
        copy = pltpu.make_async_copy(gi_v, gin_buf.at[i], local_sem.at[0])
        copy.start()
        copy.wait()
        return carry

    lax.fori_loop(0, S, in_grad, 0)
    in_begin()
    out_middle()
    second(3)
    in_middle()
    for k in range(3):
        exchange[k].wait_recv()
        gn_v[...] += part_recv[k].astype(F32)
    scaled = gn_v[...] * gain_row[...]
    scaled = scaled - unit[...] * jnp.mean(scaled * unit[...], axis=-1, keepdims=True)
    gx = (gh[...] + inverse[...] * scaled).astype(BF16)
    for j in range(N):
        gx_v[j] = gx[j * pr : (j + 1) * pr, :]
    done.append(pltpu.make_async_copy(gx_v.at[f], gx_out.at[f], local_sem.at[5 + N]))
    done[1].start()
    for k in range(1, N):
        to = lax.rem(f + k, N)
        homing.append(remote(gx_v.at[to], gx_out.at[f], home_send.at[1, k - 1], home_recv.at[1, k - 1], (s, to)))
        homing[-1].start()
    gain = jnp.sum(gn_v[...] * unit[...], axis=0, keepdims=True)
    for line in range(D // 128):
        vec_v[line : line + 1, :] = gain[:, line * 128 : (line + 1) * 128]
    vec_v[D // 128 + 16 :, :] = ready[...]
    small = []
    for k in range(1, N):
        to = lax.rem(f + k, N)
        small.append(remote(vec_v, vec_far.at[k - 1], vec_sems.at[k - 1], vec_semr.at[k - 1], (s, to)))
        small[-1].start()
    second(0)
    second(1)
    vec_sum[...] = vec_v[...]
    for k in range(1, N):
        small[k - 1].wait_recv()
        copy = pltpu.make_async_copy(vec_far.at[k - 1], vec_tmp, local_sem.at[2])
        copy.start()
        copy.wait()
        vec_sum[...] += vec_tmp[...]
    for k, other in enumerate((px, py, pd)):
        small.append(remote(vec_sum, vec_near.at[k], near_sems.at[k], near_semr.at[k], (other, f)))
        small[-1].start()
    gout_out[...] = out_end()
    in_stage[0] = in_end().astype(BF16)
    last = [
        remote(in_stage.at[0, other], gin_out.at[s], last_send.at[k], last_recv.at[k], (other, f))
        for k, other in enumerate((px, py, pd))
    ]
    for copy in last:
        copy.start()
    done.append(pltpu.make_async_copy(in_stage.at[0, s], gin_out.at[s], local_sem.at[1]))
    done[2].start()
    for i in range(6):
        for way in range(2):
            then_copy(i, way).wait_recv()
            if i < 2:
                give_copy(i, way).wait_send()
            then_copy(i, way).wait_send()
    in_drain()
    out_drain()
    for copy in spread + exchange + small:
        copy.wait_send()
    for copy in last + homing:
        copy.wait()
    bias_out[s] = vec_sum[D // 128 : D // 128 + 16, :]
    for k, other in enumerate((px, py, pd)):
        small[N - 1 + k].wait_recv()
        bias_out[other] = vec_near[k, D // 128 : D // 128 + 16, :]
    small_out[...] = vec_sum[...] + vec_near[0] + vec_near[1] + vec_near[2]
    for copy in done:
        copy.wait()


def backward(S, N, to_x, to_y, from_x, from_y, keep, w_in, w_back, normed_all, qkv, mixed, gh, unit, inverse, gain_row, ready, ctx, tables):
    own, D = w_back.shape[1:]
    L = gh.shape[0]
    R = S * L
    heads = H // S
    width = heads * HD
    chips = N // 2
    dma = pltpu.SemaphoreType.DMA
    shape = jax.ShapeDtypeStruct
    vmem = pltpu.VMEM
    eighth = D // 8
    blocks = [(eighth, u.shape[1]) if i < 2 else (u.shape[0], eighth) for i, u in enumerate(keep)]
    wholes = [(2 * eighth, u.shape[1]) if i < 2 else (u.shape[0], 2 * eighth) for i, u in enumerate(keep)]
    kinds = [blocks[i] for i in (0, 2, 4)]
    in_block, out_block = (S, own, 3 * width), (own, D)
    vec = (D // 128 + 16 + ready.shape[0], 128)
    out = [
        shape(mixed.shape, BF16), shape(mixed.shape, BF16), shape(in_block, BF16), shape(out_block, F32), shape(vec, F32),
        shape((S, 16, 128), F32),
        shape((N - 1,) + vec, F32),
        shape((S, N) + in_block[1:], BF16), shape((N,) + out_block, BF16), shape((chips,) + in_block, BF16),
        shape((chips,) + out_block, BF16),
    ]
    out += [shape(w, BF16) for w in wholes[:2] * 2] + [shape(b, BF16) for b in blocks * 4]
    anywhere = pl.BlockSpec(memory_space=pl.ANY)
    in_vmem = pl.BlockSpec(memory_space=vmem)
    result = pl.pallas_call(
        functools.partial(backward_kernel, S, N, (D, own, heads)),
        out_shape=out,
        in_specs=[anywhere] * 17 + [in_vmem] * 11,
        out_specs=[anywhere] * 3 + [in_vmem] * 3 + [anywhere] * (len(out) - 6),
        scratch_shapes=[vmem((2,) + k, BF16) for k in kinds]
        + [
            vmem(w_in.shape, BF16), vmem(w_back.shape, BF16), vmem((S, L, D), BF16), vmem((S, L, D), BF16),
            vmem(qkv.shape, BF16), vmem((heads, R, HD), BF16), vmem((R, HD), F32), vmem((R, HD), F32),
            vmem((3, L, D), BF16), vmem((3, L, D), BF16), vmem((L, D), F32), vmem((N, own, 3 * width), BF16),
            vmem((width, D), BF16),
            vmem(in_block, BF16), vmem(in_block, BF16), vmem((chips,) + in_block, BF16), vmem((chips - 1,) + in_block, BF16),
            vmem(out_block, BF16), vmem(out_block, BF16), vmem((chips,) + out_block, BF16),
            vmem((chips - 1,) + out_block, BF16),
            vmem(vec, F32), vmem(vec, F32), vmem(vec, F32), vmem((3,) + vec, F32),
            vmem(mixed.shape[1:], BF16), vmem(mixed.shape, BF16),
            dma((6, 4)), dma((6, 4)), dma((3,)), dma((3,)), dma((3,)), dma((3,)), dma((3,)), dma((2, chips)),
            dma((2, chips)), dma((2, chips - 1)), dma((2, chips - 1)), dma((3,)), dma((3,)), dma((N - 1,)), dma((N - 1,)),
            dma((3,)), dma((3,)), dma((2, N - 1)), dma((2, N - 1)), dma((6 + N,)),
        ],
        compiler_params=pltpu.CompilerParams(collective_id=1, has_side_effects=True, vmem_limit_bytes=VMEM_LIMIT),
        name="backward",
    )(*to_x, *to_y, from_x, from_y, *keep, w_in, w_back, normed_all, qkv, mixed, gh, unit, inverse, gain_row, ready, ctx, *tables)
    first_x, first_y, then_y, then_x = result[11:13], result[13:15], result[15:21], result[21:27]
    grads, line = [], 0
    for i, block in enumerate(keep):
        if i < 2:
            sources = (first_x[i][:eighth], first_y[i][:eighth])
            halves = (block[:eighth], block[eighth : 2 * eighth])
        else:
            lines = slice(line, line + block.shape[0])
            sources = (from_x[lines, :eighth], from_y[lines, :eighth])
            halves = (block[:, :eighth], block[:, eighth : 2 * eighth])
            line += block.shape[0]
        sums = [
            a.astype(F32) + b.astype(F32) + c.astype(F32)
            for a, b, c in zip(halves, sources, (then_y[i], then_x[i]))
        ]
        grads.append(jnp.concatenate(sums, axis=min(i // 2, 1)))
    return grads, result[:6]


def shards(
    tokens, cotangent, ids, deal, lengths, w_qkv, b_qkv, w_out, gain_attn, gain_ffn, w_router,
    w_shared_gate, e_gate, e_up, e_down, s_gate, s_up, s_down,
):
    S, N = lax.axis_size("seq"), lax.axis_size("fsdp")
    s, f = lax.axis_index("seq"), lax.axis_index("fsdp")
    MB, T, D = tokens.shape
    E = w_router.shape[1]
    assert S == 4 and e_gate.shape[0] == 1 and E == N
    FE, FS = e_gate.shape[2], s_gate.shape[1]
    piece = T // N
    pack = T * S
    heads = H // S
    width = heads * HD
    rows = N * MB * T
    own = w_out.shape[0]

    order = jnp.stack([jnp.bitwise_xor(s, rel) * 2 + half for rel, half in ORDER])
    inverse_order = jnp.argsort(order)

    def arrange(u, by):
        return jnp.take(u.reshape(u.shape[:-1] + (8, D // 8)), by, axis=u.ndim - 1).reshape(u.shape)

    inverse_deal = jnp.argsort(deal, axis=2)

    def deal_out(u):
        u = u.reshape(MB, piece, N, D)
        u = jnp.stack([jnp.take(u[m], inverse_deal[m, f], axis=1) for m in range(MB)])
        return u.transpose(2, 0, 1, 3).reshape(N, MB * piece, D)

    index = s * N + f

    def placed(u, length):
        return lax.dynamic_update_slice(jnp.zeros((length,), F32), u.astype(F32), ((index * u.shape[0]) % 128,))

    parts = [placed(gain_attn, 128), placed(gain_ffn, 128), placed(b_qkv, 256), placed(w_shared_gate, 128)]
    for u in (w_router.reshape(-1), ids.reshape(-1)):
        parts.append(jnp.pad(u.astype(F32), (0, -u.shape[0] % 128)))
    r_line = 5
    i_line = r_line + parts[4].shape[0] // 128
    small = jnp.concatenate(parts)
    small = jnp.pad(small, (0, -small.shape[0] % 1024)).reshape(-1, 128)

    spots = ((jnp.arange(S)[:, None, None] * piece + jnp.arange(piece)[None, None, :]) * N + jnp.arange(N)[None, :, None])
    spots = jnp.broadcast_to(spots[:, :, None, :], (S, N, MB, piece)).astype(jnp.int32)
    micro = jnp.arange(MB, dtype=jnp.int32)[None, None, :, None]
    my_lengths = lengths[:, f]
    ends = jnp.cumsum(my_lengths, axis=1)
    past = ends[None, None, :, None, :] <= spots[..., None]
    start = jnp.sum(jnp.where(past, my_lengths[None, None, :, None, :], 0), axis=4)
    frequency = THETA ** (-jnp.arange(0, HD, 2, dtype=F32) / HD)
    angle = (spots - start).astype(F32).reshape(-1, 1) * frequency
    cosine, sine = jnp.cos(angle), jnp.sin(angle)
    cosine = jnp.concatenate([cosine, cosine], axis=1)
    sine = jnp.concatenate([-sine, sine], axis=1)
    place = (spots + pack * micro).reshape(-1)
    first = (start + pack * micro).reshape(-1)
    tables = (cosine, sine, first[:, None], place[:, None], place[None, :])

    wq = w_qkv.reshape(own, 3, S, width).transpose(2, 0, 1, 3).reshape(S, own, 3 * width)
    x_rows, g_all, w_in, w_back, small, normed_all, qkv, context, hidden, x_all, *fulls = forward(
        S, N, MB, deal_out(tokens), deal_out(arrange(cotangent, order)), wq, w_out, small,
        (e_gate[0], e_up[0], s_gate.T, s_up.T, e_down[0], s_down), tables,
    )
    L, R = MB * T, MB * pack

    def vector(row):
        return small[:, :, row].swapaxes(0, 1).reshape(D // 128, 128 // own, 128).sum(1).reshape(D)

    gain_1, gain_2, shared_w = vector(0), vector(1), vector(4).astype(BF16)
    router_w = small[:, :, r_line:i_line].swapaxes(0, 1).reshape(S * N, -1)[:, : own * E].reshape(D, E).astype(BF16)
    all_ids = small[:, :, i_line:].reshape(N, S, -1)[:, :, : MB * T * TOP]
    x0 = x_rows.reshape(L, D).astype(F32)
    cot = arrange(lax.dynamic_index_in_dim(g_all, f, 0, keepdims=False).reshape(L, D), inverse_order)
    g_rows = g_all.reshape(rows, D)
    all_ids = lax.dynamic_index_in_dim(all_ids, s, 1, keepdims=False).reshape(N, MB, piece, N, TOP)
    where = inverse_deal.transpose(2, 1, 0)
    chosen = jnp.take_along_axis(
        all_ids[None], where[:, :, :, None, None, None], axis=4
    ).reshape(N, L, TOP).astype(jnp.int32)
    own_ids = lax.dynamic_index_in_dim(chosen, f, 0, keepdims=False)
    chosen = chosen.reshape(rows, TOP)
    x = x_all.reshape(rows, D)
    x_own = lax.dynamic_index_in_dim(x_all, f, 0, keepdims=False)
    unit_1, inverse_1 = rms_forward(x0)
    unit_2, inverse_2 = rms_forward(hidden)

    lead = jnp.concatenate([router_w, shared_w[:, None]], axis=1)
    lead_order = jnp.take(lead.reshape(8, D // 8, E + 1), order, axis=0).reshape(D, E + 1)
    picked_rows = jnp.any(chosen == f, axis=1, keepdims=True).astype(F32)
    y, *saved, act, sact = experts_forward(
        N, E, x, g_rows, picked_rows, jnp.pad(lead_order, ((0, 0), (0, 127 - E))), fulls
    )
    y = lax.psum_scatter(y, "fsdp", scatter_dimension=0, tiled=True)
    geo, gso = saved[1:3]
    dx, grad_gate, grad_up, grad_sgate, grad_sup = experts_backward(saved, fulls)
    dx = lax.psum_scatter(dx, "fsdp", scatter_dimension=0, tiled=True)

    half = D // 8
    cuts = (slice(4 * half, 6 * half), slice(6 * half, 8 * half), slice(0, 4 * half))

    def by_columns(cut):
        return (
            dot_t(grad_sgate, x[:, cut]).astype(BF16), dot_t(grad_sup, x[:, cut]).astype(BF16),
            dot_t(act, geo[:, cut]).astype(BF16), dot_t(sact, gso[:, cut]).astype(BF16),
        )

    def by_rows(cut):
        return dot_t(x[:, cut], grad_gate).astype(BF16), dot_t(x[:, cut], grad_up).astype(BF16)

    by_x, by_y = jnp.concatenate(by_columns(cuts[0])), jnp.concatenate(by_columns(cuts[1]))
    x, by_x, by_y = lax.optimization_barrier((x, by_x, by_y))
    from_x, from_y = across(by_x, 1), across(by_y, 2)
    to_x, to_y = by_rows(cuts[0]), by_rows(cuts[1])
    keep = by_rows(cuts[2]) + by_columns(cuts[2])
    dx, from_x, from_y, to_x, to_y, keep = lax.optimization_barrier((dx, from_x, from_y, to_x, to_y, keep))
    dx = dx.astype(F32)

    mixed = (hidden + arrange(y, inverse_order).astype(F32)).astype(BF16)
    base = D
    gg_own = sum(dx[:, base + i * N : base + (i + 1) * N] for i in range(3))
    gs_own = jnp.sum(dx[:, base + 3 * N : base + 6 * N], axis=1)
    grad_normed2 = arrange(dx[:, :D], inverse_order)
    flat2 = arrange(x_own, inverse_order)
    logits = dot(x_own, lead_order)
    shifted = jnp.exp(logits[:, :E] - jnp.max(logits[:, :E], axis=-1, keepdims=True))
    router = shifted / jnp.sum(shifted, axis=-1, keepdims=True)
    sigma = jax.nn.sigmoid(logits[:, E])
    picked = jnp.any(own_ids[:, :, None] == jnp.arange(E)[None, None, :], axis=1)
    grad_router = jnp.where(picked, gg_own, 0.0)
    grad_logits = (router * (grad_router - jnp.sum(router * grad_router, axis=-1, keepdims=True))).astype(BF16)
    grad_sigma = gs_own * sigma * (1.0 - sigma)
    grad_normed2 = grad_normed2 + dot_nt(grad_logits, router_w) + grad_sigma[:, None] * shared_w.astype(F32)[None, :]
    g_router = dot_t(flat2, grad_logits)
    g_shared = jnp.sum(grad_sigma[:, None] * flat2.astype(F32), axis=0)
    from_norm, g_gain_2 = rms_backward(grad_normed2, unit_2, inverse_2, gain_2)
    grad_hidden = cot.astype(F32) + from_norm

    ready = jnp.concatenate([g_gain_2, g_shared, g_router.reshape(-1)]).reshape(-1, 128)
    expert_grads, (mixed, grad_x, g_in, g_out, small, g_bias) = backward(
        S, N, to_x, to_y, from_x, from_y, keep, w_in, w_back, normed_all, qkv, mixed.reshape(N, MB * piece, D), grad_hidden, unit_1,
        inverse_1, gain_1[None], ready, context, tables,
    )
    def take_home(u):
        u = u.reshape(N, MB, piece, D)
        return jnp.stack([jnp.take(u[:, m], deal[m, f], axis=0).swapaxes(0, 1) for m in range(MB)]).reshape(MB, T, D)

    mixed, grad_tokens = take_home(mixed), take_home(grad_x).astype(F32)

    g_in = g_in.reshape(S, own, 3, width).transpose(1, 2, 0, 3).reshape(own, 3 * D).astype(F32)
    g_bias = g_bias[:, : 3 * heads].reshape(S, 3, width).swapaxes(0, 1).reshape(-1)

    def mine(u):
        return lax.dynamic_slice_in_dim(u, index * (u.shape[0] // (S * N)), u.shape[0] // (S * N))

    small = small.reshape(-1)
    after = D + 16 * 128
    g_gain_1, g_gain_2, g_shared = mine(small[:D]), mine(small[after : after + D]), mine(small[after + D : after + 2 * D])
    g_router = mine(small[after + 2 * D :]).reshape(own, E)
    return (
        mixed, grad_tokens, g_in, mine(g_bias), g_out, g_gain_1, g_gain_2, g_router, g_shared,
        expert_grads[0][None], expert_grads[1][None], expert_grads[4][None], expert_grads[2].T, expert_grads[3].T, expert_grads[5],
    )


def solution(mesh):
    both = ("seq", "fsdp")
    in_specs = (
        P(None, both, None), P(None, both, None), P(None, both, None), P(), P(), P(both, None), P(both), P(both, None),
        P(both), P(both), P(both, None), P(both), P("fsdp", "seq", None), P("fsdp", "seq", None),
        P("fsdp", None, "seq"), P("seq", "fsdp"), P("seq", "fsdp"), P("fsdp", "seq"),
    )
    out_specs = (
        P(None, both, None), P(None, both, None), P(both, None), P(both), P(both, None), P(both), P(both),
        P(both, None), P(both), P("fsdp", "seq", None), P("fsdp", "seq", None), P("fsdp", None, "seq"),
        P("seq", "fsdp"), P("seq", "fsdp"), P("fsdp", "seq"),
    )
    return jax.shard_map(shards, mesh=mesh, in_specs=in_specs, out_specs=out_specs, check_vma=False)
```
